256 devices in a mesh: row: 16 (over z_lo, x, core), col: 16 (over z_hi, y).
Axes of the slice: x: 4, y: 4, z: 8 (z_hi: 4, z_lo: 2; z = z_hi * 2 + z_lo), core: 2. Of those that a mesh axis runs over, the one named last changes fastest.
Arguments:
- pair_input: bfloat16 [384, 384, 128], P('row', 'col'), may hold values from -6 to 6
- norm_mean: float32 [384, 384], P('row', 'col'), may hold values from -0.5 to 0.5
- norm_scale: float32 [384, 384], P('row', 'col'), may hold values from 0.5 to 2
- pair_mask: int32 [384, 384], P('row', 'col'), may hold values 0 or 1
- cotangent: bfloat16 [384, 384, 128], P('row', 'col'), may hold values from -6 to 6
- left_gate: bfloat16 [128, 128], replicated, may hold values from -0.5 to 0.5
- left_value: bfloat16 [128, 128], replicated, may hold values from -0.5 to 0.5
- right_gate: bfloat16 [128, 128], replicated, may hold values from -0.5 to 0.5
- right_value: bfloat16 [128, 128], replicated, may hold values from -0.5 to 0.5
- output_gate: bfloat16 [128, 128], replicated, may hold values from -0.5 to 0.5
- output_weight: bfloat16 [128, 128], replicated, may hold values from -0.5 to 0.5
Outputs:
- pair_grad: float32 [384, 384, 128], P('row', 'col')
The draws below stay inside these ranges and needn't reach their ends.
Inputs may be any that keep to these rules, and one draw needn't show every extreme that they name: `pair_mask`: 1 marks a pair that takes part.
All inputs are finite; a program needn't handle non-finite values. No bound on the sum of `pair_mask` on one device may be relied on, other than what follows from the above.
Results may differ from the reference program's by a relative error of at most 0.0072.
Values may be sent and summed in bfloat16 or wider, within the bound.
No kernel may reach another device: no remote copies, remote signals or barrier semaphores. Data moves between devices by JAX's collectives and lax.ppermute only.
A program may use at most 128 MiB of HBM per device.

```python
import math
import jax
import jax.numpy as jnp
from jax import lax

PAIR = 128
HIDDEN_SIZE = 128
TOKENS = 384


def place_ends(entries, own_key, least, largest):
    longest = entries.shape.index(max(entries.shape))
    spots = []
    for shift in (0, 1):
        where = [jax.random.randint(jax.random.fold_in(own_key, axis), (), 0, length) for axis, length in enumerate(entries.shape)]
        where[longest] = (where[longest] + shift) % entries.shape[longest]
        spots.append(tuple(where))
    return entries.at[spots[0]].set(least).at[spots[1]].set(largest)


def block_scale(stream_key, shape, split, smallest, high):
    def one(axis_at, shards_of):
        heights = jax.random.uniform(jax.random.fold_in(jax.random.fold_in(stream_key, 6), axis_at), (shards_of,), jnp.float32, smallest / len(split), high / len(split))
        return jnp.repeat(jnp.exp(heights), shape[axis_at] // shards_of).reshape((-1,) + (1,) * (len(shape) - axis_at - 1))

    factor_of = one(*split[0])
    for cut in split[1:]:
        factor_of = factor_of * one(*cut)
    return factor_of


def normal_values(stream_key, shape, deviation, reach, cuts=(), held_as=jnp.bfloat16):
    factor_of = block_scale(stream_key, shape, cuts, -0.22, 0.18) if cuts else 1.0
    entries = jax.random.normal(stream_key, shape, jnp.float32) * deviation * factor_of
    return jnp.minimum(jnp.maximum(entries, -reach), reach).astype(held_as)


def setup_inputs(seed: int = 0) -> dict:
    keys = jax.random.split(jax.random.key(seed), 12)
    return {
        "pair_input": normal_values(keys[0], (TOKENS, TOKENS, PAIR), 1.0, 6.0, ((0, 16), (1, 16))),
        "norm_mean": jnp.clip(jax.random.uniform(keys[1], (TOKENS, TOKENS), jnp.float32, -0.5, 0.5) * block_scale(keys[1], (TOKENS, TOKENS), ((0, 16), (1, 16)), -0.4, 0.0), -0.5, 0.5),
        "norm_scale": jnp.clip(jnp.exp(math.log(2.0) - 1.3862944 * jax.random.uniform(keys[2], (TOKENS, TOKENS), jnp.float32) ** block_scale(keys[2], (TOKENS, TOKENS), ((0, 16), (1, 16)), -0.2, 0.2)), 0.5, 2.0),
        "pair_mask": place_ends((jax.random.randint(keys[3], (TOKENS, TOKENS), 0, 8) < 7).astype(jnp.int32), jax.random.fold_in(keys[3], 1), 0, 1),
        "cotangent": normal_values(keys[4], (TOKENS, TOKENS, PAIR), 1.0, 6.0, ((0, 16), (1, 16))),
        "left_gate": normal_values(keys[5], (PAIR, HIDDEN_SIZE), PAIR ** -0.5, 0.5),
        "left_value": normal_values(keys[6], (PAIR, HIDDEN_SIZE), PAIR ** -0.5, 0.5),
        "right_gate": normal_values(keys[7], (PAIR, HIDDEN_SIZE), PAIR ** -0.5, 0.5),
        "right_value": normal_values(keys[8], (PAIR, HIDDEN_SIZE), PAIR ** -0.5, 0.5),
        "output_gate": normal_values(keys[9], (PAIR, PAIR), PAIR ** -0.5, 0.5),
        "output_weight": normal_values(keys[10], (HIDDEN_SIZE, PAIR), HIDDEN_SIZE ** -0.5, 0.5),
    }


epsilon = 1e-05

def layer_back(grad, normed, scale):
    centre = lax.optimization_barrier(jnp.mean(grad, axis=-1, keepdims=True))
    along = lax.optimization_barrier(jnp.mean(grad * normed, axis=-1, keepdims=True))
    return scale * (grad - centre - normed * along)

def reference(pair_input, norm_mean, norm_scale, pair_mask, cotangent, left_gate, left_value, right_gate, right_value, output_gate, output_weight):
    normed = (pair_input.astype(jnp.float32) - norm_mean[:, :, None]) * norm_scale[:, :, None]
    normed_low = normed.astype(jnp.bfloat16)
    stacked = jnp.concatenate([left_gate, left_value, right_gate, right_value, output_gate], axis=1)
    projected = jnp.dot(normed_low.reshape(TOKENS * TOKENS, PAIR), stacked, preferred_element_type=jnp.float32)
    keep = pair_mask.reshape(TOKENS * TOKENS, 1).astype(jnp.float32)
    left_sig = jax.nn.sigmoid(projected[:, :HIDDEN_SIZE])
    left_lin = projected[:, HIDDEN_SIZE:2 * HIDDEN_SIZE]
    right_sig = jax.nn.sigmoid(projected[:, 2 * HIDDEN_SIZE:3 * HIDDEN_SIZE])
    right_lin = projected[:, 3 * HIDDEN_SIZE:4 * HIDDEN_SIZE]
    out_sig = jax.nn.sigmoid(projected[:, 4 * HIDDEN_SIZE:])
    left_edge = (left_sig * left_lin * keep).astype(jnp.bfloat16).reshape(TOKENS, TOKENS, HIDDEN_SIZE)
    right_edge = (right_sig * right_lin * keep).astype(jnp.bfloat16).reshape(TOKENS, TOKENS, HIDDEN_SIZE)
    left_wide = left_edge.astype(jnp.float32)
    right_wide = right_edge.astype(jnp.float32)
    mixed = jnp.einsum('ikh,jkh->ijh', left_wide, right_wide)
    centred = mixed - lax.optimization_barrier(jnp.mean(mixed, axis=-1, keepdims=True))
    mix_scale = jax.lax.rsqrt(lax.optimization_barrier(jnp.mean(centred * centred, axis=-1, keepdims=True)) + epsilon)
    mix_normed = centred * mix_scale
    out_lin = jnp.dot(mix_normed.astype(jnp.bfloat16).reshape(TOKENS * TOKENS, HIDDEN_SIZE), output_weight, preferred_element_type=jnp.float32)
    upstream = cotangent.reshape(TOKENS * TOKENS, PAIR).astype(jnp.float32)
    grad_y = (upstream * out_sig).astype(jnp.bfloat16)
    grad_gate = upstream * out_lin * out_sig * (1.0 - out_sig)
    grad_mixnorm = jnp.dot(grad_y, output_weight.T, preferred_element_type=jnp.float32).reshape(TOKENS, TOKENS, HIDDEN_SIZE)
    grad_mix = layer_back(grad_mixnorm, mix_normed, mix_scale).astype(jnp.bfloat16)
    grad_wide = grad_mix.astype(jnp.float32)
    grad_left = jnp.einsum('ijh,jkh->ikh', grad_wide, right_wide).reshape(TOKENS * TOKENS, HIDDEN_SIZE) * keep
    grad_right = jnp.einsum('ijh,ikh->jkh', grad_wide, left_wide).reshape(TOKENS * TOKENS, HIDDEN_SIZE) * keep
    pre_grads = jnp.concatenate([grad_left * left_lin * left_sig * (1.0 - left_sig), grad_left * left_sig, grad_right * right_lin * right_sig * (1.0 - right_sig), grad_right * right_sig, grad_gate], axis=1).astype(jnp.bfloat16)
    grad_normed = jnp.dot(pre_grads, stacked.T, preferred_element_type=jnp.float32).reshape(TOKENS, TOKENS, PAIR)
    return layer_back(grad_normed, normed, norm_scale[:, :, None])
```

```python
import jax
import jax.numpy as jnp
from jax import lax
from jax.experimental import pallas as pl
from jax.experimental.pallas import tpu as pltpu
from jax.sharding import Mesh, PartitionSpec as P

epsilon = 1e-05
SIDE = 24
BLOCKS = 16
PAIRS = SIDE * SIDE
WIDTH = 128
HALF = 64
XS = 4
QUARTER = XS * SIDE
TOKENS = SIDE * BLOCKS
SPREAD = ("x", "z_hi", "y")
f32 = jnp.float32
bf16 = jnp.bfloat16


def dot(a, b, over=((1,), (0,))):
    return lax.dot_general(a, b, (over, ((), ())), preferred_element_type=f32)


def columns(ref):
    turned = jnp.transpose(ref[...].astype(f32))
    return jnp.concatenate([turned[:, i : i + 1] for i in range(SIDE)], axis=0)


def lanes(rows):
    return lax.broadcasted_iota(jnp.int32, (rows, WIDTH), 1)


def roll(value, by):
    by = by % WIDTH
    return value if by == 0 else pltpu.roll(value, by, 1)


def place(c):
    return ((c // 8) * 2 + c % 2) * XS + (c // 2) % XS


def layer_back(grad, normed, scale):
    centre = jnp.mean(grad, axis=-1, keepdims=True)
    along = jnp.mean(grad * normed, axis=-1, keepdims=True)
    return scale * (grad - centre - normed * along)


def spread_rows(parts, scratch):
    count = len(parts)
    step = count * SIDE
    per = WIDTH // step if count == 2 else 4
    low = lanes(HALF) < step
    for first in range(0, SIDE, per):
        stack = []
        for i in range(first, first + per):
            stack += [part[i * SIDE : (i + 1) * SIDE] for part in parts]
        stack.append(jnp.zeros((WIDTH - per * step, WIDTH), f32))
        turned = jnp.transpose(jnp.concatenate(stack, axis=0))
        for p in range(per):
            row = jnp.where(low, roll(turned[:HALF], -p * step), roll(turned[HALF:], step - p * step))
            scratch[pl.ds(first + p, HALF, stride=SIDE), :] = row


def gather_rows(scratch, combine):
    low = lanes(SIDE) < HALF
    found = []
    for first in range(0, SIDE, 2):
        stack = [scratch[pl.ds(first + p, HALF, stride=SIDE), :] for p in range(2)]
        pairs = combine(jnp.transpose(jnp.concatenate(stack, axis=0)))
        found.append([jnp.where(low, a, roll(b, HALF)) for a, b in pairs])
        found.append([jnp.where(low, roll(a, HALF), b) for a, b in pairs])
    return [jnp.concatenate([row[n] for row in found], axis=0) for n in range(len(found[0]))]


def assemble(messages, x, offset, spot):
    lane = lanes(SIDE)
    order = {spot(c): c for c in range(BLOCKS)}
    tiles = []
    for t in range(TOKENS // WIDTH):
        tile = None
        for at in range(BLOCKS):
            begin, end = at * SIDE - t * WIDTH, (at + 1) * SIDE - t * WIDTH
            if end <= 0 or begin >= WIDTH:
                continue
            piece = roll(messages(x * BLOCKS + order[at]), begin - offset)
            tile = piece if tile is None else jnp.where(lane >= begin, piece, tile)
        tiles.append(tile)
    return jnp.concatenate(tiles, axis=1)


def extract(wide, at, offset):
    begin = at * SIDE
    first, last = begin // WIDTH, (begin + SIDE - 1) // WIDTH
    shift = offset - begin
    piece = roll(wide[:, first * WIDTH : (first + 1) * WIDTH], shift)
    if last != first:
        other = roll(wide[:, last * WIDTH : (last + 1) * WIDTH], shift)
        piece = jnp.where(lanes(SIDE) < offset + last * WIDTH - begin, piece, other)
    return piece


def normalise(pair_ref, mean_ref, scale_ref):
    scale = columns(scale_ref)
    normed = (pair_ref[...].astype(f32) - columns(mean_ref)) * scale
    return normed, scale


def edges_kernel(pair_ref, mean_ref, scale_ref, mask_ref, lg, lv, rg, rv, out_ref, scratch):
    normed, _ = normalise(pair_ref, mean_ref, scale_ref)
    low = normed.astype(bf16)
    keep = columns(mask_ref)
    left = jax.nn.sigmoid(dot(low, lg[...])) * dot(low, lv[...]) * keep
    right = jax.nn.sigmoid(dot(low, rg[...])) * dot(low, rv[...]) * keep
    spread_rows([left, right], scratch)
    out_ref[...] = scratch[...].reshape(HALF, SIDE, WIDTH).astype(bf16)


def assemble_kernel(edge, in_ref, out_ref):
    for x in range(XS):
        for ch in range(2):
            wide = assemble(lambda n: in_ref[n].astype(f32), x, (2 * ch + edge) * SIDE, lambda c: c)
            out_ref[ch, x * SIDE : (x + 1) * SIDE, :] = wide.astype(bf16)


def mixed_kernel(left_ref, r0, r1, r2, r3, right_ref, out_ref):
    own = lax.axis_index("z_lo") * 2 + lax.axis_index("core")
    for p, part in enumerate((r0, r1, r2, r3)):
        right_ref[own ^ p] = part[...]
    mixed = []
    for ch in range(2):
        right = right_ref[:, ch].reshape(TOKENS, TOKENS)
        mixed.append(dot(left_ref[ch], right, ((1,), (1,))))
    lane = lanes(SIDE)
    for x in range(XS):
        rows = [m[x * SIDE : (x + 1) * SIDE] for m in mixed]
        for c in range(BLOCKS):
            both = jnp.where(lane < SIDE, extract(rows[0], place(c), 0), extract(rows[1], place(c), SIDE))
            high = both.astype(bf16).astype(f32)
            rest = roll(both - high, 2 * SIDE)
            out_ref[x * BLOCKS + c] = jnp.where(lane < 2 * SIDE, high, rest).astype(bf16)


def middle_kernel(
    in_ref, pair_ref, mean_ref, scale_ref, cot_ref, gate_ref, weight_ref, out_ref, grad_gate_ref, scratch
):
    scratch[...] = in_ref[...].astype(f32).reshape(HALF * SIDE, WIDTH)

    def combine(turned):
        both = turned[: 2 * SIDE] + turned[2 * SIDE : 4 * SIDE]
        return [(both[:SIDE], both[SIDE:])]

    (mixed,) = gather_rows(scratch, combine)
    normed, _ = normalise(pair_ref, mean_ref, scale_ref)
    out_sig = jax.nn.sigmoid(dot(normed.astype(bf16), gate_ref[...]))
    upstream = cot_ref[...].astype(f32)
    grad_y = (upstream * out_sig).astype(bf16)
    grad_mixnorm = dot(grad_y, weight_ref[...], ((1,), (1,)))
    centred = mixed - jnp.mean(mixed, axis=-1, keepdims=True)
    mix_scale = lax.rsqrt(jnp.mean(centred * centred, axis=-1, keepdims=True) + epsilon)
    mix_normed = centred * mix_scale
    out_lin = dot(mix_normed.astype(bf16), weight_ref[...])
    grad_gate_ref[...] = (upstream * out_lin * out_sig * (1.0 - out_sig)).astype(bf16)
    grad_mix = layer_back(grad_mixnorm, mix_normed, mix_scale)
    spread_rows([grad_mix], scratch)
    out_ref[...] = scratch[...].reshape(HALF, SIDE, WIDTH).astype(bf16)


def right_grad_kernel(in_ref, left_ref, grad_ref, own_ref, s1, s2, s3):
    for ch in range(2):
        for x in range(XS):
            wide = assemble(lambda n: in_ref[n].astype(f32), x, ch * SIDE, place)
            grad_ref[ch, x * SIDE : (x + 1) * SIDE, :] = wide.astype(bf16)
    own = lax.axis_index("z_lo") * 2 + lax.axis_index("core")
    for ch in range(2):
        turned = jnp.transpose(grad_ref[ch].astype(f32)).astype(bf16)
        s1_s = dot(turned, left_ref[ch])
        for q in range(4):
            rows = s1_s[q * QUARTER : (q + 1) * QUARTER]
            for p, ref in enumerate((own_ref, s1, s2, s3)):

                @pl.when((own ^ p) == q)
                def _(rows=rows, ref=ref, ch=ch):
                    ref[ch] = rows.astype(ref.dtype)


def left_grad_kernel(grad_ref, right_ref, out_ref):
    for ch in range(2):
        right = right_ref[:, ch].reshape(TOKENS, TOKENS)
        out_ref[ch] = dot(grad_ref[ch], right)


def return_kernel(left_ref, r0, r1, r2, r3, out_ref):
    lane = lanes(SIDE)
    for x in range(XS):
        here = slice(x * SIDE, (x + 1) * SIDE)
        wides = []
        for ch in range(2):
            total = r0[ch, here]
            for part in (r1, r2, r3):
                total = total + part[ch, here].astype(f32)
            wides += [left_ref[ch, here], total]
        for c in range(BLOCKS):
            tile = extract(wides[0], c, 0)
            for n in range(1, 4):
                tile = jnp.where(lane >= n * SIDE, extract(wides[n], c, n * SIDE), tile)
            out_ref[x * BLOCKS + c] = tile.astype(bf16)


def last_kernel(
    in_ref, pair_ref, mean_ref, scale_ref, mask_ref, grad_gate_ref, lg, lv, rg, rv, og, out_ref, scratch
):
    scratch[...] = in_ref[...].astype(f32).reshape(HALF * SIDE, WIDTH)

    def combine(turned):
        cut = [turned[n * SIDE : (n + 1) * SIDE] for n in range(4)]
        return [(cut[0], cut[2]), (cut[1], cut[3])]

    grad_left, grad_right = gather_rows(scratch, combine)
    normed, scale = normalise(pair_ref, mean_ref, scale_ref)
    low = normed.astype(bf16)
    keep = columns(mask_ref)
    over = ((1,), (1,))
    grad_normed = dot(grad_gate_ref[...], og[...], over)
    for grad, gate, value in ((grad_left, lg, lv), (grad_right, rg, rv)):
        sig = jax.nn.sigmoid(dot(low, gate[...]))
        lin = dot(low, value[...])
        kept = grad * keep
        grad_normed += dot((kept * lin * sig * (1.0 - sig)).astype(bf16), gate[...], over)
        grad_normed += dot((kept * sig).astype(bf16), value[...], over)
    out_ref[...] = layer_back(grad_normed, normed, scale)


def call(kernel, outs, *args, scratch=False, name=None):
    return pl.pallas_call(
        kernel,
        out_shape=[jax.ShapeDtypeStruct(shape, dtype) for shape, dtype in outs],
        in_specs=[pl.BlockSpec(memory_space=pltpu.VMEM) for _ in args],
        out_specs=[pl.BlockSpec(memory_space=pltpu.VMEM) for _ in outs],
        scratch_shapes=[pltpu.VMEM((HALF * SIDE, WIDTH), f32)] if scratch else [],
        compiler_params=pltpu.CompilerParams(vmem_limit_bytes=48 * 1024 * 1024),
        name=name,
    )(*args)


def spread(messages):
    return lax.all_to_all(messages, SPREAD, 0, 0, tiled=True)


def swap(value, axis):
    return lax.ppermute(value, axis, [(0, 1), (1, 0)])


def per_device(
    pair_input,
    norm_mean,
    norm_scale,
    pair_mask,
    cotangent,
    left_gate,
    left_value,
    right_gate,
    right_value,
    output_gate,
    output_weight,
):
    pair = pair_input.reshape(PAIRS, WIDTH)
    cot = cotangent.reshape(PAIRS, WIDTH)
    message = ((HALF, SIDE, WIDTH), bf16)
    panel = ((2, QUARTER, TOKENS), bf16)
    (sent,) = call(
        edges_kernel, [message], pair, norm_mean, norm_scale, pair_mask, left_gate, left_value, right_gate, right_value,
        scratch=True, name="edges",
    )
    came = spread(sent)
    (right_own,) = call(lambda *r: assemble_kernel(1, *r), [panel], came, name="take_right")
    right_z = swap(right_own, "z_lo")
    right_core = swap(right_own, "core")
    (left,) = call(lambda *r: assemble_kernel(0, *r), [panel], came, name="take_left")
    right_both = swap(right_z, "core")
    right, sent = call(
        mixed_kernel, [((4, 2, QUARTER, TOKENS), bf16), message], left, right_own, right_core, right_z, right_both,
        name="mix",
    )
    came = spread(sent)
    sent, grad_gate = call(
        middle_kernel, [message, ((PAIRS, WIDTH), bf16)], came, pair, norm_mean, norm_scale, cot, output_gate,
        output_weight, scratch=True, name="middle",
    )
    came = spread(sent)
    grad, own, s1, s2, s3 = call(
        right_grad_kernel, [panel, ((2, QUARTER, TOKENS), f32), panel, panel, panel], came, left, name="right_grad"
    )
    s3 = lax.ppermute(s3, ("z_lo", "core"), [(0, 3), (3, 0), (1, 2), (2, 1)])
    s2 = swap(s2, "z_lo")
    s1 = swap(s1, "core")
    (grad_left,) = call(left_grad_kernel, [((2, QUARTER, TOKENS), f32)], grad, right, name="left_grad")
    (sent,) = call(return_kernel, [message], grad_left, own, s1, s2, s3, name="return")
    came = spread(sent)
    (out,) = call(
        last_kernel, [((PAIRS, WIDTH), f32)], came, pair, norm_mean, norm_scale, pair_mask, grad_gate, left_gate,
        left_value, right_gate, right_value, output_gate, scratch=True, name="last",
    )
    return out.reshape(SIDE, SIDE, WIDTH)


def solution(mesh):
    fine = Mesh(mesh.devices.reshape(2, 4, 2, 4, 4), ("z_lo", "x", "core", "z_hi", "y"))
    row, col = ("z_lo", "x", "core"), ("z_hi", "y")
    placed = (P(row, col, None), P(row, col), P(row, col), P(row, col), P(row, col, None)) + (P(),) * 6
    return jax.shard_map(per_device, mesh=fine, in_specs=placed, out_specs=P(row, col, None), check_vma=False)
```

```python
import jax
import jax.numpy as jnp
from jax import lax
from jax.experimental import pallas as pl
from jax.experimental.pallas import tpu as pltpu
from jax.sharding import Mesh, PartitionSpec as P

epsilon = 1e-05
SIDE = 24
BLOCKS = 16
PAIRS = SIDE * SIDE
WIDTH = 128
GROUPS = 8
HALF = GROUPS * SIDE
TOKENS = SIDE * BLOCKS
SPREAD = ("z_lo", "x", "z_hi", "y")
TILES = TOKENS // WIDTH
ALONE, PAIRED = 6, 5
f32 = jnp.float32
bf16 = jnp.bfloat16
VMEM = pl.BlockSpec(memory_space=pltpu.VMEM)
HBM = pl.BlockSpec(memory_space=pltpu.HBM)


def dot(a, b, over=((1,), (0,))):
    return lax.dot_general(a, b, (over, ((), ())), preferred_element_type=f32)


def columns(ref):
    turned = jnp.transpose(ref[...].astype(f32))
    return jnp.concatenate([turned[:, i : i + 1] for i in range(SIDE)], axis=0)


def lanes(rows):
    return lax.broadcasted_iota(jnp.int32, (rows, WIDTH), 1)


def roll(value, by):
    by = by % WIDTH
    return value if by == 0 else pltpu.roll(value, by, 1)


def place(c):
    return (c % 2) * GROUPS + c // 2


def layer_back(grad, normed, scale):
    centre = jnp.mean(grad, axis=-1, keepdims=True)
    along = jnp.mean(grad * normed, axis=-1, keepdims=True)
    return scale * (grad - centre - normed * along)


def to_messages(parts, scratch):
    total = scratch.shape[0] // WIDTH
    lines = total // len(parts)
    for p, part in enumerate(parts):
        for r in range(lines):
            stack = [part[i * SIDE : (i + 1) * SIDE] for i in range(r, SIDE, lines)]
            stack.append(jnp.zeros((WIDTH - len(stack) * SIDE, WIDTH), f32))
            turned = jnp.transpose(jnp.concatenate(stack, axis=0))
            scratch[pl.ds(lines * p + r, WIDTH, stride=total), :] = turned
    return scratch[...].astype(bf16)


def from_messages(in_ref, scratch, count):
    total = in_ref.shape[0] // WIDTH
    lines = total // count
    scratch[...] = in_ref[...].astype(f32)
    parts = []
    for p in range(count):
        rows = [None] * SIDE
        for r in range(lines):
            turned = jnp.transpose(scratch[pl.ds(lines * p + r, WIDTH, stride=total), :])
            for n, i in enumerate(range(r, SIDE, lines)):
                rows[i] = turned[n * SIDE : (n + 1) * SIDE]
        parts.append(jnp.concatenate(rows, axis=0))
    return parts


def assemble(scratch, panels, lines, first, spot):
    total = scratch.shape[0] // WIDTH
    lane = lanes(GROUPS)
    order = {spot(c): c for c in range(BLOCKS)}
    for r in range(lines):
        found = [scratch[pl.ds(c * total + first + r, GROUPS, stride=BLOCKS * total), :] for c in range(BLOCKS)]
        for n, i in enumerate(range(r, SIDE, lines)):
            for t in range(TILES):
                tile = None
                for at in range(BLOCKS):
                    begin, end = at * SIDE - t * WIDTH, (at + 1) * SIDE - t * WIDTH
                    if end <= 0 or begin >= WIDTH:
                        continue
                    piece = roll(found[order[at]], begin - n * SIDE)
                    tile = piece if tile is None else jnp.where(lane >= begin, piece, tile)
                panels[t, pl.ds(i, GROUPS, stride=SIDE), :] = tile


def whole(panels):
    return jnp.concatenate([panels[t] for t in range(TILES)], axis=1)


def fill(panels, value):
    for t in range(TILES):
        panels[t] = value[:, t * WIDTH : (t + 1) * WIDTH]


def disassemble(panels, scratch, lines, first, spot):
    total = scratch.shape[0] // WIDTH
    lane = lanes(GROUPS)
    for c in range(BLOCKS):
        begin = spot(c) * SIDE
        t, after = begin // WIDTH, (begin + SIDE - 1) // WIDTH
        for r in range(lines):
            line = None
            for n, i in enumerate(range(r, SIDE, lines)):
                rows = pl.ds(i, GROUPS, stride=SIDE)
                shift = n * SIDE - begin
                piece = roll(panels[t, rows, :], shift)
                if after != t:
                    border = n * SIDE + after * WIDTH - begin
                    piece = jnp.where(lane < border, piece, roll(panels[after, rows, :], shift))
                line = piece if line is None else jnp.where(lane >= n * SIDE, piece, line)
            scratch[pl.ds(c * total + first + r, GROUPS, stride=BLOCKS * total), :] = line


def normalise(pair_ref, mean_ref, scale_ref):
    scale = columns(scale_ref)
    normed = (pair_ref[...].astype(f32) - columns(mean_ref)) * scale
    return normed, scale


def edges_kernel(*refs):
    given, out_ref, scratch, held, sems = refs[:8], refs[8], refs[9], refs[10:18], refs[18]
    copies = [pltpu.make_async_copy(a, b, sems.at[n]) for n, (a, b) in enumerate(zip(given, held))]
    for copy in copies:
        copy.start()
    for copy in copies:
        copy.wait()
    pair_ref, mean_ref, scale_ref, mask_ref, lg, lv, rg, rv = held
    normed, _ = normalise(pair_ref, mean_ref, scale_ref)
    low = normed.astype(bf16)
    keep = columns(mask_ref)
    left = jax.nn.sigmoid(dot(low, lg[...])) * dot(low, lv[...]) * keep
    right = jax.nn.sigmoid(dot(low, rg[...])) * dot(low, rv[...]) * keep
    out_ref[...] = to_messages([left, right], scratch)


def assemble_kernel(edge, in_ref, out_ref, scratch, panels):
    scratch[...] = in_ref[...].astype(f32)
    assemble(scratch, panels, PAIRED, edge * PAIRED, lambda c: c)
    out_ref[...] = whole(panels).astype(bf16)


def mixed_kernel(left_ref, own_ref, other_ref, right_ref, out_ref, scratch, panels):
    core = lax.axis_index("core")
    right_ref[core] = own_ref[...]
    right_ref[1 - core] = other_ref[...]
    fill(panels, dot(left_ref[...], right_ref[...].reshape(TOKENS, TOKENS), ((1,), (1,))))
    disassemble(panels, scratch, ALONE, 0, place)
    out_ref[...] = scratch[...].astype(bf16)


def middle_kernel(
    in_ref, pair_ref, mean_ref, scale_ref, cot_ref, gate_ref, weight_ref, out_ref, grad_gate_ref, scratch
):
    (mixed,) = from_messages(in_ref, scratch, 1)
    normed, _ = normalise(pair_ref, mean_ref, scale_ref)
    out_sig = jax.nn.sigmoid(dot(normed.astype(bf16), gate_ref[...]))
    upstream = cot_ref[...].astype(f32)
    grad_y = (upstream * out_sig).astype(bf16)
    grad_mixnorm = dot(grad_y, weight_ref[...], ((1,), (1,)))
    centred = mixed - jnp.mean(mixed, axis=-1, keepdims=True)
    mix_scale = lax.rsqrt(jnp.mean(centred * centred, axis=-1, keepdims=True) + epsilon)
    mix_normed = centred * mix_scale
    out_lin = dot(mix_normed.astype(bf16), weight_ref[...])
    grad_gate_ref[...] = (upstream * out_lin * out_sig * (1.0 - out_sig)).astype(bf16)
    grad_mix = layer_back(grad_mixnorm, mix_normed, mix_scale)
    out_ref[...] = to_messages([grad_mix], scratch)


def right_grad_kernel(in_ref, left_ref, grad_ref, own_ref, sent_ref, scratch, panels, sums):
    scratch[...] = in_ref[...].astype(f32)
    assemble(scratch, panels, ALONE, 0, place)
    grad = whole(panels)
    grad_ref[...] = grad.astype(bf16)
    sums[...] = dot(jnp.transpose(grad).astype(bf16), left_ref[...]).reshape(2, HALF, TOKENS)
    core = lax.axis_index("core")
    own_ref[...] = sums[core]
    sent_ref[...] = sums[1 - core].astype(bf16)


def left_grad_kernel(grad_ref, right_ref, out_ref):
    out_ref[...] = dot(grad_ref[...], right_ref[...].reshape(TOKENS, TOKENS))


def return_kernel(left_ref, own_ref, other_ref, out_ref, scratch, panels):
    fill(panels, left_ref[...])
    disassemble(panels, scratch, PAIRED, 0, lambda c: c)
    fill(panels, own_ref[...] + other_ref[...].astype(f32))
    disassemble(panels, scratch, PAIRED, PAIRED, lambda c: c)
    out_ref[...] = scratch[...].astype(bf16)


def last_kernel(
    in_ref, pair_ref, mean_ref, scale_ref, mask_ref, grad_gate_ref, lg, lv, rg, rv, og, out_ref, scratch
):
    grad_left, grad_right = from_messages(in_ref, scratch, 2)
    normed, scale = normalise(pair_ref, mean_ref, scale_ref)
    low = normed.astype(bf16)
    keep = columns(mask_ref)
    over = ((1,), (1,))
    grad_normed = dot(grad_gate_ref[...], og[...], over)
    for grad, gate, value in ((grad_left, lg, lv), (grad_right, rg, rv)):
        sig = jax.nn.sigmoid(dot(low, gate[...]))
        lin = dot(low, value[...])
        kept = grad * keep
        grad_normed += dot((kept * lin * sig * (1.0 - sig)).astype(bf16), gate[...], over)
        grad_normed += dot((kept * sig).astype(bf16), value[...], over)
    out_ref[...] = layer_back(grad_normed, normed, scale)


def call(kernel, outs, *args, scratch=(), name=None, space=VMEM, limit=48):
    return pl.pallas_call(
        kernel,
        out_shape=[jax.ShapeDtypeStruct(shape, dtype) for shape, dtype in outs],
        in_specs=[space for _ in args],
        out_specs=[VMEM for _ in outs],
        scratch_shapes=list(scratch),
        compiler_params=pltpu.CompilerParams(vmem_limit_bytes=limit * 1024 * 1024),
        name=name,
    )(*args)


def spread(messages):
    paired = messages.reshape(WIDTH, -1, 2, WIDTH)
    return lax.all_to_all(paired, SPREAD, 0, 0, tiled=True).reshape(messages.shape)


def swap(value):
    return lax.ppermute(value, "core", [(0, 1), (1, 0)])


def per_device(
    pair_input,
    norm_mean,
    norm_scale,
    pair_mask,
    cotangent,
    left_gate,
    left_value,
    right_gate,
    right_value,
    output_gate,
    output_weight,
):
    pair = pair_input.reshape(PAIRS, WIDTH)
    cot = cotangent.reshape(PAIRS, WIDTH)
    one, two = (WIDTH * ALONE, WIDTH), (WIDTH * 2 * PAIRED, WIDTH)
    line_one, line_two = pltpu.VMEM(one, f32), pltpu.VMEM(two, f32)
    panels = pltpu.VMEM((TILES, HALF, WIDTH), f32)
    one, two = (one, bf16), (two, bf16)
    panel, wide = ((HALF, TOKENS), bf16), ((HALF, TOKENS), f32)
    given = [pair, norm_mean, norm_scale, pair_mask, left_gate, left_value, right_gate, right_value]
    held = [pltpu.VMEM(a.shape, a.dtype) for a in given]
    (sent,) = call(
        edges_kernel, [two], *given, scratch=[line_two] + held + [pltpu.SemaphoreType.DMA((len(given),))],
        name="edges", space=HBM, limit=60,
    )
    came = spread(sent)
    (right_own,) = call(lambda *r: assemble_kernel(1, *r), [panel], came, scratch=[line_two, panels], name="take_right")
    right_other = swap(right_own)
    (left,) = call(lambda *r: assemble_kernel(0, *r), [panel], came, scratch=[line_two, panels], name="take_left")
    right, sent = call(
        mixed_kernel, [((2, HALF, TOKENS), bf16), one], left, right_own, right_other, scratch=[line_one, panels],
        name="mix",
    )
    came = spread(sent)
    sent, grad_gate = call(
        middle_kernel, [one, ((PAIRS, WIDTH), bf16)], came, pair, norm_mean, norm_scale, cot, output_gate,
        output_weight, scratch=[line_one], name="middle",
    )
    came = spread(sent)
    grad, own, sent = call(
        right_grad_kernel, [panel, wide, panel], came, left,
        scratch=[line_one, panels, pltpu.VMEM((2, HALF, TOKENS), f32)],
        name="right_grad",
    )
    other = swap(sent)
    (grad_left,) = call(left_grad_kernel, [wide], grad, right, name="left_grad")
    (sent,) = call(return_kernel, [two], grad_left, own, other, scratch=[line_two, panels], name="return")
    came = spread(sent)
    (out,) = call(
        last_kernel, [((PAIRS, WIDTH), f32)], came, pair, norm_mean, norm_scale, pair_mask, grad_gate, left_gate,
        left_value, right_gate, right_value, output_gate, scratch=[line_two], name="last",
    )
    return out.reshape(SIDE, SIDE, WIDTH)


def solution(mesh):
    fine = Mesh(mesh.devices.reshape(2, 4, 2, 4, 4), ("z_lo", "x", "core", "z_hi", "y"))
    row, col = ("z_lo", "x", "core"), ("z_hi", "y")
    placed = (P(row, col, None), P(row, col), P(row, col), P(row, col), P(row, col, None)) + (P(),) * 6
    return jax.shard_map(per_device, mesh=fine, in_specs=placed, out_specs=P(row, col, None), check_vma=False)
```

```python
import jax
import jax.numpy as jnp
from jax import lax
from jax.experimental import pallas as pl
from jax.experimental.pallas import tpu as pltpu
from jax.sharding import Mesh, PartitionSpec as P

epsilon = 1e-05
SIDE = 24
BLOCKS = 16
PAIRS = SIDE * SIDE
WIDTH = 128
GROUPS = 8
HALF = GROUPS * SIDE
TOKENS = SIDE * BLOCKS
SPREAD = ("z_hi", "y", "z_lo", "x")
TILES = TOKENS // WIDTH
ALONE, PAIRED = 6, 5
f32 = jnp.float32
bf16 = jnp.bfloat16
VMEM = pl.BlockSpec(memory_space=pltpu.VMEM)
HBM = pl.BlockSpec(memory_space=pltpu.HBM)


def dot(a, b, over=((1,), (0,))):
    return lax.dot_general(a, b, (over, ((), ())), preferred_element_type=f32)


def spread_pairs(ref):
    turned = jnp.transpose(ref[...].astype(f32))
    return jnp.concatenate([jnp.broadcast_to(turned[:, i : i + 1], (SIDE, WIDTH)) for i in range(SIDE)], axis=0)


def lanes(rows):
    return lax.broadcasted_iota(jnp.int32, (rows, WIDTH), 1)


def roll(value, by):
    by = by % WIDTH
    return value if by == 0 else pltpu.roll(value, by, 1)


def place(c):
    return (c % 2) * GROUPS + c // 2


def layer_back(grad, normed, scale):
    centre = jnp.mean(grad, axis=-1, keepdims=True)
    along = jnp.mean(grad * normed, axis=-1, keepdims=True)
    return scale * (grad - centre - normed * along)


def to_messages(parts, scratch):
    total = scratch.shape[0] // WIDTH
    lines = total // len(parts)
    for p, part in enumerate(parts):
        for r in range(lines):
            stack = [part[i * SIDE : (i + 1) * SIDE] for i in range(r, SIDE, lines)]
            stack.append(jnp.zeros((WIDTH - len(stack) * SIDE, WIDTH), f32))
            turned = jnp.transpose(jnp.concatenate(stack, axis=0))
            scratch[pl.ds(lines * p + r, WIDTH, stride=total), :] = turned
    return scratch[...].astype(bf16)


def from_messages(in_ref, scratch, count):
    total = in_ref.shape[0] // WIDTH
    lines = total // count
    scratch[...] = in_ref[...].astype(f32)
    parts = []
    for p in range(count):
        rows = [None] * SIDE
        for r in range(lines):
            turned = jnp.transpose(scratch[pl.ds(lines * p + r, WIDTH, stride=total), :])
            for n, i in enumerate(range(r, SIDE, lines)):
                rows[i] = turned[n * SIDE : (n + 1) * SIDE]
        parts.append(jnp.concatenate(rows, axis=0))
    return parts


def assemble(scratch, lines, first, spot, store):
    total = scratch.shape[0] // WIDTH
    lane = lanes(GROUPS)
    order = {spot(c): c for c in range(BLOCKS)}
    for r in range(lines):
        found = [scratch[pl.ds(c * GROUPS * total + first + r, GROUPS, stride=total), :] for c in range(BLOCKS)]
        for n, i in enumerate(range(r, SIDE, lines)):
            for t in range(TILES):
                tile = None
                for at in range(BLOCKS):
                    begin, end = at * SIDE - t * WIDTH, (at + 1) * SIDE - t * WIDTH
                    if end <= 0 or begin >= WIDTH:
                        continue
                    piece = roll(found[order[at]], begin - n * SIDE)
                    tile = piece if tile is None else jnp.where(lane >= begin, piece, tile)
                store(i, t, tile)


def disassemble(load, scratch, lines, first, blocks):
    total = scratch.shape[0] // (GROUPS * blocks)
    lane = lanes(GROUPS)
    for c in range(blocks):
        begin = c * SIDE
        t, after = begin // WIDTH, (begin + SIDE - 1) // WIDTH
        for r in range(lines):
            line = None
            for n, i in enumerate(range(r, SIDE, lines)):
                shift = n * SIDE - begin
                piece = roll(load(i, t), shift)
                if after != t:
                    border = n * SIDE + after * WIDTH - begin
                    piece = jnp.where(lane < border, piece, roll(load(i, after), shift))
                line = piece if line is None else jnp.where(lane >= n * SIDE, piece, line)
            scratch[pl.ds(c * GROUPS * total + first + r, GROUPS, stride=total), :] = line


def columns_of(t):
    return slice(t * WIDTH, (t + 1) * WIDTH)


def normalise(pair_ref, mean_ref, scale_ref):
    scale = spread_pairs(scale_ref)
    normed = (pair_ref[...].astype(f32) - spread_pairs(mean_ref)) * scale
    return normed, scale


def edges_kernel(*refs):
    given, out_ref, scratch, held, sems = refs[:8], refs[8], refs[9], refs[10:18], refs[18]
    copies = [pltpu.make_async_copy(a, b, sems.at[n]) for n, (a, b) in enumerate(zip(given, held))]
    for copy in copies:
        copy.start()
    for copy in copies:
        copy.wait()
    pair_ref, mean_ref, scale_ref, mask_ref, lg, lv, rg, rv = held
    normed, _ = normalise(pair_ref, mean_ref, scale_ref)
    low = normed.astype(bf16)
    keep = spread_pairs(mask_ref)
    parts = []
    for gate, value in ((lg, lv), (rg, rv)):
        both = dot(low, jnp.concatenate([gate[...], value[...]], axis=1))
        parts.append(jax.nn.sigmoid(both[:, :WIDTH]) * both[:, WIDTH:] * keep)
    out_ref[...] = to_messages(parts, scratch)


def take_right_kernel(in_ref, out_ref, scratch, panels):
    scratch[...] = in_ref[...].astype(f32)

    def store(i, t, tile):
        panels[t, pl.ds(i * (GROUPS + 1), GROUPS), :] = tile

    assemble(scratch, PAIRED, PAIRED, lambda c: c, store)
    for group in range(GROUPS):
        rows = [panels[t, pl.ds(group, SIDE, stride=GROUPS + 1), :] for t in range(TILES)]
        out_ref[group * SIDE : (group + 1) * SIDE, :] = jnp.concatenate(rows, axis=1).astype(bf16)


def assemble_left(in_ref, scratch, panel, lines, spot):
    scratch[...] = in_ref[...].astype(f32)

    def store(i, t, tile):
        panel[i * GROUPS : (i + 1) * GROUPS, columns_of(t)] = tile

    assemble(scratch, lines, 0, spot, store)


def rows_of(panel):
    return lambda i, t: panel[i * GROUPS : (i + 1) * GROUPS, columns_of(t)]


def take_left_kernel(in_ref, out_ref, scratch, panel):
    assemble_left(in_ref, scratch, panel, PAIRED, lambda c: c)
    out_ref[...] = panel[...].astype(bf16)


def half_mixed(left_ref, right_ref, scratch, panel):
    panel[:, :HALF] = dot(left_ref[...], right_ref[...], ((1,), (1,)))
    disassemble(rows_of(panel), scratch, ALONE, 0, BLOCKS // 2)


def mix_own_kernel(left_ref, right_ref, out_ref, panel):
    half_mixed(left_ref, right_ref, out_ref, panel)


def mix_kernel(left_ref, right_ref, own_ref, out_ref, scratch, panel):
    half_mixed(left_ref, right_ref, scratch, panel)
    first = lax.axis_index("core") == 0
    size = GROUPS * ALONE
    for n in range(BLOCKS // 2):
        here = slice(n * size, (n + 1) * size)
        own, other = own_ref[here, :], scratch[here, :]
        out_ref[2 * n * size : (2 * n + 1) * size, :] = jnp.where(first, own, other).astype(bf16)
        out_ref[(2 * n + 1) * size : (2 * n + 2) * size, :] = jnp.where(first, other, own).astype(bf16)


def ready_kernel(pair_ref, mean_ref, scale_ref, cot_ref, gate_ref, weight_ref, grad_ref, factor_ref):
    normed, _ = normalise(pair_ref, mean_ref, scale_ref)
    out_sig = jax.nn.sigmoid(dot(normed.astype(bf16), gate_ref[...]))
    grad_y = cot_ref[...].astype(f32) * out_sig
    grad_ref[...] = dot(grad_y.astype(bf16), weight_ref[...], ((1,), (1,)))
    factor_ref[...] = grad_y * (1.0 - out_sig)


def middle_kernel(in_ref, grad_ref, factor_ref, weight_ref, out_ref, grad_gate_ref, scratch):
    (mixed,) = from_messages(in_ref, scratch, 1)
    centred = mixed - jnp.mean(mixed, axis=-1, keepdims=True)
    mix_scale = lax.rsqrt(jnp.mean(centred * centred, axis=-1, keepdims=True) + epsilon)
    mix_normed = centred * mix_scale
    out_lin = dot(mix_normed.astype(bf16), weight_ref[...])
    grad_gate_ref[...] = (factor_ref[...] * out_lin).astype(bf16)
    grad_mix = layer_back(grad_ref[...], mix_normed, mix_scale)
    out_ref[...] = to_messages([grad_mix], scratch)


def right_grad_kernel(in_ref, left_ref, grad_ref, own_ref, sent_ref, scratch, panel, sums):
    assemble_left(in_ref, scratch, panel, ALONE, place)
    grad = panel[...]
    grad_ref[...] = grad.astype(bf16)
    sums[...] = dot(jnp.transpose(grad).astype(bf16), left_ref[...]).reshape(2, HALF, TOKENS)
    core = lax.axis_index("core")
    own_ref[...] = sums[core]
    sent_ref[...] = sums[1 - core].astype(bf16)


def left_grad_kernel(grad_ref, own_ref, other_ref, out_ref, right, panel):
    core = lax.axis_index("core")
    right[core] = own_ref[...]
    right[1 - core] = other_ref[...]
    panel[...] = dot(grad_ref[...], right[...].reshape(TOKENS, TOKENS))
    disassemble(rows_of(panel), out_ref, PAIRED, 0, BLOCKS)


def return_kernel(lines_ref, own_ref, other_ref, kept_ref, out_ref, panels):
    for group in range(GROUPS):
        here = slice(group * SIDE, (group + 1) * SIDE)
        total = own_ref[here, :] + other_ref[here, :].astype(f32)
        for t in range(TILES):
            panels[t, pl.ds(group * (SIDE + 1), SIDE), :] = total[:, columns_of(t)]
    load = lambda i, t: panels[t, pl.ds(i, GROUPS, stride=SIDE + 1), :]
    disassemble(load, kept_ref, PAIRED, PAIRED, BLOCKS)
    out_ref[...] = kept_ref[...].astype(bf16)


def prepare_kernel(
    pair_ref, mean_ref, scale_ref, mask_ref, grad_gate_ref, lg, lv, rg, rv, og, normed_ref, scaled_ref, base_ref, factors_ref
):
    normed, scale = normalise(pair_ref, mean_ref, scale_ref)
    normed_ref[...] = normed
    scaled_ref[...] = scale
    base_ref[...] = dot(grad_gate_ref[...], og[...], ((1,), (1,)))
    low = normed.astype(bf16)
    keep = spread_pairs(mask_ref)
    for n, (gate, value) in enumerate(((lg, lv), (rg, rv))):
        both = dot(low, jnp.concatenate([gate[...], value[...]], axis=1))
        sig, lin = jax.nn.sigmoid(both[:, :WIDTH]), both[:, WIDTH:]
        factors_ref[2 * n + 1] = keep * sig
        factors_ref[2 * n] = keep * lin * sig * (1.0 - sig)


def last_kernel(in_ref, normed_ref, scale_ref, base_ref, factors_ref, lg, lv, rg, rv, out_ref, scratch):
    grads = from_messages(in_ref, scratch, 2)
    grad_normed = base_ref[...]
    for n, (gate, value) in enumerate(((lg, lv), (rg, rv))):
        pre_grads = jnp.concatenate([grads[n] * factors_ref[2 * n], grads[n] * factors_ref[2 * n + 1]], axis=1)
        weights = jnp.concatenate([gate[...], value[...]], axis=1)
        grad_normed += dot(pre_grads.astype(bf16), weights, ((1,), (1,)))
    out_ref[...] = layer_back(grad_normed, normed_ref[...], scale_ref[...])


def call(kernel, outs, *args, scratch=(), name=None, space=VMEM, aliases={}):
    return pl.pallas_call(
        kernel,
        out_shape=[jax.ShapeDtypeStruct(shape, dtype) for shape, dtype in outs],
        in_specs=[space for _ in args],
        out_specs=[VMEM for _ in outs],
        scratch_shapes=list(scratch),
        input_output_aliases=aliases,
        compiler_params=pltpu.CompilerParams(vmem_limit_bytes=48 * 1024 * 1024),
        name=name,
    )(*args)


def spread(messages):
    paired = messages.reshape(WIDTH, -1, 2, WIDTH)
    return lax.all_to_all(paired, SPREAD, 0, 0, tiled=True).reshape(messages.shape)


def swap(value):
    return lax.ppermute(value, "core", [(0, 1), (1, 0)])


def per_device(
    pair_input,
    norm_mean,
    norm_scale,
    pair_mask,
    cotangent,
    left_gate,
    left_value,
    right_gate,
    right_value,
    output_gate,
    output_weight,
):
    pair = pair_input.reshape(PAIRS, WIDTH)
    cot = cotangent.reshape(PAIRS, WIDTH)
    one, two = (WIDTH * ALONE, WIDTH), (WIDTH * 2 * PAIRED, WIDTH)
    line_one, line_two = pltpu.VMEM(one, f32), pltpu.VMEM(two, f32)
    panel_left = pltpu.VMEM((HALF, TOKENS), f32)
    panels_in = pltpu.VMEM((TILES, SIDE * (GROUPS + 1), WIDTH), f32)
    panels_out = pltpu.VMEM((TILES, GROUPS * (SIDE + 1), WIDTH), f32)
    one, two = (one, bf16), (two, bf16)
    panel, wide = ((HALF, TOKENS), bf16), ((HALF, TOKENS), f32)
    given = [
        pltpu.with_memory_space_constraint(a, pltpu.HBM)
        for a in (pair, norm_mean, norm_scale, pair_mask, left_gate, left_value, right_gate, right_value)
    ]
    held = [pltpu.VMEM(a.shape, a.dtype) for a in given]
    (sent,) = call(
        edges_kernel, [two], *given, scratch=[line_two] + held + [pltpu.SemaphoreType.DMA((len(given),))],
        name="edges", space=HBM,
    )
    came = spread(sent)
    (right_own,) = call(take_right_kernel, [panel], came, scratch=[line_two, panels_in], name="take_right")
    right_other = swap(right_own)
    (left,) = call(take_left_kernel, [panel], came, scratch=[line_two, panel_left], name="take_left")
    line_half, panel_half = pltpu.VMEM((WIDTH * ALONE // 2, WIDTH), f32), pltpu.VMEM((HALF, 2 * WIDTH), f32)
    (mixed_own,) = call(
        mix_own_kernel, [((WIDTH * ALONE // 2, WIDTH), f32)], left, right_own, scratch=[panel_half], name="mix_own",
    )
    grad_mixnorm, factor = call(
        ready_kernel, [((PAIRS, WIDTH), f32)] * 2, pair, norm_mean, norm_scale, cot, output_gate, output_weight,
        name="ready",
    )
    mixed_own, grad_mixnorm, factor = lax.optimization_barrier((mixed_own, grad_mixnorm, factor))
    (sent,) = call(mix_kernel, [one], left, right_other, mixed_own, scratch=[line_half, panel_half], name="mix")
    came = spread(sent)
    sent, grad_gate = call(
        middle_kernel, [one, ((PAIRS, WIDTH), bf16)], came, grad_mixnorm, factor, output_weight, scratch=[line_one],
        name="middle",
    )
    came = spread(sent)
    grad, own, sent = call(
        right_grad_kernel, [panel, wide, panel], came, left,
        scratch=[line_one, panel_left, pltpu.VMEM((2, HALF, TOKENS), f32)],
        name="right_grad",
    )
    other = swap(sent)
    lined = ((WIDTH * 2 * PAIRED, WIDTH), f32)
    (lines,) = call(
        left_grad_kernel, [lined], grad, right_own, right_other,
        scratch=[pltpu.VMEM((2, HALF, TOKENS), bf16), panel_left], name="left_grad",
    )
    many = ((PAIRS, WIDTH), f32)
    prepared = call(
        prepare_kernel, [many, many, many, ((4, PAIRS, WIDTH), f32)], pair, norm_mean, norm_scale, pair_mask, grad_gate,
        left_gate, left_value, right_gate, right_value, output_gate, name="prepare",
    )
    lines, prepared = lax.optimization_barrier((lines, prepared))
    _, sent = call(return_kernel, [lined, two], lines, own, other, scratch=[panels_out], name="return", aliases={0: 0})
    came = spread(sent)
    (out,) = call(
        last_kernel, [many], came, *prepared, left_gate, left_value, right_gate, right_value, scratch=[line_two],
        name="last",
    )
    return out.reshape(SIDE, SIDE, WIDTH)


def solution(mesh):
    fine = Mesh(mesh.devices.reshape(2, 4, 2, 4, 4), ("z_lo", "x", "core", "z_hi", "y"))
    row, col = ("z_lo", "x", "core"), ("z_hi", "y")
    placed = (P(row, col, None), P(row, col), P(row, col), P(row, col), P(row, col, None)) + (P(),) * 6
    return jax.shard_map(per_device, mesh=fine, in_specs=placed, out_specs=P(row, col, None), check_vma=False)
```

```python
import jax
import jax.numpy as jnp
from jax import lax
from jax.experimental import pallas as pl
from jax.experimental.pallas import tpu as pltpu
from jax.sharding import Mesh, PartitionSpec as P

epsilon = 1e-05
SIDE = 24
BLOCKS = 16
PAIRS = SIDE * SIDE
WIDTH = 128
GROUPS = 8
HALF = GROUPS * SIDE
TOKENS = SIDE * BLOCKS
SPREAD = ("z_hi", "y", "z_lo", "x")
TILES = TOKENS // WIDTH
ALONE, PAIRED = 6, 5
f32 = jnp.float32
bf16 = jnp.bfloat16
VMEM = pl.BlockSpec(memory_space=pltpu.VMEM)
HBM = pl.BlockSpec(memory_space=pltpu.HBM)


def dot(a, b, over=((1,), (0,))):
    return lax.dot_general(a, b, (over, ((), ())), preferred_element_type=f32)


def spread_pairs(value):
    turned = jnp.transpose(value)
    return jnp.concatenate([jnp.broadcast_to(turned[:, i : i + 1], (SIDE, WIDTH)) for i in range(SIDE)], axis=0)


def lanes(rows):
    return lax.broadcasted_iota(jnp.int32, (rows, WIDTH), 1)


def roll(value, by):
    by = by % WIDTH
    return value if by == 0 else pltpu.roll(value, by, 1)


def place(c):
    return (c % 2) * GROUPS + c // 2


def layer_back(grad, normed, scale):
    centre = jnp.mean(grad, axis=-1, keepdims=True)
    along = jnp.mean(grad * normed, axis=-1, keepdims=True)
    return scale * (grad - centre - normed * along)


def rows_in(line, lines):
    many = -(-SIDE // lines)
    return range(line * many, min((line + 1) * many, SIDE))


def to_messages(parts, scratch):
    total = scratch.shape[0] // WIDTH
    lines = total // len(parts)
    for p, part in enumerate(parts):
        for r in range(lines):
            stack = [part[i * SIDE : (i + 1) * SIDE] for i in rows_in(r, lines)]
            stack.append(jnp.zeros((WIDTH - len(stack) * SIDE, WIDTH), f32))
            turned = jnp.transpose(jnp.concatenate(stack, axis=0))
            scratch[pl.ds(lines * p + r, WIDTH, stride=total), :] = turned
    return scratch[...].astype(bf16)


def from_messages(in_ref, scratch, count):
    total = in_ref.shape[0] // WIDTH
    lines = total // count
    scratch[...] = in_ref[...].astype(f32)
    parts = []
    for p in range(count):
        rows = [None] * SIDE
        for r in range(lines):
            turned = jnp.transpose(scratch[pl.ds(lines * p + r, WIDTH, stride=total), :])
            for n, i in enumerate(rows_in(r, lines)):
                rows[i] = turned[n * SIDE : (n + 1) * SIDE]
        parts.append(jnp.concatenate(rows, axis=0))
    return parts


def assemble(scratch, lines, first, spot, store):
    total = scratch.shape[0] // WIDTH
    lane = lanes(GROUPS)
    order = {spot(c): c for c in range(BLOCKS)}
    for r in range(lines):
        found = [scratch[pl.ds(c * GROUPS * total + first + r, GROUPS, stride=total), :] for c in range(BLOCKS)]
        for n, i in enumerate(rows_in(r, lines)):
            for t in range(TILES):
                tile = None
                for at in range(BLOCKS):
                    begin, end = at * SIDE - t * WIDTH, (at + 1) * SIDE - t * WIDTH
                    if end <= 0 or begin >= WIDTH:
                        continue
                    piece = roll(found[order[at]], begin - n * SIDE)
                    tile = piece if tile is None else jnp.where(lane >= begin, piece, tile)
                store(i, t, tile)


def disassemble(load, scratch, lines, first, blocks):
    total = scratch.shape[0] // (GROUPS * blocks)
    lane = lanes(GROUPS)
    for c in range(blocks):
        begin = c * SIDE
        t, after = begin // WIDTH, (begin + SIDE - 1) // WIDTH
        for r in range(lines):
            line = None
            for n, i in enumerate(rows_in(r, lines)):
                shift = n * SIDE - begin
                piece = roll(load(i, t), shift)
                if after != t:
                    border = n * SIDE + after * WIDTH - begin
                    piece = jnp.where(lane < border, piece, roll(load(i, after), shift))
                line = piece if line is None else jnp.where(lane >= n * SIDE, piece, line)
            scratch[pl.ds(c * GROUPS * total + first + r, GROUPS, stride=total), :] = line


def columns_of(t):
    return slice(t * WIDTH, (t + 1) * WIDTH)


def normalise(pair_ref, mean_ref, scale_ref):
    scale = spread_pairs(scale_ref[...])
    normed = (pair_ref[...].astype(f32) - spread_pairs(mean_ref[...])) * scale
    return normed, scale


def edges_kernel(*refs):
    given, out_ref, scratch, held, sems = refs[:8], refs[8], refs[9], refs[10:18], refs[18]
    copies = [pltpu.make_async_copy(a, b, sems.at[n]) for n, (a, b) in enumerate(zip(given, held))]
    for copy in copies:
        copy.start()
    for copy in copies:
        copy.wait()
    pair_ref, mean_ref, scale_ref, mask_ref, lg, lv, rg, rv = held
    kept_scale = spread_pairs(scale_ref[...] * mask_ref[...].astype(f32))
    low = ((pair_ref[...].astype(f32) - spread_pairs(mean_ref[...])) * kept_scale).astype(bf16)
    parts = []
    for gate, value in ((lg, lv), (rg, rv)):
        both = dot(low, jnp.concatenate([gate[...], value[...]], axis=1))
        parts.append(jax.nn.sigmoid(both[:, :WIDTH]) * both[:, WIDTH:])
    out_ref[...] = to_messages(parts, scratch)


def take_right_kernel(in_ref, out_ref, scratch, panels):
    scratch[...] = in_ref[...].astype(f32)

    def store(i, t, tile):
        panels[t, pl.ds(i * (GROUPS + 1), GROUPS), :] = tile

    assemble(scratch, PAIRED, PAIRED, lambda c: c, store)
    for group in range(GROUPS):
        rows = [panels[t, pl.ds(group, SIDE, stride=GROUPS + 1), :] for t in range(TILES)]
        out_ref[group * SIDE : (group + 1) * SIDE, :] = jnp.concatenate(rows, axis=1).astype(bf16)


def assemble_left(in_ref, scratch, panel, lines, spot):
    scratch[...] = in_ref[...].astype(f32)

    def store(i, t, tile):
        panel[i * GROUPS : (i + 1) * GROUPS, columns_of(t)] = tile

    assemble(scratch, lines, 0, spot, store)


def rows_of(panel):
    return lambda i, t: panel[i * GROUPS : (i + 1) * GROUPS, columns_of(t)]


def take_left_kernel(in_ref, out_ref, scratch, panel):
    assemble_left(in_ref, scratch, panel, PAIRED, lambda c: c)
    out_ref[...] = panel[...].astype(bf16)


def half_mixed(left_ref, right_ref, scratch, panel):
    panel[:, :HALF] = dot(left_ref[...], right_ref[...], ((1,), (1,)))
    disassemble(rows_of(panel), scratch, ALONE, 0, BLOCKS // 2)


def mix_own_kernel(left_ref, right_ref, out_ref, panel):
    half_mixed(left_ref, right_ref, out_ref, panel)


def mix_kernel(left_ref, right_ref, own_ref, out_ref, scratch, panel):
    half_mixed(left_ref, right_ref, scratch, panel)
    first = lax.axis_index("core") == 0
    size = GROUPS * ALONE
    for n in range(BLOCKS // 2):
        here = slice(n * size, (n + 1) * size)
        own, other = own_ref[here, :], scratch[here, :]
        out_ref[2 * n * size : (2 * n + 1) * size, :] = jnp.where(first, own, other).astype(bf16)
        out_ref[(2 * n + 1) * size : (2 * n + 2) * size, :] = jnp.where(first, other, own).astype(bf16)


def ready_kernel(pair_ref, mean_ref, scale_ref, cot_ref, gate_ref, weight_ref, grad_ref, factor_ref):
    normed, _ = normalise(pair_ref, mean_ref, scale_ref)
    out_sig = jax.nn.sigmoid(dot(normed.astype(bf16), gate_ref[...]))
    grad_y = cot_ref[...].astype(f32) * out_sig
    grad_ref[...] = dot(grad_y.astype(bf16), weight_ref[...], ((1,), (1,)))
    factor_ref[...] = grad_y * (1.0 - out_sig)


def middle_kernel(in_ref, grad_ref, factor_ref, weight_ref, out_ref, grad_gate_ref, scratch):
    (mixed,) = from_messages(in_ref, scratch, 1)
    centred = mixed - jnp.mean(mixed, axis=-1, keepdims=True)
    mix_scale = lax.rsqrt(jnp.mean(centred * centred, axis=-1, keepdims=True) + epsilon)
    mix_normed = centred * mix_scale
    out_lin = dot(mix_normed.astype(bf16), weight_ref[...])
    grad_gate_ref[...] = (factor_ref[...] * out_lin).astype(bf16)
    grad_mix = layer_back(grad_ref[...], mix_normed, mix_scale)
    out_ref[...] = to_messages([grad_mix], scratch)


def right_grad_kernel(in_ref, left_ref, grad_ref, own_ref, sent_ref, scratch, panel):
    assemble_left(in_ref, scratch, panel, ALONE, place)
    grad = panel[...]
    grad_ref[...] = grad.astype(bf16)
    first = lax.axis_index("core") == 0
    sums = dot(jnp.transpose(grad).astype(bf16), left_ref[...])
    own_ref[...] = jnp.where(first, sums[:HALF], sums[HALF:])
    sent_ref[...] = jnp.where(first, sums[HALF:], sums[:HALF]).astype(bf16)


def left_grad_kernel(grad_ref, own_ref, other_ref, out_ref, right, panel):
    core = lax.axis_index("core")
    right[core] = own_ref[...]
    right[1 - core] = other_ref[...]
    panel[...] = dot(grad_ref[...], right[...].reshape(TOKENS, TOKENS))
    disassemble(rows_of(panel), out_ref, PAIRED, 0, BLOCKS)


def return_kernel(lines_ref, own_ref, other_ref, kept_ref, out_ref, panels):
    for group in range(GROUPS):
        here = slice(group * SIDE, (group + 1) * SIDE)
        total = own_ref[here, :] + other_ref[here, :].astype(f32)
        for t in range(TILES):
            panels[t, pl.ds(group * (SIDE + 1), SIDE), :] = total[:, columns_of(t)]
    load = lambda i, t: panels[t, pl.ds(i, GROUPS, stride=SIDE + 1), :]
    disassemble(load, kept_ref, PAIRED, PAIRED, BLOCKS)
    out_ref[...] = kept_ref[...].astype(bf16)


def prepare_kernel(
    pair_ref, mean_ref, scale_ref, mask_ref, grad_gate_ref, lg, lv, rg, rv, og, normed_ref, scaled_ref, base_ref, factors_ref
):
    normed, scale = normalise(pair_ref, mean_ref, scale_ref)
    normed_ref[...] = normed
    scaled_ref[...] = scale
    base_ref[...] = dot(grad_gate_ref[...], og[...], ((1,), (1,)))
    low = normed.astype(bf16)
    keep = spread_pairs(mask_ref[...].astype(f32))
    for n, (gate, value) in enumerate(((lg, lv), (rg, rv))):
        both = dot(low, jnp.concatenate([gate[...], value[...]], axis=1))
        sig, lin = jax.nn.sigmoid(both[:, :WIDTH]), both[:, WIDTH:]
        factors_ref[2 * n + 1] = keep * sig
        factors_ref[2 * n] = keep * lin * sig * (1.0 - sig)


def last_kernel(
    in_ref, normed_ref, scale_ref, base_ref, factors_ref, lg, lv, rg, rv, out_ref, scratch, held, sems
):
    scratch[...] = in_ref[...].astype(f32)
    weights = [jnp.concatenate([gate[...], value[...]], axis=1) for gate, value in ((lg, lv), (rg, rv))]
    copies = []
    for r in range(PAIRED):
        rows = rows_in(r, PAIRED)
        here = slice(rows[0] * SIDE, (rows[-1] + 1) * SIDE)
        grad_normed = base_ref[here, :]
        for n in range(2):
            turned = jnp.transpose(scratch[pl.ds(PAIRED * n + r, WIDTH, stride=2 * PAIRED), :])
            grad = turned[: len(rows) * SIDE]
            pre_grads = jnp.concatenate([grad * factors_ref[2 * n, here], grad * factors_ref[2 * n + 1, here]], axis=1)
            grad_normed += dot(pre_grads.astype(bf16), weights[n], ((1,), (1,)))
        held[here, :] = layer_back(grad_normed, normed_ref[here, :], scale_ref[here, :])
        copies.append(pltpu.make_async_copy(held.at[here], out_ref.at[here], sems.at[r]))
        copies[-1].start()
    for copy in copies:
        copy.wait()


def call(kernel, outs, *args, scratch=(), name=None, space=VMEM, aliases={}, out_space=VMEM):
    return pl.pallas_call(
        kernel,
        out_shape=[jax.ShapeDtypeStruct(shape, dtype) for shape, dtype in outs],
        in_specs=[space for _ in args],
        out_specs=[out_space for _ in outs],
        scratch_shapes=list(scratch),
        input_output_aliases=aliases,
        compiler_params=pltpu.CompilerParams(vmem_limit_bytes=48 * 1024 * 1024),
        name=name,
    )(*args)


def spread(messages):
    paired = messages.reshape(WIDTH, -1, 2, WIDTH)
    return lax.all_to_all(paired, SPREAD, 0, 0, tiled=True).reshape(messages.shape)


def swap(value):
    return lax.ppermute(value, "core", [(0, 1), (1, 0)])


def per_device(
    pair_input,
    norm_mean,
    norm_scale,
    pair_mask,
    cotangent,
    left_gate,
    left_value,
    right_gate,
    right_value,
    output_gate,
    output_weight,
):
    pair = pair_input.reshape(PAIRS, WIDTH)
    cot = cotangent.reshape(PAIRS, WIDTH)
    one, two = (WIDTH * ALONE, WIDTH), (WIDTH * 2 * PAIRED, WIDTH)
    line_one, line_two = pltpu.VMEM(one, f32), pltpu.VMEM(two, f32)
    panel_left = pltpu.VMEM((HALF, TOKENS), f32)
    panels_in = pltpu.VMEM((TILES, SIDE * (GROUPS + 1), WIDTH), f32)
    panels_out = pltpu.VMEM((TILES, GROUPS * (SIDE + 1), WIDTH), f32)
    one, two = (one, bf16), (two, bf16)
    panel, wide = ((HALF, TOKENS), bf16), ((HALF, TOKENS), f32)
    given = [
        pltpu.with_memory_space_constraint(a, pltpu.HBM)
        for a in (pair, norm_mean, norm_scale, pair_mask, left_gate, left_value, right_gate, right_value)
    ]
    held = [pltpu.VMEM(a.shape, a.dtype) for a in given]
    (sent,) = call(
        edges_kernel, [two], *given, scratch=[line_two] + held + [pltpu.SemaphoreType.DMA((len(given),))],
        name="edges", space=HBM,
    )
    came = spread(sent)
    (right_own,) = call(take_right_kernel, [panel], came, scratch=[line_two, panels_in], name="take_right")
    right_other = swap(right_own)
    (left,) = call(take_left_kernel, [panel], came, scratch=[line_two, panel_left], name="take_left")
    line_half, panel_half = pltpu.VMEM((WIDTH * ALONE // 2, WIDTH), f32), pltpu.VMEM((HALF, 2 * WIDTH), f32)
    (mixed_own,) = call(
        mix_own_kernel, [((WIDTH * ALONE // 2, WIDTH), f32)], left, right_own, scratch=[panel_half], name="mix_own",
    )
    grad_mixnorm, factor = call(
        ready_kernel, [((PAIRS, WIDTH), f32)] * 2, pair, norm_mean, norm_scale, cot, output_gate, output_weight,
        name="ready",
    )
    mixed_own, grad_mixnorm, factor = lax.optimization_barrier((mixed_own, grad_mixnorm, factor))
    (sent,) = call(mix_kernel, [one], left, right_other, mixed_own, scratch=[line_half, panel_half], name="mix")
    came = spread(sent)
    sent, grad_gate = call(
        middle_kernel, [one, ((PAIRS, WIDTH), bf16)], came, grad_mixnorm, factor, output_weight, scratch=[line_one],
        name="middle",
    )
    came = spread(sent)
    grad, own, sent = call(
        right_grad_kernel, [panel, wide, panel], came, left,
        scratch=[line_one, panel_left],
        name="right_grad",
    )
    other = swap(sent)
    lined = ((WIDTH * 2 * PAIRED, WIDTH), f32)
    (lines,) = call(
        left_grad_kernel, [lined], grad, right_own, right_other,
        scratch=[pltpu.VMEM((2, HALF, TOKENS), bf16), panel_left], name="left_grad",
    )
    many = ((PAIRS, WIDTH), f32)
    prepared = call(
        prepare_kernel, [many, many, many, ((4, PAIRS, WIDTH), f32)], pair, norm_mean, norm_scale, pair_mask, grad_gate,
        left_gate, left_value, right_gate, right_value, output_gate, name="prepare",
    )
    lines, prepared = lax.optimization_barrier((lines, prepared))
    _, sent = call(return_kernel, [lined, two], lines, own, other, scratch=[panels_out], name="return", aliases={0: 0})
    came = spread(sent)
    (out,) = call(
        last_kernel, [many], came, *prepared, left_gate, left_value, right_gate, right_value,
        scratch=[line_two, pltpu.VMEM((PAIRS, WIDTH), f32), pltpu.SemaphoreType.DMA((PAIRED,))], name="last",
        out_space=HBM,
    )
    return out.reshape(SIDE, SIDE, WIDTH)


def solution(mesh):
    fine = Mesh(mesh.devices.reshape(2, 4, 2, 4, 4), ("z_lo", "x", "core", "z_hi", "y"))
    row, col = ("z_lo", "x", "core"), ("z_hi", "y")
    placed = (P(row, col, None), P(row, col), P(row, col), P(row, col), P(row, col, None)) + (P(),) * 6
    return jax.shard_map(per_device, mesh=fine, in_specs=placed, out_specs=P(row, col, None), check_vma=False)
```

```python
import functools

import jax
import jax.numpy as jnp
from jax import lax
from jax.experimental import pallas as pl
from jax.experimental.pallas import tpu as pltpu
from jax.sharding import Mesh, PartitionSpec as P

epsilon = 1e-05
SIDE = 24
BLOCKS = 16
PAIRS = SIDE * SIDE
WIDTH = 128
GROUPS = 8
HALF = GROUPS * SIDE
TOKENS = SIDE * BLOCKS
SPREAD = ("z_hi", "y", "z_lo", "x")
TILES = TOKENS // WIDTH
ALONE, PAIRED = 6, 5
f32 = jnp.float32
bf16 = jnp.bfloat16
VMEM = pl.BlockSpec(memory_space=pltpu.VMEM)
HBM = pl.BlockSpec(memory_space=pltpu.HBM)


def dot(a, b, over=((1,), (0,))):
    return lax.dot_general(a, b, (over, ((), ())), preferred_element_type=f32)


def spread_pairs(value):
    turned = jnp.transpose(value)
    return jnp.concatenate([jnp.broadcast_to(turned[:, i : i + 1], (SIDE, WIDTH)) for i in range(SIDE)], axis=0)


def lanes(rows):
    return lax.broadcasted_iota(jnp.int32, (rows, WIDTH), 1)


def roll(value, by):
    by = by % WIDTH
    return value if by == 0 else pltpu.roll(value, by, 1)


def place(c):
    return (c % 2) * GROUPS + c // 2


def layer_back(grad, normed, scale):
    centre = jnp.mean(grad, axis=-1, keepdims=True)
    along = jnp.mean(grad * normed, axis=-1, keepdims=True)
    return scale * (grad - centre - normed * along)


def rows_in(line, lines):
    many = -(-SIDE // lines)
    return range(line * many, min((line + 1) * many, SIDE))


def to_messages(parts, scratch):
    total = scratch.shape[0] // WIDTH
    lines = total // len(parts)
    for p, part in enumerate(parts):
        for r in range(lines):
            stack = [part[i * SIDE : (i + 1) * SIDE] for i in rows_in(r, lines)]
            stack.append(jnp.zeros((WIDTH - len(stack) * SIDE, WIDTH), f32))
            turned = jnp.transpose(jnp.concatenate(stack, axis=0))
            scratch[pl.ds(lines * p + r, WIDTH, stride=total), :] = turned
    return scratch[...].astype(bf16)


def from_messages(in_ref, scratch, count):
    total = in_ref.shape[0] // WIDTH
    lines = total // count
    scratch[...] = in_ref[...].astype(f32)
    parts = []
    for p in range(count):
        rows = [None] * SIDE
        for r in range(lines):
            turned = jnp.transpose(scratch[pl.ds(lines * p + r, WIDTH, stride=total), :])
            for n, i in enumerate(rows_in(r, lines)):
                rows[i] = turned[n * SIDE : (n + 1) * SIDE]
        parts.append(jnp.concatenate(rows, axis=0))
    return parts


def assemble(scratch, lines, first, spot, store):
    total = scratch.shape[0] // WIDTH
    lane = lanes(GROUPS)
    order = {spot(c): c for c in range(BLOCKS)}
    for r in range(lines):
        found = [scratch[pl.ds(c * GROUPS * total + first + r, GROUPS, stride=total), :] for c in range(BLOCKS)]
        for n, i in enumerate(rows_in(r, lines)):
            for t in range(TILES):
                tile = None
                for at in range(BLOCKS):
                    begin, end = at * SIDE - t * WIDTH, (at + 1) * SIDE - t * WIDTH
                    if end <= 0 or begin >= WIDTH:
                        continue
                    piece = roll(found[order[at]], begin - n * SIDE)
                    tile = piece if tile is None else jnp.where(lane >= begin, piece, tile)
                store(i, t, tile)


def disassemble(load, scratch, lines, first, blocks):
    total = scratch.shape[0] // (GROUPS * blocks)
    lane = lanes(GROUPS)
    for c in range(blocks):
        begin = c * SIDE
        t, after = begin // WIDTH, (begin + SIDE - 1) // WIDTH
        for r in range(lines):
            line = None
            for n, i in enumerate(rows_in(r, lines)):
                shift = n * SIDE - begin
                piece = roll(load(i, t), shift)
                if after != t:
                    border = n * SIDE + after * WIDTH - begin
                    piece = jnp.where(lane < border, piece, roll(load(i, after), shift))
                line = piece if line is None else jnp.where(lane >= n * SIDE, piece, line)
            scratch[pl.ds(c * GROUPS * total + first + r, GROUPS, stride=total), :] = line


def columns_of(t):
    return slice(t * WIDTH, (t + 1) * WIDTH)


def normalise(pair_ref, mean_ref, scale_ref):
    scale = spread_pairs(scale_ref[...])
    normed = (pair_ref[...].astype(f32) - spread_pairs(mean_ref[...])) * scale
    return normed, scale


def edges_kernel(*refs):
    given, out_ref, scratch, held, sems = refs[:8], refs[8], refs[9], refs[10:18], refs[18]
    copies = [pltpu.make_async_copy(a, b, sems.at[n]) for n, (a, b) in enumerate(zip(given, held))]
    for copy in copies:
        copy.start()
    for copy in copies:
        copy.wait()
    pair_ref, mean_ref, scale_ref, mask_ref, lg, lv, rg, rv = held
    kept_scale = spread_pairs(scale_ref[...] * mask_ref[...].astype(f32))
    low = ((pair_ref[...].astype(f32) - spread_pairs(mean_ref[...])) * kept_scale).astype(bf16)
    parts = []
    for gate, value in ((lg, lv), (rg, rv)):
        both = dot(low, jnp.concatenate([gate[...], value[...]], axis=1))
        parts.append(jax.nn.sigmoid(both[:, :WIDTH]) * both[:, WIDTH:])
    out_ref[...] = to_messages(parts, scratch)


def take_right_kernel(in_ref, *refs):
    given, (out_ref, *made), (scratch, panels) = refs[:6], refs[6:9], refs[9:]
    scratch[...] = in_ref[...].astype(f32)

    def store(i, t, tile):
        panels[t, pl.ds(i * (GROUPS + 1), GROUPS), :] = tile

    assemble(scratch, PAIRED, PAIRED, lambda c: c, store)
    for group in range(GROUPS):
        rows = [panels[t, pl.ds(group, SIDE, stride=GROUPS + 1), :] for t in range(TILES)]
        out_ref[group * SIDE : (group + 1) * SIDE, :] = jnp.concatenate(rows, axis=1).astype(bf16)
    on_core(1, ready, given, made)


def assemble_left(in_ref, scratch, panel, lines, spot):
    scratch[...] = in_ref[...].astype(f32)

    def store(i, t, tile):
        panel[i * GROUPS : (i + 1) * GROUPS, columns_of(t)] = tile

    assemble(scratch, lines, 0, spot, store)


def rows_of(panel):
    return lambda i, t: panel[i * GROUPS : (i + 1) * GROUPS, columns_of(t)]


def take_left_kernel(in_ref, out_ref, scratch, panel):
    assemble_left(in_ref, scratch, panel, PAIRED, lambda c: c)
    out_ref[...] = panel[...].astype(bf16)


def half_mixed(left_ref, right_ref, scratch, panel):
    panel[:, :HALF] = dot(left_ref[...], right_ref[...], ((1,), (1,)))
    disassemble(rows_of(panel), scratch, ALONE, 0, BLOCKS // 2)


def mix_own_kernel(left_ref, right_ref, out_ref, panel):
    half_mixed(left_ref, right_ref, out_ref, panel)


def mix_kernel(left_ref, right_ref, own_ref, out_ref, scratch, panel):
    half_mixed(left_ref, right_ref, scratch, panel)
    first = lax.axis_index("core") == 0
    size = GROUPS * ALONE
    for n in range(BLOCKS // 2):
        here = slice(n * size, (n + 1) * size)
        own, other = own_ref[here, :], scratch[here, :]
        out_ref[2 * n * size : (2 * n + 1) * size, :] = jnp.where(first, own, other).astype(bf16)
        out_ref[(2 * n + 1) * size : (2 * n + 2) * size, :] = jnp.where(first, other, own).astype(bf16)


def ready(given, grad_ref, factor_ref):
    pair_ref, mean_ref, scale_ref, cot_ref, gate_ref, weight_ref = given
    normed, _ = normalise(pair_ref, mean_ref, scale_ref)
    out_sig = jax.nn.sigmoid(dot(normed.astype(bf16), gate_ref[...]))
    grad_y = cot_ref[...].astype(f32) * out_sig
    grad_ref[...] = dot(grad_y.astype(bf16), weight_ref[...], ((1,), (1,)))
    factor_ref[...] = grad_y * (1.0 - out_sig)


def on_core(core, work, given, made):
    @pl.when(lax.axis_index("core") == core)
    def _():
        work(given, *made)


def later_kernel(work, count, *refs):
    on_core(0, work, refs[count:-count], refs[-count:])


def middle_kernel(in_ref, grad_ref, factor_ref, weight_ref, out_ref, grad_gate_ref, scratch):
    (mixed,) = from_messages(in_ref, scratch, 1)
    centred = mixed - jnp.mean(mixed, axis=-1, keepdims=True)
    mix_scale = lax.rsqrt(jnp.mean(centred * centred, axis=-1, keepdims=True) + epsilon)
    mix_normed = centred * mix_scale
    out_lin = dot(mix_normed.astype(bf16), weight_ref[...])
    grad_gate_ref[...] = (factor_ref[...] * out_lin).astype(bf16)
    grad_mix = layer_back(grad_ref[...], mix_normed, mix_scale)
    out_ref[...] = to_messages([grad_mix], scratch)


def right_grad_kernel(in_ref, left_ref, *refs):
    given, (grad_ref, own_ref, sent_ref), made, (scratch, panel) = refs[:10], refs[10:13], refs[13:17], refs[17:]
    assemble_left(in_ref, scratch, panel, ALONE, place)
    grad = panel[...]
    grad_ref[...] = grad.astype(bf16)
    first = lax.axis_index("core") == 0
    sums = dot(jnp.transpose(grad).astype(bf16), left_ref[...])
    own_ref[...] = jnp.where(first, sums[:HALF], sums[HALF:])
    sent_ref[...] = jnp.where(first, sums[HALF:], sums[:HALF]).astype(bf16)
    on_core(1, prepare, given, made)


def left_grad_kernel(grad_ref, own_ref, other_ref, out_ref, right, panel):
    core = lax.axis_index("core")
    right[core] = own_ref[...]
    right[1 - core] = other_ref[...]
    panel[...] = dot(grad_ref[...], right[...].reshape(TOKENS, TOKENS))
    disassemble(rows_of(panel), out_ref, PAIRED, 0, BLOCKS)


def return_kernel(lines_ref, own_ref, other_ref, kept_ref, out_ref, panels):
    for group in range(GROUPS):
        here = slice(group * SIDE, (group + 1) * SIDE)
        total = own_ref[here, :] + other_ref[here, :].astype(f32)
        for t in range(TILES):
            panels[t, pl.ds(group * (SIDE + 1), SIDE), :] = total[:, columns_of(t)]
    load = lambda i, t: panels[t, pl.ds(i, GROUPS, stride=SIDE + 1), :]
    disassemble(load, kept_ref, PAIRED, PAIRED, BLOCKS)
    out_ref[...] = kept_ref[...].astype(bf16)


def prepare(given, normed_ref, scaled_ref, base_ref, factors_ref):
    pair_ref, mean_ref, scale_ref, mask_ref, grad_gate_ref, lg, lv, rg, rv, og = given
    normed, scale = normalise(pair_ref, mean_ref, scale_ref)
    normed_ref[...] = normed
    scaled_ref[...] = scale
    base_ref[...] = dot(grad_gate_ref[...], og[...], ((1,), (1,)))
    low = normed.astype(bf16)
    keep = spread_pairs(mask_ref[...].astype(f32))
    for n, (gate, value) in enumerate(((lg, lv), (rg, rv))):
        both = dot(low, jnp.concatenate([gate[...], value[...]], axis=1))
        sig, lin = jax.nn.sigmoid(both[:, :WIDTH]), both[:, WIDTH:]
        factors_ref[2 * n + 1] = keep * sig
        factors_ref[2 * n] = keep * lin * sig * (1.0 - sig)


def last_kernel(
    in_ref, normed_ref, scale_ref, base_ref, factors_ref, lg, lv, rg, rv, out_ref, scratch, held, sems
):
    scratch[...] = in_ref[...].astype(f32)
    weights = [jnp.concatenate([gate[...], value[...]], axis=1) for gate, value in ((lg, lv), (rg, rv))]
    copies = []
    for r in range(PAIRED):
        rows = rows_in(r, PAIRED)
        here = slice(rows[0] * SIDE, (rows[-1] + 1) * SIDE)
        grad_normed = base_ref[here, :]
        for n in range(2):
            turned = jnp.transpose(scratch[pl.ds(PAIRED * n + r, WIDTH, stride=2 * PAIRED), :])
            grad = turned[: len(rows) * SIDE]
            pre_grads = jnp.concatenate([grad * factors_ref[2 * n, here], grad * factors_ref[2 * n + 1, here]], axis=1)
            grad_normed += dot(pre_grads.astype(bf16), weights[n], ((1,), (1,)))
        held[here, :] = layer_back(grad_normed, normed_ref[here, :], scale_ref[here, :])
        copies.append(pltpu.make_async_copy(held.at[here], out_ref.at[here], sems.at[r]))
        copies[-1].start()
    for copy in copies:
        copy.wait()


def call(kernel, outs, *args, scratch=(), name=None, space=VMEM, aliases={}, out_space=VMEM):
    return pl.pallas_call(
        kernel,
        out_shape=[jax.ShapeDtypeStruct(shape, dtype) for shape, dtype in outs],
        in_specs=[space for _ in args],
        out_specs=[out_space for _ in outs],
        scratch_shapes=list(scratch),
        input_output_aliases=aliases,
        compiler_params=pltpu.CompilerParams(vmem_limit_bytes=48 * 1024 * 1024),
        name=name,
    )(*args)


def spread(messages):
    paired = messages.reshape(WIDTH, -1, 2, WIDTH)
    return lax.all_to_all(paired, SPREAD, 0, 0, tiled=True).reshape(messages.shape)


def swap(value):
    return lax.ppermute(value, "core", [(0, 1), (1, 0)])


def per_device(
    pair_input,
    norm_mean,
    norm_scale,
    pair_mask,
    cotangent,
    left_gate,
    left_value,
    right_gate,
    right_value,
    output_gate,
    output_weight,
):
    pair = pair_input.reshape(PAIRS, WIDTH)
    cot = cotangent.reshape(PAIRS, WIDTH)
    one, two = (WIDTH * ALONE, WIDTH), (WIDTH * 2 * PAIRED, WIDTH)
    line_one, line_two = pltpu.VMEM(one, f32), pltpu.VMEM(two, f32)
    panel_left = pltpu.VMEM((HALF, TOKENS), f32)
    panels_in = pltpu.VMEM((TILES, SIDE * (GROUPS + 1), WIDTH), f32)
    panels_out = pltpu.VMEM((TILES, GROUPS * (SIDE + 1), WIDTH), f32)
    one, two = (one, bf16), (two, bf16)
    panel, wide = ((HALF, TOKENS), bf16), ((HALF, TOKENS), f32)
    given = [
        pltpu.with_memory_space_constraint(a, pltpu.HBM)
        for a in (pair, norm_mean, norm_scale, pair_mask, left_gate, left_value, right_gate, right_value)
    ]
    held = [pltpu.VMEM(a.shape, a.dtype) for a in given]
    (sent,) = call(
        edges_kernel, [two], *given, scratch=[line_two] + held + [pltpu.SemaphoreType.DMA((len(given),))],
        name="edges", space=HBM,
    )
    came = spread(sent)
    many = ((PAIRS, WIDTH), f32)
    given = [pair, norm_mean, norm_scale, cot, output_gate, output_weight]
    right_own, *made = call(
        take_right_kernel, [panel, many, many], came, *given, scratch=[line_two, panels_in], name="take_right"
    )
    right_other = swap(right_own)
    (left,) = call(take_left_kernel, [panel], came, scratch=[line_two, panel_left], name="take_left")
    line_half, panel_half = pltpu.VMEM((WIDTH * ALONE // 2, WIDTH), f32), pltpu.VMEM((HALF, 2 * WIDTH), f32)
    (mixed_own,) = call(
        mix_own_kernel, [((WIDTH * ALONE // 2, WIDTH), f32)], left, right_own, scratch=[panel_half], name="mix_own",
    )
    grad_mixnorm, factor = call(
        functools.partial(later_kernel, ready, 2), [many, many], *made, *given, name="ready", aliases={0: 0, 1: 1}
    )
    mixed_own, grad_mixnorm, factor = lax.optimization_barrier((mixed_own, grad_mixnorm, factor))
    (sent,) = call(mix_kernel, [one], left, right_other, mixed_own, scratch=[line_half, panel_half], name="mix")
    came = spread(sent)
    sent, grad_gate = call(
        middle_kernel, [one, ((PAIRS, WIDTH), bf16)], came, grad_mixnorm, factor, output_weight, scratch=[line_one],
        name="middle",
    )
    came = spread(sent)
    given = [
        pair, norm_mean, norm_scale, pair_mask, grad_gate, left_gate, left_value, right_gate, right_value, output_gate
    ]
    factors = ((4, PAIRS, WIDTH), f32)
    grad, own, sent, *made = call(
        right_grad_kernel, [panel, wide, panel, many, many, many, factors], came, left, *given,
        scratch=[line_one, panel_left], name="right_grad",
    )
    other = swap(sent)
    lined = ((WIDTH * 2 * PAIRED, WIDTH), f32)
    (lines,) = call(
        left_grad_kernel, [lined], grad, right_own, right_other,
        scratch=[pltpu.VMEM((2, HALF, TOKENS), bf16), panel_left], name="left_grad",
    )
    prepared = call(
        functools.partial(later_kernel, prepare, 4), [many, many, many, factors], *made, *given, name="prepare",
        aliases={n: n for n in range(4)},
    )
    lines, prepared = lax.optimization_barrier((lines, prepared))
    _, sent = call(return_kernel, [lined, two], lines, own, other, scratch=[panels_out], name="return", aliases={0: 0})
    came = spread(sent)
    (out,) = call(
        last_kernel, [many], came, *prepared, left_gate, left_value, right_gate, right_value,
        scratch=[line_two, pltpu.VMEM((PAIRS, WIDTH), f32), pltpu.SemaphoreType.DMA((PAIRED,))], name="last",
        out_space=HBM,
    )
    return out.reshape(SIDE, SIDE, WIDTH)


def solution(mesh):
    fine = Mesh(mesh.devices.reshape(2, 4, 2, 4, 4), ("z_lo", "x", "core", "z_hi", "y"))
    row, col = ("z_lo", "x", "core"), ("z_hi", "y")
    placed = (P(row, col, None), P(row, col), P(row, col), P(row, col), P(row, col, None)) + (P(),) * 6
    return jax.shard_map(per_device, mesh=fine, in_specs=placed, out_specs=P(row, col, None), check_vma=False)
```

```python
import jax
import jax.numpy as jnp
from jax import lax
from jax.experimental import pallas as pl
from jax.experimental.pallas import tpu as pltpu
from jax.sharding import Mesh, PartitionSpec as P

epsilon = 1e-05
SIDE = 24
BLOCKS = 16
PAIRS = SIDE * SIDE
WIDTH = 128
GROUPS = 8
HALF = GROUPS * SIDE
TOKENS = SIDE * BLOCKS
SPREAD = ("z_hi", "y", "z_lo", "x")
TILES = TOKENS // WIDTH
ALONE, PAIRED = 6, 5
f32 = jnp.float32
bf16 = jnp.bfloat16
VMEM = pl.BlockSpec(memory_space=pltpu.VMEM)
HBM = pl.BlockSpec(memory_space=pltpu.HBM)


def dot(a, b, over=((1,), (0,))):
    return lax.dot_general(a, b, (over, ((), ())), preferred_element_type=f32)


def spread_pairs(value):
    turned = jnp.transpose(value)
    return jnp.concatenate([jnp.broadcast_to(turned[:, i : i + 1], (SIDE, WIDTH)) for i in range(SIDE)], axis=0)


def lanes(rows):
    return lax.broadcasted_iota(jnp.int32, (rows, WIDTH), 1)


def roll(value, by):
    by = by % WIDTH
    return value if by == 0 else pltpu.roll(value, by, 1)


def place(c):
    return (c % 2) * GROUPS + c // 2


def layer_back(grad, normed, scale):
    centre = jnp.mean(grad, axis=-1, keepdims=True)
    along = jnp.mean(grad * normed, axis=-1, keepdims=True)
    return scale * (grad - centre - normed * along)


def rows_in(line, lines):
    many = -(-SIDE // lines)
    return range(line * many, min((line + 1) * many, SIDE))


def to_messages(parts, scratch):
    total = scratch.shape[0] // WIDTH
    lines = total // len(parts)
    for p, part in enumerate(parts):
        for r in range(lines):
            stack = [part[i * SIDE : (i + 1) * SIDE] for i in rows_in(r, lines)]
            stack.append(jnp.zeros((WIDTH - len(stack) * SIDE, WIDTH), f32))
            turned = jnp.transpose(jnp.concatenate(stack, axis=0))
            scratch[pl.ds(lines * p + r, WIDTH, stride=total), :] = turned
    return scratch[...].astype(bf16)


def from_messages(in_ref, scratch, count):
    total = in_ref.shape[0] // WIDTH
    lines = total // count
    scratch[...] = in_ref[...].astype(f32)
    parts = []
    for p in range(count):
        rows = [None] * SIDE
        for r in range(lines):
            turned = jnp.transpose(scratch[pl.ds(lines * p + r, WIDTH, stride=total), :])
            for n, i in enumerate(rows_in(r, lines)):
                rows[i] = turned[n * SIDE : (n + 1) * SIDE]
        parts.append(jnp.concatenate(rows, axis=0))
    return parts


def assemble(scratch, lines, first, spot, store, spots=range(BLOCKS)):
    total = scratch.shape[0] // WIDTH
    lane = lanes(GROUPS)
    order = {spot(c): c for c in range(BLOCKS)}
    for r in range(lines):
        found = {
            at: scratch[pl.ds(order[at] * GROUPS * total + first + r, GROUPS, stride=total), :] for at in spots
        }
        for n, i in enumerate(rows_in(r, lines)):
            for t in range(TILES):
                tile = None
                for at in spots:
                    begin, end = at * SIDE - t * WIDTH, (at + 1) * SIDE - t * WIDTH
                    if end <= 0 or begin >= WIDTH:
                        continue
                    piece = roll(found[at], begin - n * SIDE)
                    tile = piece if tile is None else jnp.where(lane >= begin, piece, tile)
                if tile is not None:
                    store(i, t, tile)


def disassemble(load, scratch, lines, first, blocks):
    total = scratch.shape[0] // (GROUPS * blocks)
    lane = lanes(GROUPS)
    for c in range(blocks):
        begin = c * SIDE
        t, after = begin // WIDTH, (begin + SIDE - 1) // WIDTH
        for r in range(lines):
            line = None
            for n, i in enumerate(rows_in(r, lines)):
                shift = n * SIDE - begin
                piece = roll(load(i, t), shift)
                if after != t:
                    border = n * SIDE + after * WIDTH - begin
                    piece = jnp.where(lane < border, piece, roll(load(i, after), shift))
                line = piece if line is None else jnp.where(lane >= n * SIDE, piece, line)
            scratch[pl.ds(c * GROUPS * total + first + r, GROUPS, stride=total), :] = line


def columns_of(t):
    return slice(t * WIDTH, (t + 1) * WIDTH)


def normalise(pair_ref, mean_ref, scale_ref):
    scale = spread_pairs(scale_ref[...])
    normed = (pair_ref[...].astype(f32) - spread_pairs(mean_ref[...])) * scale
    return normed, scale


def edges_kernel(*refs):
    given, out_ref, scratch, held, sems = refs[:8], refs[8], refs[9], refs[10:18], refs[18]
    copies = [pltpu.make_async_copy(a, b, sems.at[n]) for n, (a, b) in enumerate(zip(given, held))]
    for copy in copies:
        copy.start()
    for copy in copies:
        copy.wait()
    pair_ref, mean_ref, scale_ref, mask_ref, lg, lv, rg, rv = held
    kept_scale = spread_pairs(scale_ref[...] * mask_ref[...].astype(f32))
    low = ((pair_ref[...].astype(f32) - spread_pairs(mean_ref[...])) * kept_scale).astype(bf16)
    parts = []
    for gate, value in ((lg, lv), (rg, rv)):
        both = dot(low, jnp.concatenate([gate[...], value[...]], axis=1))
        parts.append(jax.nn.sigmoid(both[:, :WIDTH]) * both[:, WIDTH:])
    out_ref[...] = to_messages(parts, scratch)


def take_right_kernel(in_ref, *refs):
    given, (out_ref, *made), (scratch, panels) = refs[:6], refs[6:9], refs[9:]
    scratch[...] = in_ref[...].astype(f32)

    def store(i, t, tile):
        panels[t, pl.ds(i * (GROUPS + 1), GROUPS), :] = tile

    assemble(scratch, PAIRED, PAIRED, lambda c: c, store)
    for group in range(GROUPS):
        rows = [panels[t, pl.ds(group, SIDE, stride=GROUPS + 1), :] for t in range(TILES)]
        out_ref[group * SIDE : (group + 1) * SIDE, :] = jnp.concatenate(rows, axis=1).astype(bf16)
    on_core(1, ready, given, made)


def assemble_left(in_ref, scratch, panel, lines, spot, spots=range(BLOCKS)):
    scratch[...] = in_ref[...].astype(f32)

    def store(i, t, tile):
        panel[i * GROUPS : (i + 1) * GROUPS, columns_of(t)] = tile

    assemble(scratch, lines, 0, spot, store, spots)


def rows_of(panel):
    return lambda i, t: panel[i * GROUPS : (i + 1) * GROUPS, columns_of(t)]


def take_left_kernel(in_ref, out_ref, scratch, panel):
    assemble_left(in_ref, scratch, panel, PAIRED, lambda c: c)
    out_ref[...] = panel[...].astype(bf16)


def half_mixed(left_ref, right_ref, scratch, panel):
    panel[:, :HALF] = dot(left_ref[...], right_ref[...], ((1,), (1,)))
    disassemble(rows_of(panel), scratch, ALONE, 0, BLOCKS // 2)


def put_half(scratch, out_ref, own):
    size = GROUPS * ALONE
    for core in range(2):

        @pl.when(lax.axis_index("core") == (core if own else 1 - core))
        def _(core=core):
            for n in range(BLOCKS // 2):
                there = (2 * n + core) * size
                out_ref[there : there + size, :] = scratch[n * size : (n + 1) * size, :].astype(bf16)


def mix_own_kernel(left_ref, right_ref, out_ref, scratch, panel):
    half_mixed(left_ref, right_ref, scratch, panel)
    put_half(scratch, out_ref, True)


def mix_kernel(_, left_ref, right_ref, out_ref, scratch, panel):
    half_mixed(left_ref, right_ref, scratch, panel)
    put_half(scratch, out_ref, False)


def ready(given, grad_ref, factor_ref):
    pair_ref, mean_ref, scale_ref, cot_ref, gate_ref, weight_ref = given
    normed, _ = normalise(pair_ref, mean_ref, scale_ref)
    out_sig = jax.nn.sigmoid(dot(normed.astype(bf16), gate_ref[...]))
    grad_y = cot_ref[...].astype(f32) * out_sig
    grad_ref[...] = dot(grad_y.astype(bf16), weight_ref[...], ((1,), (1,)))
    factor_ref[...] = grad_y * (1.0 - out_sig)


def on_core(core, work, given, made):
    @pl.when(lax.axis_index("core") == core)
    def _():
        work(given, *made)


def ready_later_kernel(*refs):
    on_core(0, ready, refs[2:-2], refs[-2:])


def middle_kernel(in_ref, grad_ref, out_ref, normed_ref, scratch):
    (mixed,) = from_messages(in_ref, scratch, 1)
    centred = mixed - jnp.mean(mixed, axis=-1, keepdims=True)
    mix_scale = lax.rsqrt(jnp.mean(centred * centred, axis=-1, keepdims=True) + epsilon)
    mix_normed = centred * mix_scale
    normed_ref[...] = mix_normed.astype(bf16)
    grad_mix = layer_back(grad_ref[...], mix_normed, mix_scale)
    out_ref[...] = to_messages([grad_mix], scratch)


def right_grad_all(in_ref, left_ref, grad_ref, own_ref, scratch, panel):
    assemble_left(in_ref, scratch, panel, ALONE, place)
    grad = panel[...]
    grad_ref[...] = grad.astype(bf16)
    first = lax.axis_index("core") == 0
    sums = dot(jnp.transpose(grad).astype(bf16), left_ref[...])
    own_ref[...] = jnp.where(first, sums[:HALF], sums[HALF:])
    return jnp.where(first, sums[HALF:], sums[:HALF])


def right_grad_kernel(in_ref, left_ref, *refs):
    given, (grad_ref, own_ref, sent_ref), made, (scratch, panel) = refs[:12], refs[12:15], refs[15:19], refs[19:]
    core = lax.axis_index("core")

    @pl.when(core == 0)
    def _():
        assemble_left(in_ref, scratch, panel, ALONE, place, range(BLOCKS // 2, BLOCKS))
        turned = jnp.transpose(panel[:, WIDTH:])[HALF - WIDTH :]
        sent_ref[...] = dot(turned.astype(bf16), left_ref[...]).astype(bf16)

    @pl.when(core == 1)
    def _():
        sent_ref[...] = right_grad_all(in_ref, left_ref, grad_ref, own_ref, scratch, panel).astype(bf16)
        prepare(given, *made)


def right_grad_later_kernel(*refs):
    in_ref, left_ref, *given = refs[6:20]
    (grad_ref, own_ref), made, (scratch, panel) = refs[20:22], refs[22:26], refs[26:]

    @pl.when(lax.axis_index("core") == 0)
    def _():
        right_grad_all(in_ref, left_ref, grad_ref, own_ref, scratch, panel)
        prepare(given, *made)


def left_grad_kernel(grad_ref, own_ref, other_ref, out_ref, right, panel):
    core = lax.axis_index("core")
    right[core] = own_ref[...]
    right[1 - core] = other_ref[...]
    panel[...] = dot(grad_ref[...], right[...].reshape(TOKENS, TOKENS))
    disassemble(rows_of(panel), out_ref, PAIRED, 0, BLOCKS)


def return_kernel(lines_ref, own_ref, other_ref, kept_ref, out_ref, panels):
    for group in range(GROUPS):
        here = slice(group * SIDE, (group + 1) * SIDE)
        total = own_ref[here, :] + other_ref[here, :].astype(f32)
        for t in range(TILES):
            panels[t, pl.ds(group * (SIDE + 1), SIDE), :] = total[:, columns_of(t)]
    load = lambda i, t: panels[t, pl.ds(i, GROUPS, stride=SIDE + 1), :]
    disassemble(load, kept_ref, PAIRED, PAIRED, BLOCKS)
    out_ref[...] = kept_ref[...].astype(bf16)


def prepare(given, normed_ref, scaled_ref, base_ref, factors_ref):
    pair_ref, mean_ref, scale_ref, mask_ref, mix_normed_ref, factor_ref, weight_ref, lg, lv, rg, rv, og = given
    normed, scale = normalise(pair_ref, mean_ref, scale_ref)
    normed_ref[...] = normed
    scaled_ref[...] = scale
    grad_gate = factor_ref[...] * dot(mix_normed_ref[...], weight_ref[...])
    base_ref[...] = dot(grad_gate.astype(bf16), og[...], ((1,), (1,)))
    low = normed.astype(bf16)
    keep = spread_pairs(mask_ref[...].astype(f32))
    for n, (gate, value) in enumerate(((lg, lv), (rg, rv))):
        both = dot(low, jnp.concatenate([gate[...], value[...]], axis=1))
        sig, lin = jax.nn.sigmoid(both[:, :WIDTH]), both[:, WIDTH:]
        factors_ref[2 * n + 1] = keep * sig
        factors_ref[2 * n] = keep * lin * sig * (1.0 - sig)


def last_kernel(
    in_ref, normed_ref, scale_ref, base_ref, factors_ref, lg, lv, rg, rv, out_ref, scratch, held, sems
):
    scratch[...] = in_ref[...].astype(f32)
    weights = [jnp.concatenate([gate[...], value[...]], axis=1) for gate, value in ((lg, lv), (rg, rv))]
    copies = []
    for r in range(PAIRED):
        rows = rows_in(r, PAIRED)
        here = slice(rows[0] * SIDE, (rows[-1] + 1) * SIDE)
        grad_normed = base_ref[here, :]
        for n in range(2):
            turned = jnp.transpose(scratch[pl.ds(PAIRED * n + r, WIDTH, stride=2 * PAIRED), :])
            grad = turned[: len(rows) * SIDE]
            pre_grads = jnp.concatenate([grad * factors_ref[2 * n, here], grad * factors_ref[2 * n + 1, here]], axis=1)
            grad_normed += dot(pre_grads.astype(bf16), weights[n], ((1,), (1,)))
        held[here, :] = layer_back(grad_normed, normed_ref[here, :], scale_ref[here, :])
        copies.append(pltpu.make_async_copy(held.at[here], out_ref.at[here], sems.at[r]))
        copies[-1].start()
    for copy in copies:
        copy.wait()


def call(kernel, outs, *args, scratch=(), name=None, space=VMEM, aliases={}, out_space=VMEM):
    return pl.pallas_call(
        kernel,
        out_shape=[jax.ShapeDtypeStruct(shape, dtype) for shape, dtype in outs],
        in_specs=[space for _ in args],
        out_specs=[out_space for _ in outs],
        scratch_shapes=list(scratch),
        input_output_aliases=aliases,
        compiler_params=pltpu.CompilerParams(vmem_limit_bytes=48 * 1024 * 1024),
        name=name,
    )(*args)


def spread(messages):
    paired = messages.reshape(WIDTH, -1, 2, WIDTH)
    return lax.all_to_all(paired, SPREAD, 0, 0, tiled=True).reshape(messages.shape)


def swap(value):
    return lax.ppermute(value, "core", [(0, 1), (1, 0)])


def per_device(
    pair_input,
    norm_mean,
    norm_scale,
    pair_mask,
    cotangent,
    left_gate,
    left_value,
    right_gate,
    right_value,
    output_gate,
    output_weight,
):
    pair = pair_input.reshape(PAIRS, WIDTH)
    cot = cotangent.reshape(PAIRS, WIDTH)
    one, two = (WIDTH * ALONE, WIDTH), (WIDTH * 2 * PAIRED, WIDTH)
    line_one, line_two = pltpu.VMEM(one, f32), pltpu.VMEM(two, f32)
    panel_left = pltpu.VMEM((HALF, TOKENS), f32)
    panels_in = pltpu.VMEM((TILES, SIDE * (GROUPS + 1), WIDTH), f32)
    panels_out = pltpu.VMEM((TILES, GROUPS * (SIDE + 1), WIDTH), f32)
    one, two = (one, bf16), (two, bf16)
    panel, wide = ((HALF, TOKENS), bf16), ((HALF, TOKENS), f32)
    given = [
        pltpu.with_memory_space_constraint(a, pltpu.HBM)
        for a in (pair, norm_mean, norm_scale, pair_mask, left_gate, left_value, right_gate, right_value)
    ]
    held = [pltpu.VMEM(a.shape, a.dtype) for a in given]
    (sent,) = call(
        edges_kernel, [two], *given, scratch=[line_two] + held + [pltpu.SemaphoreType.DMA((len(given),))],
        name="edges", space=HBM,
    )
    came = spread(sent)
    many = ((PAIRS, WIDTH), f32)
    given = [pair, norm_mean, norm_scale, cot, output_gate, output_weight]
    right_own, *made = call(
        take_right_kernel, [panel, many, many], came, *given, scratch=[line_two, panels_in], name="take_right"
    )
    right_other = swap(right_own)
    (left,) = call(take_left_kernel, [panel], came, scratch=[line_two, panel_left], name="take_left")
    line_half, panel_half = pltpu.VMEM((WIDTH * ALONE // 2, WIDTH), f32), pltpu.VMEM((HALF, 2 * WIDTH), f32)
    (mixed_own,) = call(
        mix_own_kernel, [one], left, right_own, scratch=[line_half, panel_half], name="mix_own",
    )
    grad_mixnorm, factor = call(
        ready_later_kernel, [many, many], *made, *given, name="ready", aliases={0: 0, 1: 1}
    )
    mixed_own, grad_mixnorm, factor = lax.optimization_barrier((mixed_own, grad_mixnorm, factor))
    (sent,) = call(
        mix_kernel, [one], mixed_own, left, right_other, scratch=[line_half, panel_half], name="mix", aliases={0: 0}
    )
    came = spread(sent)
    sent, mix_normed = call(
        middle_kernel, [one, ((PAIRS, WIDTH), bf16)], came, grad_mixnorm, scratch=[line_one], name="middle"
    )
    came = spread(sent)
    given = [
        pair, norm_mean, norm_scale, pair_mask, mix_normed, factor, output_weight, left_gate, left_value, right_gate,
        right_value, output_gate,
    ]
    factors = ((4, PAIRS, WIDTH), f32)
    grad, own, sent, *made = call(
        right_grad_kernel, [panel, wide, panel, many, many, many, factors], came, left, *given,
        scratch=[line_one, panel_left], name="right_grad",
    )
    other = swap(sent)
    lined = ((WIDTH * 2 * PAIRED, WIDTH), f32)
    grad, own, *prepared = call(
        right_grad_later_kernel, [panel, wide, many, many, many, factors], grad, own, *made, came, left, *given,
        scratch=[line_one, panel_left], name="right_grad_later", aliases={n: n for n in range(6)},
    )
    (lines,) = call(
        left_grad_kernel, [lined], grad, right_own, right_other,
        scratch=[pltpu.VMEM((2, HALF, TOKENS), bf16), panel_left], name="left_grad",
    )
    lines, prepared = lax.optimization_barrier((lines, prepared))
    _, sent = call(return_kernel, [lined, two], lines, own, other, scratch=[panels_out], name="return", aliases={0: 0})
    came = spread(sent)
    (out,) = call(
        last_kernel, [many], came, *prepared, left_gate, left_value, right_gate, right_value,
        scratch=[line_two, pltpu.VMEM((PAIRS, WIDTH), f32), pltpu.SemaphoreType.DMA((PAIRED,))], name="last",
        out_space=HBM,
    )
    return out.reshape(SIDE, SIDE, WIDTH)


def solution(mesh):
    fine = Mesh(mesh.devices.reshape(2, 4, 2, 4, 4), ("z_lo", "x", "core", "z_hi", "y"))
    row, col = ("z_lo", "x", "core"), ("z_hi", "y")
    placed = (P(row, col, None), P(row, col), P(row, col), P(row, col), P(row, col, None)) + (P(),) * 6
    return jax.shard_map(per_device, mesh=fine, in_specs=placed, out_specs=P(row, col, None), check_vma=False)
```

```python
import jax
import jax.numpy as jnp
from jax import lax
from jax.experimental import pallas as pl
from jax.experimental.pallas import tpu as pltpu
from jax.sharding import Mesh, PartitionSpec as P

epsilon = 1e-05
SIDE = 24
BLOCKS = 16
PAIRS = SIDE * SIDE
WIDTH = 128
GROUPS = 8
HALF = GROUPS * SIDE
TOKENS = SIDE * BLOCKS
SPREAD = ("z_hi", "y", "z_lo", "x")
TILES = TOKENS // WIDTH
ALONE, PAIRED = 6, 5
f32 = jnp.float32
bf16 = jnp.bfloat16
VMEM = pl.BlockSpec(memory_space=pltpu.VMEM)
HBM = pl.BlockSpec(memory_space=pltpu.HBM)


def dot(a, b, over=((1,), (0,))):
    return lax.dot_general(a, b, (over, ((), ())), preferred_element_type=f32)


def spread_pairs(value):
    turned = jnp.transpose(value)
    return jnp.concatenate([jnp.broadcast_to(turned[:, i : i + 1], (SIDE, WIDTH)) for i in range(SIDE)], axis=0)


def lanes(rows):
    return lax.broadcasted_iota(jnp.int32, (rows, WIDTH), 1)


def roll(value, by):
    by = by % WIDTH
    return value if by == 0 else pltpu.roll(value, by, 1)


def place(c):
    return (c % 2) * GROUPS + c // 2


def layer_back(grad, normed, scale):
    centre = jnp.mean(grad, axis=-1, keepdims=True)
    along = jnp.mean(grad * normed, axis=-1, keepdims=True)
    return scale * (grad - centre - normed * along)


def rows_in(line, lines):
    many = -(-SIDE // lines)
    return range(line * many, min((line + 1) * many, SIDE))


def to_messages(parts, scratch):
    total = scratch.shape[0] // WIDTH
    lines = total // len(parts)
    for p, part in enumerate(parts):
        for r in range(lines):
            stack = [part[i * SIDE : (i + 1) * SIDE] for i in rows_in(r, lines)]
            stack.append(jnp.zeros((WIDTH - len(stack) * SIDE, WIDTH), f32))
            turned = jnp.transpose(jnp.concatenate(stack, axis=0))
            scratch[pl.ds(lines * p + r, WIDTH, stride=total), :] = turned
    return scratch[...].astype(bf16)


def from_messages(in_ref, scratch, count):
    total = in_ref.shape[0] // WIDTH
    lines = total // count
    scratch[...] = in_ref[...].astype(f32)
    parts = []
    for p in range(count):
        rows = [None] * SIDE
        for r in range(lines):
            turned = jnp.transpose(scratch[pl.ds(lines * p + r, WIDTH, stride=total), :])
            for n, i in enumerate(rows_in(r, lines)):
                rows[i] = turned[n * SIDE : (n + 1) * SIDE]
        parts.append(jnp.concatenate(rows, axis=0))
    return parts


def assemble(scratch, lines, first, spot, store, spots=range(BLOCKS)):
    total = scratch.shape[0] // WIDTH
    lane = lanes(GROUPS)
    order = {spot(c): c for c in range(BLOCKS)}
    for r in range(lines):
        found = {
            at: scratch[pl.ds(order[at] * GROUPS * total + first + r, GROUPS, stride=total), :] for at in spots
        }
        for n, i in enumerate(rows_in(r, lines)):
            for t in range(TILES):
                tile = None
                for at in spots:
                    begin, end = at * SIDE - t * WIDTH, (at + 1) * SIDE - t * WIDTH
                    if end <= 0 or begin >= WIDTH:
                        continue
                    piece = roll(found[at], begin - n * SIDE)
                    tile = piece if tile is None else jnp.where(lane >= begin, piece, tile)
                if tile is not None:
                    store(i, t, tile)


def disassemble(load, scratch, lines, first, blocks):
    total = scratch.shape[0] // (GROUPS * blocks)
    lane = lanes(GROUPS)
    for c in range(blocks):
        begin = c * SIDE
        t, after = begin // WIDTH, (begin + SIDE - 1) // WIDTH
        for r in range(lines):
            line = None
            for n, i in enumerate(rows_in(r, lines)):
                shift = n * SIDE - begin
                piece = roll(load(i, t), shift)
                if after != t:
                    border = n * SIDE + after * WIDTH - begin
                    piece = jnp.where(lane < border, piece, roll(load(i, after), shift))
                line = piece if line is None else jnp.where(lane >= n * SIDE, piece, line)
            scratch[pl.ds(c * GROUPS * total + first + r, GROUPS, stride=total), :] = line


def columns_of(t):
    return slice(t * WIDTH, (t + 1) * WIDTH)


def normalise(pair_ref, mean_ref, scale_ref):
    scale = spread_pairs(scale_ref[...])
    normed = (pair_ref[...].astype(f32) - spread_pairs(mean_ref[...])) * scale
    return normed, scale


def edges_kernel(*refs):
    given, out_ref, scratch, held, sems = refs[:8], refs[8], refs[9], refs[10:18], refs[18]
    copies = [pltpu.make_async_copy(a, b, sems.at[n]) for n, (a, b) in enumerate(zip(given, held))]
    for copy in copies:
        copy.start()
    for copy in copies:
        copy.wait()
    pair_ref, mean_ref, scale_ref, mask_ref, lg, lv, rg, rv = held
    kept_scale = spread_pairs(scale_ref[...] * mask_ref[...].astype(f32))
    low = ((pair_ref[...].astype(f32) - spread_pairs(mean_ref[...])) * kept_scale).astype(bf16)
    parts = []
    for gate, value in ((lg, lv), (rg, rv)):
        both = dot(low, jnp.concatenate([gate[...], value[...]], axis=1))
        parts.append(jax.nn.sigmoid(both[:, :WIDTH]) * both[:, WIDTH:])
    out_ref[...] = to_messages(parts, scratch)


def take_right_kernel(in_ref, *refs):
    given, (out_ref, *made), (scratch, panels) = refs[:6], refs[6:9], refs[9:]
    scratch[...] = in_ref[...].astype(f32)

    def store(i, t, tile):
        panels[t, pl.ds(i * (GROUPS + 1), GROUPS), :] = tile

    assemble(scratch, PAIRED, PAIRED, lambda c: c, store)
    for group in range(GROUPS):
        rows = [panels[t, pl.ds(group, SIDE, stride=GROUPS + 1), :] for t in range(TILES)]
        out_ref[group * SIDE : (group + 1) * SIDE, :] = jnp.concatenate(rows, axis=1).astype(bf16)
    on_core(1, lambda: ready(given, *made))


def assemble_left(in_ref, scratch, panel, lines, spot, spots=range(BLOCKS)):
    scratch[...] = in_ref[...].astype(f32)

    def store(i, t, tile):
        panel[i * GROUPS : (i + 1) * GROUPS, columns_of(t)] = tile

    assemble(scratch, lines, 0, spot, store, spots)


def rows_of(panel):
    return lambda i, t: panel[i * GROUPS : (i + 1) * GROUPS, columns_of(t)]


def take_left_kernel(in_ref, out_ref, scratch, panel):
    assemble_left(in_ref, scratch, panel, PAIRED, lambda c: c)
    out_ref[...] = panel[...].astype(bf16)


def half_mixed(left_ref, right_ref, scratch, panel):
    panel[:, :HALF] = dot(left_ref[...], right_ref[...], ((1,), (1,)))
    disassemble(rows_of(panel), scratch, ALONE, 0, BLOCKS // 2)


def mix_own_kernel(left_ref, right_ref, out_ref, scratch, panel):
    half_mixed(left_ref, right_ref, scratch, panel)
    out_ref[...] = scratch[...].astype(bf16)


def mix_kernel(own_ref, left_ref, right_ref, out_ref, scratch, panel):
    half_mixed(left_ref, right_ref, scratch, panel)
    size = GROUPS * ALONE
    for core in range(2):

        @pl.when(lax.axis_index("core") == core)
        def _(core=core):
            for n in range(BLOCKS // 2):
                here, mine, other = (slice(at * size, (at + 1) * size) for at in (n, 2 * n + core, 2 * n + 1 - core))
                out_ref[mine, :] = own_ref[here, :]
                out_ref[other, :] = scratch[here, :].astype(bf16)


def ready(given, grad_ref, factor_ref):
    pair_ref, mean_ref, scale_ref, cot_ref, gate_ref, weight_ref = given
    normed, _ = normalise(pair_ref, mean_ref, scale_ref)
    out_sig = jax.nn.sigmoid(dot(normed.astype(bf16), gate_ref[...]))
    grad_y = cot_ref[...].astype(f32) * out_sig
    grad_ref[...] = dot(grad_y.astype(bf16), weight_ref[...], ((1,), (1,)))
    factor_ref[...] = grad_y * (1.0 - out_sig)


def on_core(core, work):
    pl.when(lax.axis_index("core") == core)(work)


def hand_on(early, made):
    def work():
        for a, b in zip(early, made):
            b[...] = a[...]

    on_core(1, work)


def ready_later_kernel(*refs):
    early, given, made = refs[:2], refs[2:-2], refs[-2:]
    hand_on(early, made)
    on_core(0, lambda: ready(given, *made))


def middle_kernel(in_ref, grad_ref, out_ref, normed_ref, scratch):
    (mixed,) = from_messages(in_ref, scratch, 1)
    centred = mixed - jnp.mean(mixed, axis=-1, keepdims=True)
    mix_scale = lax.rsqrt(jnp.mean(centred * centred, axis=-1, keepdims=True) + epsilon)
    mix_normed = centred * mix_scale
    normed_ref[...] = mix_normed.astype(bf16)
    grad_mix = layer_back(grad_ref[...], mix_normed, mix_scale)
    out_ref[...] = to_messages([grad_mix], scratch)


def right_grad_all(in_ref, left_ref, grad_ref, own_ref, scratch, panel):
    assemble_left(in_ref, scratch, panel, ALONE, place)
    grad = panel[...]
    grad_ref[...] = grad.astype(bf16)
    first = lax.axis_index("core") == 0
    sums = dot(jnp.transpose(grad).astype(bf16), left_ref[...])
    own_ref[...] = jnp.where(first, sums[:HALF], sums[HALF:])
    return jnp.where(first, sums[HALF:], sums[:HALF])


def right_grad_kernel(in_ref, left_ref, *refs):
    given, (grad_ref, own_ref, sent_ref), made, (scratch, panel) = refs[:12], refs[12:15], refs[15:19], refs[19:]

    def only_sent():
        assemble_left(in_ref, scratch, panel, ALONE, place, range(BLOCKS // 2, BLOCKS))
        turned = jnp.transpose(panel[:, WIDTH:])[HALF - WIDTH :]
        sent_ref[...] = dot(turned.astype(bf16), left_ref[...]).astype(bf16)

    def everything():
        sent_ref[...] = right_grad_all(in_ref, left_ref, grad_ref, own_ref, scratch, panel).astype(bf16)
        prepare(given, *made)

    on_core(0, only_sent)
    on_core(1, everything)


def right_grad_later_kernel(*refs):
    early, (in_ref, left_ref, *given), made, (scratch, panel) = refs[:6], refs[6:20], refs[20:26], refs[26:]
    hand_on(early, made)

    def everything():
        right_grad_all(in_ref, left_ref, *made[:2], scratch, panel)
        prepare(given, *made[2:])

    on_core(0, everything)


def left_grad_kernel(grad_ref, own_ref, other_ref, out_ref, right, panel):
    core = lax.axis_index("core")
    right[core] = own_ref[...]
    right[1 - core] = other_ref[...]
    panel[...] = dot(grad_ref[...], right[...].reshape(TOKENS, TOKENS))
    disassemble(rows_of(panel), out_ref, PAIRED, 0, BLOCKS)


def return_kernel(lines_ref, own_ref, other_ref, out_ref, scratch, panels):
    for group in range(GROUPS):
        here = slice(group * SIDE, (group + 1) * SIDE)
        total = own_ref[here, :] + other_ref[here, :].astype(f32)
        for t in range(TILES):
            panels[t, pl.ds(group * (SIDE + 1), SIDE), :] = total[:, columns_of(t)]
    load = lambda i, t: panels[t, pl.ds(i, GROUPS, stride=SIDE + 1), :]
    disassemble(load, scratch, PAIRED, PAIRED, BLOCKS)
    size = GROUPS * 2 * PAIRED
    is_left = lax.broadcasted_iota(jnp.int32, (size, WIDTH), 0) % (2 * PAIRED) < PAIRED
    for c in range(BLOCKS):
        here = slice(c * size, (c + 1) * size)
        out_ref[here, :] = jnp.where(is_left, lines_ref[here, :], scratch[here, :]).astype(bf16)


def prepare(given, normed_ref, scaled_ref, base_ref, factors_ref):
    pair_ref, mean_ref, scale_ref, mask_ref, mix_normed_ref, factor_ref, weight_ref, lg, lv, rg, rv, og = given
    normed, scale = normalise(pair_ref, mean_ref, scale_ref)
    normed_ref[...] = normed
    scaled_ref[...] = scale
    grad_gate = factor_ref[...] * dot(mix_normed_ref[...], weight_ref[...])
    base_ref[...] = dot(grad_gate.astype(bf16), og[...], ((1,), (1,)))
    low = normed.astype(bf16)
    keep = spread_pairs(mask_ref[...].astype(f32))
    for n, (gate, value) in enumerate(((lg, lv), (rg, rv))):
        both = dot(low, jnp.concatenate([gate[...], value[...]], axis=1))
        sig, lin = jax.nn.sigmoid(both[:, :WIDTH]), both[:, WIDTH:]
        factors_ref[2 * n + 1] = keep * sig
        factors_ref[2 * n] = keep * lin * sig * (1.0 - sig)


def last_kernel(
    in_ref, normed_ref, scale_ref, base_ref, factors_ref, lg, lv, rg, rv, out_ref, scratch, held, sems
):
    scratch[...] = in_ref[...].astype(f32)
    weights = [jnp.concatenate([gate[...], value[...]], axis=1) for gate, value in ((lg, lv), (rg, rv))]
    copies = []
    for r in range(PAIRED):
        rows = rows_in(r, PAIRED)
        here = slice(rows[0] * SIDE, (rows[-1] + 1) * SIDE)
        grad_normed = base_ref[here, :]
        for n in range(2):
            turned = jnp.transpose(scratch[pl.ds(PAIRED * n + r, WIDTH, stride=2 * PAIRED), :])
            grad = turned[: len(rows) * SIDE]
            pre_grads = jnp.concatenate([grad * factors_ref[2 * n, here], grad * factors_ref[2 * n + 1, here]], axis=1)
            grad_normed += dot(pre_grads.astype(bf16), weights[n], ((1,), (1,)))
        held[here, :] = layer_back(grad_normed, normed_ref[here, :], scale_ref[here, :])
        copies.append(pltpu.make_async_copy(held.at[here], out_ref.at[here], sems.at[r]))
        copies[-1].start()
    for copy in copies:
        copy.wait()


def call(kernel, outs, *args, scratch=(), name=None, space=VMEM, out_space=VMEM):
    return pl.pallas_call(
        kernel,
        out_shape=[jax.ShapeDtypeStruct(shape, dtype) for shape, dtype in outs],
        in_specs=[space for _ in args],
        out_specs=[out_space for _ in outs],
        scratch_shapes=list(scratch),
        compiler_params=pltpu.CompilerParams(vmem_limit_bytes=48 * 1024 * 1024),
        name=name,
    )(*args)


def spread(messages):
    paired = messages.reshape(WIDTH, -1, 2, WIDTH)
    return lax.all_to_all(paired, SPREAD, 0, 0, tiled=True).reshape(messages.shape)


def swap(value):
    return lax.ppermute(value, "core", [(0, 1), (1, 0)])


def per_device(
    pair_input,
    norm_mean,
    norm_scale,
    pair_mask,
    cotangent,
    left_gate,
    left_value,
    right_gate,
    right_value,
    output_gate,
    output_weight,
):
    pair = pair_input.reshape(PAIRS, WIDTH)
    cot = cotangent.reshape(PAIRS, WIDTH)
    one, two = (WIDTH * ALONE, WIDTH), (WIDTH * 2 * PAIRED, WIDTH)
    line_one, line_two = pltpu.VMEM(one, f32), pltpu.VMEM(two, f32)
    panel_left = pltpu.VMEM((HALF, TOKENS), f32)
    panels_in = pltpu.VMEM((TILES, SIDE * (GROUPS + 1), WIDTH), f32)
    panels_out = pltpu.VMEM((TILES, GROUPS * (SIDE + 1), WIDTH), f32)
    one, two = (one, bf16), (two, bf16)
    panel, wide = ((HALF, TOKENS), bf16), ((HALF, TOKENS), f32)
    given = [
        pltpu.with_memory_space_constraint(a, pltpu.HBM)
        for a in (pair, norm_mean, norm_scale, pair_mask, left_gate, left_value, right_gate, right_value)
    ]
    held = [pltpu.VMEM(a.shape, a.dtype) for a in given]
    (sent,) = call(
        edges_kernel, [two], *given, scratch=[line_two] + held + [pltpu.SemaphoreType.DMA((len(given),))],
        name="edges", space=HBM,
    )
    came = spread(sent)
    many = ((PAIRS, WIDTH), f32)
    given = [pair, norm_mean, norm_scale, cot, output_gate, output_weight]
    right_own, *made = call(
        take_right_kernel, [panel, many, many], came, *given, scratch=[line_two, panels_in], name="take_right"
    )
    right_other = swap(right_own)
    (left,) = call(take_left_kernel, [panel], came, scratch=[line_two, panel_left], name="take_left")
    line_half, panel_half = pltpu.VMEM((WIDTH * ALONE // 2, WIDTH), f32), pltpu.VMEM((HALF, 2 * WIDTH), f32)
    (mixed_own,) = call(
        mix_own_kernel, [((WIDTH * ALONE // 2, WIDTH), bf16)], left, right_own, scratch=[line_half, panel_half], name="mix_own",
    )
    grad_mixnorm, factor = call(
        ready_later_kernel, [many, many], *made, *given, name="ready"
    )
    mixed_own, grad_mixnorm, factor = lax.optimization_barrier((mixed_own, grad_mixnorm, factor))
    (sent,) = call(
        mix_kernel, [one], mixed_own, left, right_other, scratch=[line_half, panel_half], name="mix"
    )
    came = spread(sent)
    sent, mix_normed = call(
        middle_kernel, [one, ((PAIRS, WIDTH), bf16)], came, grad_mixnorm, scratch=[line_one], name="middle"
    )
    came = spread(sent)
    given = [
        pair, norm_mean, norm_scale, pair_mask, mix_normed, factor, output_weight, left_gate, left_value, right_gate,
        right_value, output_gate,
    ]
    factors = ((4, PAIRS, WIDTH), f32)
    grad, own, sent, *made = call(
        right_grad_kernel, [panel, wide, panel, many, many, many, factors], came, left, *given,
        scratch=[line_one, panel_left], name="right_grad",
    )
    other = swap(sent)
    lined = ((WIDTH * 2 * PAIRED, WIDTH), f32)
    grad, own, *prepared = call(
        right_grad_later_kernel, [panel, wide, many, many, many, factors], grad, own, *made, came, left, *given,
        scratch=[line_one, panel_left], name="right_grad_later",
    )
    (lines,) = call(
        left_grad_kernel, [lined], grad, right_own, right_other,
        scratch=[pltpu.VMEM((2, HALF, TOKENS), bf16), panel_left], name="left_grad",
    )
    lines, prepared = lax.optimization_barrier((lines, prepared))
    (sent,) = call(return_kernel, [two], lines, own, other, scratch=[line_two, panels_out], name="return")
    came = spread(sent)
    (out,) = call(
        last_kernel, [many], came, *prepared, left_gate, left_value, right_gate, right_value,
        scratch=[line_two, pltpu.VMEM((PAIRS, WIDTH), f32), pltpu.SemaphoreType.DMA((PAIRED,))], name="last",
        out_space=HBM,
    )
    return out.reshape(SIDE, SIDE, WIDTH)


def solution(mesh):
    fine = Mesh(mesh.devices.reshape(2, 4, 2, 4, 4), ("z_lo", "x", "core", "z_hi", "y"))
    row, col = ("z_lo", "x", "core"), ("z_hi", "y")
    placed = (P(row, col, None), P(row, col), P(row, col), P(row, col), P(row, col, None)) + (P(),) * 6
    return jax.shard_map(per_device, mesh=fine, in_specs=placed, out_specs=P(row, col, None), check_vma=False)
```

```python
import jax
import jax.numpy as jnp
from jax import lax
from jax.experimental import pallas as pl
from jax.experimental.pallas import tpu as pltpu
from jax.sharding import Mesh, PartitionSpec as P

epsilon = 1e-05
SIDE = 24
BLOCKS = 16
PAIRS = SIDE * SIDE
WIDTH = 128
GROUPS = 8
HALF = GROUPS * SIDE
TOKENS = SIDE * BLOCKS
SPREAD = ("z_hi", "y", "z_lo", "x")
TILES = TOKENS // WIDTH
ALONE, PAIRED = 6, 5
f32 = jnp.float32
bf16 = jnp.bfloat16
VMEM = pl.BlockSpec(memory_space=pltpu.VMEM)
HBM = pl.BlockSpec(memory_space=pltpu.HBM)


def dot(a, b, over=((1,), (0,))):
    return lax.dot_general(a, b, (over, ((), ())), preferred_element_type=f32)


def spread_pairs(value):
    turned = jnp.transpose(value)
    return jnp.concatenate([jnp.broadcast_to(turned[:, i : i + 1], (SIDE, WIDTH)) for i in range(SIDE)], axis=0)


def lanes(rows):
    return lax.broadcasted_iota(jnp.int32, (rows, WIDTH), 1)


def roll(value, by):
    by = by % WIDTH
    return value if by == 0 else pltpu.roll(value, by, 1)


def place(c):
    return (c % 2) * GROUPS + c // 2


def layer_back(grad, normed, scale):
    centre = jnp.mean(grad, axis=-1, keepdims=True)
    along = jnp.mean(grad * normed, axis=-1, keepdims=True)
    return scale * (grad - centre - normed * along)


def rows_in(line, lines):
    many = -(-SIDE // lines)
    return range(line * many, min((line + 1) * many, SIDE))


def to_messages(parts, scratch):
    total = scratch.shape[0] // WIDTH
    lines = total // len(parts)
    for p, part in enumerate(parts):
        for r in range(lines):
            stack = [part[i * SIDE : (i + 1) * SIDE] for i in rows_in(r, lines)]
            stack.append(jnp.zeros((WIDTH - len(stack) * SIDE, WIDTH), f32))
            turned = jnp.transpose(jnp.concatenate(stack, axis=0))
            scratch[pl.ds(lines * p + r, WIDTH, stride=total), :] = turned
    return scratch[...].astype(bf16)


def from_messages(in_ref, scratch, count):
    total = in_ref.shape[0] // WIDTH
    lines = total // count
    scratch[...] = in_ref[...].astype(f32)
    parts = []
    for p in range(count):
        rows = [None] * SIDE
        for r in range(lines):
            turned = jnp.transpose(scratch[pl.ds(lines * p + r, WIDTH, stride=total), :])
            for n, i in enumerate(rows_in(r, lines)):
                rows[i] = turned[n * SIDE : (n + 1) * SIDE]
        parts.append(jnp.concatenate(rows, axis=0))
    return parts


def chain(segments, lane):
    line = None
    for begin, source in sorted(segments, key=lambda segment: segment[0]):
        line = source if line is None else jnp.where(lane >= begin, source, line)
    return line


def assemble(scratch, lines, first, spot, store, spots=range(BLOCKS)):
    total = scratch.shape[0] // WIDTH
    lane = lanes(GROUPS)
    order = {spot(c): c for c in range(BLOCKS)}
    for r in range(lines):
        found = {
            at: scratch[pl.ds(order[at] * GROUPS * total + first + r, GROUPS, stride=total), :] for at in spots
        }
        for n, i in enumerate(rows_in(r, lines)):
            for t in range(TILES):
                tile = None
                for at in spots:
                    begin, end = at * SIDE - t * WIDTH, (at + 1) * SIDE - t * WIDTH
                    if end <= 0 or begin >= WIDTH:
                        continue
                    piece = roll(found[at], begin - n * SIDE)
                    tile = piece if tile is None else jnp.where(lane >= begin, piece, tile)
                if tile is not None:
                    store(i, t, tile)


def disassemble(load, scratch, lines, first, blocks):
    total = scratch.shape[0] // (GROUPS * blocks)
    tiles = -(-blocks * SIDE // WIDTH)
    lane = lanes(GROUPS)
    for r in range(lines):
        turned = []
        for n, i in enumerate(rows_in(r, lines)):
            shift = n * SIDE
            moved = [roll(load(i, t), shift) for t in range(tiles)]
            if shift:
                moved = [jnp.where(lane < shift, moved[t - 1], moved[t]) for t in range(tiles)]
            turned.append(moved)
        for c in range(blocks):
            segments = []
            for n, moved in enumerate(turned):
                t, start = divmod((c + n) * SIDE, WIDTH)
                segments.append((start, moved[t % tiles]))
                if start + SIDE > WIDTH:
                    segments.append((0, moved[(t + 1) % tiles]))
            line = roll(chain(segments, lane), -c * SIDE)
            scratch[pl.ds(c * GROUPS * total + first + r, GROUPS, stride=total), :] = line


def columns_of(t):
    return slice(t * WIDTH, (t + 1) * WIDTH)


def normalise(pair_ref, mean_ref, scale_ref):
    scale = spread_pairs(scale_ref[...])
    normed = (pair_ref[...].astype(f32) - spread_pairs(mean_ref[...])) * scale
    return normed, scale


def edges_kernel(*refs):
    given, out_ref, scratch, held, sems = refs[:8], refs[8], refs[9], refs[10:18], refs[18]
    copies = [pltpu.make_async_copy(a, b, sems.at[n]) for n, (a, b) in enumerate(zip(given, held))]
    for copy in copies:
        copy.start()
    for copy in copies:
        copy.wait()
    pair_ref, mean_ref, scale_ref, mask_ref, lg, lv, rg, rv = held
    kept_scale = spread_pairs(scale_ref[...] * mask_ref[...].astype(f32))
    low = ((pair_ref[...].astype(f32) - spread_pairs(mean_ref[...])) * kept_scale).astype(bf16)
    parts = []
    for gate, value in ((lg, lv), (rg, rv)):
        both = dot(low, jnp.concatenate([gate[...], value[...]], axis=1))
        parts.append(jax.nn.sigmoid(both[:, :WIDTH]) * both[:, WIDTH:])
    out_ref[...] = to_messages(parts, scratch)


def take_right_kernel(in_ref, *refs):
    given, (out_ref, *made), (scratch, panels) = refs[:6], refs[6:9], refs[9:]
    scratch[...] = in_ref[...].astype(f32)

    def store(i, t, tile):
        panels[t, pl.ds(i * (GROUPS + 1), GROUPS), :] = tile

    assemble(scratch, PAIRED, PAIRED, lambda c: c, store)
    for group in range(GROUPS):
        rows = [panels[t, pl.ds(group, SIDE, stride=GROUPS + 1), :] for t in range(TILES)]
        out_ref[group * SIDE : (group + 1) * SIDE, :] = jnp.concatenate(rows, axis=1).astype(bf16)
    on_core(1, lambda: ready(given, *made))


def assemble_left(in_ref, scratch, panel, lines, spot, spots=range(BLOCKS)):
    scratch[...] = in_ref[...].astype(f32)

    def store(i, t, tile):
        panel[i * GROUPS : (i + 1) * GROUPS, columns_of(t)] = tile

    assemble(scratch, lines, 0, spot, store, spots)


def rows_of(panel):
    return lambda i, t: panel[i * GROUPS : (i + 1) * GROUPS, columns_of(t)]


def take_left_kernel(in_ref, out_ref, scratch, panel):
    assemble_left(in_ref, scratch, panel, PAIRED, lambda c: c)
    out_ref[...] = panel[...].astype(bf16)


def half_mixed(left_ref, right_ref, scratch, panel):
    panel[:, :HALF] = dot(left_ref[...], right_ref[...], ((1,), (1,)))
    disassemble(rows_of(panel), scratch, ALONE, 0, BLOCKS // 2)


def mix_own_kernel(left_ref, right_ref, out_ref, scratch, panel):
    half_mixed(left_ref, right_ref, scratch, panel)
    out_ref[...] = scratch[...].astype(bf16)


def mix_kernel(own_ref, left_ref, right_ref, out_ref, scratch, panel):
    half_mixed(left_ref, right_ref, scratch, panel)
    size = GROUPS * ALONE
    for core in range(2):

        @pl.when(lax.axis_index("core") == core)
        def _(core=core):
            for n in range(BLOCKS // 2):
                here, mine, other = (slice(at * size, (at + 1) * size) for at in (n, 2 * n + core, 2 * n + 1 - core))
                out_ref[mine, :] = own_ref[here, :]
                out_ref[other, :] = scratch[here, :].astype(bf16)


def ready(given, grad_ref, factor_ref):
    pair_ref, mean_ref, scale_ref, cot_ref, gate_ref, weight_ref = given
    normed, _ = normalise(pair_ref, mean_ref, scale_ref)
    out_sig = jax.nn.sigmoid(dot(normed.astype(bf16), gate_ref[...]))
    grad_y = cot_ref[...].astype(f32) * out_sig
    grad_ref[...] = dot(grad_y.astype(bf16), weight_ref[...], ((1,), (1,)))
    factor_ref[...] = grad_y * (1.0 - out_sig)


def on_core(core, work):
    pl.when(lax.axis_index("core") == core)(work)


def hand_on(early, made):
    def work():
        for a, b in zip(early, made):
            b[...] = a[...]

    on_core(1, work)


def ready_later_kernel(*refs):
    early, given, made = refs[:2], refs[2:-2], refs[-2:]
    hand_on(early, made)
    on_core(0, lambda: ready(given, *made))


def middle_kernel(in_ref, grad_ref, out_ref, normed_ref, scratch):
    (mixed,) = from_messages(in_ref, scratch, 1)
    centred = mixed - jnp.mean(mixed, axis=-1, keepdims=True)
    mix_scale = lax.rsqrt(jnp.mean(centred * centred, axis=-1, keepdims=True) + epsilon)
    mix_normed = centred * mix_scale
    normed_ref[...] = mix_normed.astype(bf16)
    grad_mix = layer_back(grad_ref[...], mix_normed, mix_scale)
    out_ref[...] = to_messages([grad_mix], scratch)


def right_grad_all(in_ref, left_ref, grad_ref, own_ref, scratch, panel):
    assemble_left(in_ref, scratch, panel, ALONE, place)
    grad = panel[...]
    grad_ref[...] = grad.astype(bf16)
    first = lax.axis_index("core") == 0
    sums = dot(jnp.transpose(grad).astype(bf16), left_ref[...])
    own_ref[...] = jnp.where(first, sums[:HALF], sums[HALF:])
    return jnp.where(first, sums[HALF:], sums[:HALF])


def right_grad_kernel(in_ref, left_ref, *refs):
    given, (grad_ref, own_ref, sent_ref), made, (scratch, panel) = refs[:12], refs[12:15], refs[15:19], refs[19:]

    def only_sent():
        assemble_left(in_ref, scratch, panel, ALONE, place, range(BLOCKS // 2, BLOCKS))
        turned = jnp.transpose(panel[:, WIDTH:])[HALF - WIDTH :]
        sent_ref[...] = dot(turned.astype(bf16), left_ref[...]).astype(bf16)

    def everything():
        sent_ref[...] = right_grad_all(in_ref, left_ref, grad_ref, own_ref, scratch, panel).astype(bf16)
        prepare(given, *made)

    on_core(0, only_sent)
    on_core(1, everything)


def right_grad_later_kernel(*refs):
    early, (in_ref, left_ref, *given), made, (scratch, panel) = refs[:6], refs[6:20], refs[20:26], refs[26:]
    hand_on(early, made)

    def everything():
        right_grad_all(in_ref, left_ref, *made[:2], scratch, panel)
        prepare(given, *made[2:])

    on_core(0, everything)


def left_grad_kernel(grad_ref, own_ref, other_ref, out_ref, right, panel):
    core = lax.axis_index("core")
    right[core] = own_ref[...]
    right[1 - core] = other_ref[...]
    panel[...] = dot(grad_ref[...], right[...].reshape(TOKENS, TOKENS))
    disassemble(rows_of(panel), out_ref, PAIRED, 0, BLOCKS)


def return_kernel(lines_ref, own_ref, other_ref, out_ref, scratch, panels):
    for group in range(GROUPS):
        here = slice(group * SIDE, (group + 1) * SIDE)
        total = own_ref[here, :] + other_ref[here, :].astype(f32)
        for t in range(TILES):
            panels[t, pl.ds(group * (SIDE + 1), SIDE), :] = total[:, columns_of(t)]
    load = lambda i, t: panels[t, pl.ds(i, GROUPS, stride=SIDE + 1), :]
    disassemble(load, scratch, PAIRED, PAIRED, BLOCKS)
    size = GROUPS * 2 * PAIRED
    is_left = lax.broadcasted_iota(jnp.int32, (size, WIDTH), 0) % (2 * PAIRED) < PAIRED
    for c in range(BLOCKS):
        here = slice(c * size, (c + 1) * size)
        out_ref[here, :] = jnp.where(is_left, lines_ref[here, :], scratch[here, :]).astype(bf16)


def prepare(given, normed_ref, scaled_ref, base_ref, factors_ref):
    pair_ref, mean_ref, scale_ref, mask_ref, mix_normed_ref, factor_ref, weight_ref, lg, lv, rg, rv, og = given
    normed, scale = normalise(pair_ref, mean_ref, scale_ref)
    normed_ref[...] = normed
    scaled_ref[...] = scale
    grad_gate = factor_ref[...] * dot(mix_normed_ref[...], weight_ref[...])
    base_ref[...] = dot(grad_gate.astype(bf16), og[...], ((1,), (1,)))
    low = normed.astype(bf16)
    keep = spread_pairs(mask_ref[...].astype(f32))
    for n, (gate, value) in enumerate(((lg, lv), (rg, rv))):
        both = dot(low, jnp.concatenate([gate[...], value[...]], axis=1))
        sig, lin = jax.nn.sigmoid(both[:, :WIDTH]), both[:, WIDTH:]
        factors_ref[2 * n + 1] = keep * sig
        factors_ref[2 * n] = keep * lin * sig * (1.0 - sig)


def last_kernel(
    in_ref, normed_ref, scale_ref, base_ref, factors_ref, lg, lv, rg, rv, out_ref, scratch, held, sems
):
    scratch[...] = in_ref[...].astype(f32)
    weights = [jnp.concatenate([gate[...], value[...]], axis=1) for gate, value in ((lg, lv), (rg, rv))]
    copies = []
    for r in range(PAIRED):
        rows = rows_in(r, PAIRED)
        here = slice(rows[0] * SIDE, (rows[-1] + 1) * SIDE)
        grad_normed = base_ref[here, :]
        for n in range(2):
            turned = jnp.transpose(scratch[pl.ds(PAIRED * n + r, WIDTH, stride=2 * PAIRED), :])
            grad = turned[: len(rows) * SIDE]
            pre_grads = jnp.concatenate([grad * factors_ref[2 * n, here], grad * factors_ref[2 * n + 1, here]], axis=1)
            grad_normed += dot(pre_grads.astype(bf16), weights[n], ((1,), (1,)))
        held[here, :] = layer_back(grad_normed, normed_ref[here, :], scale_ref[here, :])
        copies.append(pltpu.make_async_copy(held.at[here], out_ref.at[here], sems.at[r]))
        copies[-1].start()
    for copy in copies:
        copy.wait()


def call(kernel, outs, *args, scratch=(), name=None, space=VMEM, out_space=VMEM):
    return pl.pallas_call(
        kernel,
        out_shape=[jax.ShapeDtypeStruct(shape, dtype) for shape, dtype in outs],
        in_specs=[space for _ in args],
        out_specs=[out_space for _ in outs],
        scratch_shapes=list(scratch),
        compiler_params=pltpu.CompilerParams(vmem_limit_bytes=48 * 1024 * 1024),
        name=name,
    )(*args)


def spread(messages):
    paired = messages.reshape(WIDTH, -1, 2, WIDTH)
    return lax.all_to_all(paired, SPREAD, 0, 0, tiled=True).reshape(messages.shape)


def swap(value):
    return lax.ppermute(value, "core", [(0, 1), (1, 0)])


def per_device(
    pair_input,
    norm_mean,
    norm_scale,
    pair_mask,
    cotangent,
    left_gate,
    left_value,
    right_gate,
    right_value,
    output_gate,
    output_weight,
):
    pair = pair_input.reshape(PAIRS, WIDTH)
    cot = cotangent.reshape(PAIRS, WIDTH)
    one, two = (WIDTH * ALONE, WIDTH), (WIDTH * 2 * PAIRED, WIDTH)
    line_one, line_two = pltpu.VMEM(one, f32), pltpu.VMEM(two, f32)
    panel_left = pltpu.VMEM((HALF, TOKENS), f32)
    panels_in = pltpu.VMEM((TILES, SIDE * (GROUPS + 1), WIDTH), f32)
    panels_out = pltpu.VMEM((TILES, GROUPS * (SIDE + 1), WIDTH), f32)
    one, two = (one, bf16), (two, bf16)
    panel, wide = ((HALF, TOKENS), bf16), ((HALF, TOKENS), f32)
    given = [
        pltpu.with_memory_space_constraint(a, pltpu.HBM)
        for a in (pair, norm_mean, norm_scale, pair_mask, left_gate, left_value, right_gate, right_value)
    ]
    held = [pltpu.VMEM(a.shape, a.dtype) for a in given]
    (sent,) = call(
        edges_kernel, [two], *given, scratch=[line_two] + held + [pltpu.SemaphoreType.DMA((len(given),))],
        name="edges", space=HBM,
    )
    came = spread(sent)
    many = ((PAIRS, WIDTH), f32)
    given = [pair, norm_mean, norm_scale, cot, output_gate, output_weight]
    right_own, *made = call(
        take_right_kernel, [panel, many, many], came, *given, scratch=[line_two, panels_in], name="take_right"
    )
    right_other = swap(right_own)
    (left,) = call(take_left_kernel, [panel], came, scratch=[line_two, panel_left], name="take_left")
    line_half, panel_half = pltpu.VMEM((WIDTH * ALONE // 2, WIDTH), f32), pltpu.VMEM((HALF, 2 * WIDTH), f32)
    (mixed_own,) = call(
        mix_own_kernel, [((WIDTH * ALONE // 2, WIDTH), bf16)], left, right_own, scratch=[line_half, panel_half], name="mix_own",
    )
    grad_mixnorm, factor = call(
        ready_later_kernel, [many, many], *made, *given, name="ready"
    )
    mixed_own, grad_mixnorm, factor = lax.optimization_barrier((mixed_own, grad_mixnorm, factor))
    (sent,) = call(
        mix_kernel, [one], mixed_own, left, right_other, scratch=[line_half, panel_half], name="mix"
    )
    came = spread(sent)
    sent, mix_normed = call(
        middle_kernel, [one, ((PAIRS, WIDTH), bf16)], came, grad_mixnorm, scratch=[line_one], name="middle"
    )
    came = spread(sent)
    given = [
        pair, norm_mean, norm_scale, pair_mask, mix_normed, factor, output_weight, left_gate, left_value, right_gate,
        right_value, output_gate,
    ]
    factors = ((4, PAIRS, WIDTH), f32)
    grad, own, sent, *made = call(
        right_grad_kernel, [panel, wide, panel, many, many, many, factors], came, left, *given,
        scratch=[line_one, panel_left], name="right_grad",
    )
    other = swap(sent)
    lined = ((WIDTH * 2 * PAIRED, WIDTH), f32)
    grad, own, *prepared = call(
        right_grad_later_kernel, [panel, wide, many, many, many, factors], grad, own, *made, came, left, *given,
        scratch=[line_one, panel_left], name="right_grad_later",
    )
    (lines,) = call(
        left_grad_kernel, [lined], grad, right_own, right_other,
        scratch=[pltpu.VMEM((2, HALF, TOKENS), bf16), panel_left], name="left_grad",
    )
    lines, prepared = lax.optimization_barrier((lines, prepared))
    (sent,) = call(return_kernel, [two], lines, own, other, scratch=[line_two, panels_out], name="return")
    came = spread(sent)
    (out,) = call(
        last_kernel, [many], came, *prepared, left_gate, left_value, right_gate, right_value,
        scratch=[line_two, pltpu.VMEM((PAIRS, WIDTH), f32), pltpu.SemaphoreType.DMA((PAIRED,))], name="last",
        out_space=HBM,
    )
    return out.reshape(SIDE, SIDE, WIDTH)


def solution(mesh):
    fine = Mesh(mesh.devices.reshape(2, 4, 2, 4, 4), ("z_lo", "x", "core", "z_hi", "y"))
    row, col = ("z_lo", "x", "core"), ("z_hi", "y")
    placed = (P(row, col, None), P(row, col), P(row, col), P(row, col), P(row, col, None)) + (P(),) * 6
    return jax.shard_map(per_device, mesh=fine, in_specs=placed, out_specs=P(row, col, None), check_vma=False)
```

```python
import jax
import jax.numpy as jnp
from jax import lax
from jax.experimental import pallas as pl
from jax.experimental.pallas import tpu as pltpu
from jax.sharding import Mesh, PartitionSpec as P

epsilon = 1e-05
SIDE = 24
BLOCKS = 16
PAIRS = SIDE * SIDE
WIDTH = 128
GROUPS = 8
HALF = GROUPS * SIDE
TOKENS = SIDE * BLOCKS
SPREAD = ("z_hi", "y", "z_lo", "x")
TILES = TOKENS // WIDTH
ALONE, PAIRED = 6, 5
f32 = jnp.float32
bf16 = jnp.bfloat16
VMEM = pl.BlockSpec(memory_space=pltpu.VMEM)
HBM = pl.BlockSpec(memory_space=pltpu.HBM)


def dot(a, b, over=((1,), (0,))):
    return lax.dot_general(a, b, (over, ((), ())), preferred_element_type=f32)


def spread_pairs(value):
    turned = jnp.transpose(value)
    return jnp.concatenate([jnp.broadcast_to(turned[:, i : i + 1], (SIDE, WIDTH)) for i in range(SIDE)], axis=0)


def lanes(rows):
    return lax.broadcasted_iota(jnp.int32, (rows, WIDTH), 1)


def roll(value, by):
    by = by % WIDTH
    return value if by == 0 else pltpu.roll(value, by, 1)


def place(c):
    return (c % 2) * GROUPS + c // 2


def layer_back(grad, normed, scale):
    centre = jnp.mean(grad, axis=-1, keepdims=True)
    along = jnp.mean(grad * normed, axis=-1, keepdims=True)
    return scale * (grad - centre - normed * along)


def rows_in(line, lines):
    many = -(-SIDE // lines)
    return range(line * many, min((line + 1) * many, SIDE))


def to_messages(parts, scratch):
    total = scratch.shape[0] // WIDTH
    lines = total // len(parts)
    for p, part in enumerate(parts):
        for r in range(lines):
            stack = [part[i * SIDE : (i + 1) * SIDE] for i in rows_in(r, lines)]
            stack.append(jnp.zeros((WIDTH - len(stack) * SIDE, WIDTH), f32))
            turned = jnp.transpose(jnp.concatenate(stack, axis=0))
            scratch[pl.ds(lines * p + r, WIDTH, stride=total), :] = turned
    return scratch[...].astype(bf16)


def from_messages(in_ref, scratch, count):
    total = in_ref.shape[0] // WIDTH
    lines = total // count
    scratch[...] = in_ref[...].astype(f32)
    parts = []
    for p in range(count):
        rows = [None] * SIDE
        for r in range(lines):
            turned = jnp.transpose(scratch[pl.ds(lines * p + r, WIDTH, stride=total), :])
            for n, i in enumerate(rows_in(r, lines)):
                rows[i] = turned[n * SIDE : (n + 1) * SIDE]
        parts.append(jnp.concatenate(rows, axis=0))
    return parts


def chain(segments, lane):
    line = None
    for begin, source in sorted(segments, key=lambda segment: segment[0]):
        line = source if line is None else jnp.where(lane >= begin, source, line)
    return line


def assemble(scratch, lines, first, spot, store, spots=range(BLOCKS)):
    total = scratch.shape[0] // WIDTH
    lane = lanes(GROUPS)
    order = {spot(c): c for c in range(BLOCKS)}
    for r in range(lines):
        found = {
            at: scratch[pl.ds(order[at] * GROUPS * total + first + r, GROUPS, stride=total), :] for at in spots
        }
        for n, i in enumerate(rows_in(r, lines)):
            for t in range(TILES):
                tile = None
                for at in spots:
                    begin, end = at * SIDE - t * WIDTH, (at + 1) * SIDE - t * WIDTH
                    if end <= 0 or begin >= WIDTH:
                        continue
                    piece = roll(found[at], begin - n * SIDE)
                    tile = piece if tile is None else jnp.where(lane >= begin, piece, tile)
                if tile is not None:
                    store(i, t, tile)


def disassemble(load, scratch, lines, first, blocks):
    total = scratch.shape[0] // (GROUPS * blocks)
    tiles = -(-blocks * SIDE // WIDTH)
    lane = lanes(GROUPS)
    for r in range(lines):
        turned = []
        for n, i in enumerate(rows_in(r, lines)):
            shift = n * SIDE
            moved = [roll(load(i, t), shift) for t in range(tiles)]
            if shift:
                moved = [jnp.where(lane < shift, moved[t - 1], moved[t]) for t in range(tiles)]
            turned.append(moved)
        for c in range(blocks):
            segments = []
            for n, moved in enumerate(turned):
                t, start = divmod((c + n) * SIDE, WIDTH)
                segments.append((start, moved[t % tiles]))
                if start + SIDE > WIDTH:
                    segments.append((0, moved[(t + 1) % tiles]))
            line = roll(chain(segments, lane), -c * SIDE)
            scratch[pl.ds(c * GROUPS * total + first + r, GROUPS, stride=total), :] = line


def columns_of(t):
    return slice(t * WIDTH, (t + 1) * WIDTH)


def normalise(pair_ref, mean_ref, scale_ref):
    scale = spread_pairs(scale_ref[...])
    normed = (pair_ref[...].astype(f32) - spread_pairs(mean_ref[...])) * scale
    return normed, scale


def edges_kernel(*refs):
    given, out_ref, scratch, held, sems = refs[:8], refs[8], refs[9], refs[10:18], refs[18]
    copies = [pltpu.make_async_copy(a, b, sems.at[n]) for n, (a, b) in enumerate(zip(given, held))]
    for copy in copies:
        copy.start()
    for copy in copies:
        copy.wait()
    pair_ref, mean_ref, scale_ref, mask_ref, lg, lv, rg, rv = held
    kept_scale = spread_pairs(scale_ref[...] * mask_ref[...].astype(f32))
    low = ((pair_ref[...].astype(f32) - spread_pairs(mean_ref[...])) * kept_scale).astype(bf16)
    parts = []
    for gate, value in ((lg, lv), (rg, rv)):
        both = dot(low, jnp.concatenate([gate[...], value[...]], axis=1))
        parts.append(jax.nn.sigmoid(both[:, :WIDTH]) * both[:, WIDTH:])
    out_ref[...] = to_messages(parts, scratch)


def take_right_kernel(in_ref, *refs):
    given, (out_ref, *made), (scratch, panels) = refs[:6], refs[6:9], refs[9:]
    scratch[...] = in_ref[...].astype(f32)

    def store(i, t, tile):
        panels[t, pl.ds(i * (GROUPS + 1), GROUPS), :] = tile

    assemble(scratch, PAIRED, PAIRED, lambda c: c, store)
    for group in range(GROUPS):
        rows = [panels[t, pl.ds(group, SIDE, stride=GROUPS + 1), :] for t in range(TILES)]
        out_ref[group * SIDE : (group + 1) * SIDE, :] = jnp.concatenate(rows, axis=1).astype(bf16)
    on_core(1, lambda: ready(given, *made))


def assemble_left(in_ref, scratch, panel, lines, spot, spots=range(BLOCKS)):
    scratch[...] = in_ref[...].astype(f32)

    def store(i, t, tile):
        panel[i * GROUPS : (i + 1) * GROUPS, columns_of(t)] = tile

    assemble(scratch, lines, 0, spot, store, spots)


def rows_of(panel):
    return lambda i, t: panel[i * GROUPS : (i + 1) * GROUPS, columns_of(t)]


def take_left_kernel(in_ref, out_ref, scratch, panel):
    assemble_left(in_ref, scratch, panel, PAIRED, lambda c: c)
    out_ref[...] = panel[...].astype(bf16)


def half_mixed(left_ref, right_ref, scratch, panel):
    panel[:, :HALF] = dot(left_ref[...], right_ref[...], ((1,), (1,)))
    disassemble(rows_of(panel), scratch, ALONE, 0, BLOCKS // 2)


def mix_own_kernel(left_ref, right_ref, out_ref, scratch, panel):
    half_mixed(left_ref, right_ref, scratch, panel)
    out_ref[...] = scratch[...].astype(bf16)


def mix_kernel(own_ref, left_ref, right_ref, out_ref, scratch, panel):
    half_mixed(left_ref, right_ref, scratch, panel)
    size = GROUPS * ALONE
    for core in range(2):

        @pl.when(lax.axis_index("core") == core)
        def _(core=core):
            for n in range(BLOCKS // 2):
                here, mine, other = (slice(at * size, (at + 1) * size) for at in (n, 2 * n + core, 2 * n + 1 - core))
                out_ref[mine, :] = own_ref[here, :]
                out_ref[other, :] = scratch[here, :].astype(bf16)


def ready(given, grad_ref, factor_ref):
    pair_ref, mean_ref, scale_ref, cot_ref, gate_ref, weight_ref = given
    normed, _ = normalise(pair_ref, mean_ref, scale_ref)
    out_sig = jax.nn.sigmoid(dot(normed.astype(bf16), gate_ref[...]))
    grad_y = cot_ref[...].astype(f32) * out_sig
    grad = dot(grad_y.astype(bf16), weight_ref[...], ((1,), (1,)))
    grad_ref[...] = grad - jnp.mean(grad, axis=-1, keepdims=True)
    factor_ref[...] = grad_y * (1.0 - out_sig)


def on_core(core, work):
    pl.when(lax.axis_index("core") == core)(work)


def hand_on(early, made):
    def work():
        for a, b in zip(early, made):
            b[...] = a[...]

    on_core(1, work)


def ready_later_kernel(*refs):
    early, given, made = refs[:2], refs[2:-2], refs[-2:]
    hand_on(early, made)
    on_core(0, lambda: ready(given, *made))


def middle_kernel(in_ref, grad_ref, out_ref, normed_ref, scratch):
    (mixed,) = from_messages(in_ref, scratch, 1)
    centred = mixed - dot(mixed.astype(bf16), jnp.full((WIDTH, WIDTH), 1 / WIDTH, bf16))
    mix_scale = lax.rsqrt(jnp.mean(centred * centred, axis=-1, keepdims=True) + epsilon)
    mix_normed = centred * mix_scale
    normed_ref[...] = mix_normed.astype(bf16)
    grad = grad_ref[...]
    grad_mix = mix_scale * (grad - mix_normed * jnp.mean(grad * mix_normed, axis=-1, keepdims=True))
    out_ref[...] = to_messages([grad_mix], scratch)


def right_grad_all(in_ref, left_ref, grad_ref, own_ref, scratch, panel):
    assemble_left(in_ref, scratch, panel, ALONE, place)
    grad = panel[...]
    grad_ref[...] = grad.astype(bf16)
    first = lax.axis_index("core") == 0
    sums = dot(grad.astype(bf16), left_ref[...], ((0,), (0,)))
    own_ref[...] = jnp.where(first, sums[:HALF], sums[HALF:])
    return jnp.where(first, sums[HALF:], sums[:HALF])


def right_grad_kernel(in_ref, left_ref, *refs):
    given, (grad_ref, own_ref, sent_ref), made, (scratch, panel) = refs[:12], refs[12:15], refs[15:19], refs[19:]

    def only_sent():
        assemble_left(in_ref, scratch, panel, ALONE, place, range(BLOCKS // 2, BLOCKS))
        sums = dot(panel[:, WIDTH:].astype(bf16), left_ref[...], ((0,), (0,)))
        sent_ref[...] = sums[HALF - WIDTH :].astype(bf16)

    def everything():
        sent_ref[...] = right_grad_all(in_ref, left_ref, grad_ref, own_ref, scratch, panel).astype(bf16)
        prepare(given, *made)

    on_core(0, only_sent)
    on_core(1, everything)


def right_grad_later_kernel(*refs):
    early, (in_ref, left_ref, *given), made, (scratch, panel) = refs[:6], refs[6:20], refs[20:26], refs[26:]
    hand_on(early, made)

    def everything():
        right_grad_all(in_ref, left_ref, *made[:2], scratch, panel)
        prepare(given, *made[2:])

    on_core(0, everything)


def left_grad_kernel(grad_ref, own_ref, other_ref, out_ref, right, panel):
    core = lax.axis_index("core")
    right[core] = own_ref[...]
    right[1 - core] = other_ref[...]
    panel[...] = dot(grad_ref[...], right[...].reshape(TOKENS, TOKENS))
    disassemble(rows_of(panel), out_ref, PAIRED, 0, BLOCKS)


def return_kernel(lines_ref, own_ref, other_ref, out_ref, scratch, panels):
    for group in range(GROUPS):
        here = slice(group * SIDE, (group + 1) * SIDE)
        total = own_ref[here, :] + other_ref[here, :].astype(f32)
        for t in range(TILES):
            panels[t, pl.ds(group * (SIDE + 1), SIDE), :] = total[:, columns_of(t)]
    load = lambda i, t: panels[t, pl.ds(i, GROUPS, stride=SIDE + 1), :]
    disassemble(load, scratch, PAIRED, PAIRED, BLOCKS)
    size = GROUPS * 2 * PAIRED
    is_left = lax.broadcasted_iota(jnp.int32, (size, WIDTH), 0) % (2 * PAIRED) < PAIRED
    for c in range(BLOCKS):
        here = slice(c * size, (c + 1) * size)
        out_ref[here, :] = jnp.where(is_left, lines_ref[here, :], scratch[here, :]).astype(bf16)


def prepare(given, normed_ref, scaled_ref, base_ref, factors_ref):
    pair_ref, mean_ref, scale_ref, mask_ref, mix_normed_ref, factor_ref, weight_ref, lg, lv, rg, rv, og = given
    normed, scale = normalise(pair_ref, mean_ref, scale_ref)
    normed_ref[...] = normed
    scaled_ref[...] = scale
    grad_gate = factor_ref[...] * dot(mix_normed_ref[...], weight_ref[...])
    base_ref[...] = dot(grad_gate.astype(bf16), og[...], ((1,), (1,)))
    low = normed.astype(bf16)
    keep = spread_pairs(mask_ref[...].astype(f32))
    for n, (gate, value) in enumerate(((lg, lv), (rg, rv))):
        both = dot(low, jnp.concatenate([gate[...], value[...]], axis=1))
        sig, lin = jax.nn.sigmoid(both[:, :WIDTH]), both[:, WIDTH:]
        factors_ref[2 * n + 1] = keep * sig
        factors_ref[2 * n] = keep * lin * sig * (1.0 - sig)


def last_kernel(
    in_ref, normed_ref, scale_ref, base_ref, factors_ref, lg, lv, rg, rv, out_ref, scratch, held, sems
):
    scratch[...] = in_ref[...].astype(f32)
    weights = [jnp.concatenate([gate[...], value[...]], axis=1) for gate, value in ((lg, lv), (rg, rv))]
    copies = []
    for r in range(PAIRED):
        rows = rows_in(r, PAIRED)
        here = slice(rows[0] * SIDE, (rows[-1] + 1) * SIDE)
        grad_normed = base_ref[here, :]
        for n in range(2):
            turned = jnp.transpose(scratch[pl.ds(PAIRED * n + r, WIDTH, stride=2 * PAIRED), :])
            grad = turned[: len(rows) * SIDE]
            pre_grads = jnp.concatenate([grad * factors_ref[2 * n, here], grad * factors_ref[2 * n + 1, here]], axis=1)
            grad_normed += dot(pre_grads.astype(bf16), weights[n], ((1,), (1,)))
        held[here, :] = layer_back(grad_normed, normed_ref[here, :], scale_ref[here, :])
        copies.append(pltpu.make_async_copy(held.at[here], out_ref.at[here], sems.at[r]))
        copies[-1].start()
    for copy in copies:
        copy.wait()


def call(kernel, outs, *args, scratch=(), name=None, space=VMEM, out_space=VMEM):
    return pl.pallas_call(
        kernel,
        out_shape=[jax.ShapeDtypeStruct(shape, dtype) for shape, dtype in outs],
        in_specs=[space for _ in args],
        out_specs=[out_space for _ in outs],
        scratch_shapes=list(scratch),
        compiler_params=pltpu.CompilerParams(vmem_limit_bytes=48 * 1024 * 1024),
        name=name,
    )(*args)


def spread(messages):
    paired = messages.reshape(WIDTH, -1, 2, WIDTH)
    return lax.all_to_all(paired, SPREAD, 0, 0, tiled=True).reshape(messages.shape)


def swap(value):
    return lax.ppermute(value, "core", [(0, 1), (1, 0)])


def per_device(
    pair_input,
    norm_mean,
    norm_scale,
    pair_mask,
    cotangent,
    left_gate,
    left_value,
    right_gate,
    right_value,
    output_gate,
    output_weight,
):
    pair = pair_input.reshape(PAIRS, WIDTH)
    cot = cotangent.reshape(PAIRS, WIDTH)
    one, two = (WIDTH * ALONE, WIDTH), (WIDTH * 2 * PAIRED, WIDTH)
    line_one, line_two = pltpu.VMEM(one, f32), pltpu.VMEM(two, f32)
    panel_left = pltpu.VMEM((HALF, TOKENS), f32)
    panels_in = pltpu.VMEM((TILES, SIDE * (GROUPS + 1), WIDTH), f32)
    panels_out = pltpu.VMEM((TILES, GROUPS * (SIDE + 1), WIDTH), f32)
    one, two = (one, bf16), (two, bf16)
    panel, wide = ((HALF, TOKENS), bf16), ((HALF, TOKENS), f32)
    given = [
        pltpu.with_memory_space_constraint(a, pltpu.HBM)
        for a in (pair, norm_mean, norm_scale, pair_mask, left_gate, left_value, right_gate, right_value)
    ]
    held = [pltpu.VMEM(a.shape, a.dtype) for a in given]
    (sent,) = call(
        edges_kernel, [two], *given, scratch=[line_two] + held + [pltpu.SemaphoreType.DMA((len(given),))],
        name="edges", space=HBM,
    )
    came = spread(sent)
    many = ((PAIRS, WIDTH), f32)
    given = [pair, norm_mean, norm_scale, cot, output_gate, output_weight]
    right_own, *made = call(
        take_right_kernel, [panel, many, many], came, *given, scratch=[line_two, panels_in], name="take_right"
    )
    right_other = swap(right_own)
    (left,) = call(take_left_kernel, [panel], came, scratch=[line_two, panel_left], name="take_left")
    line_half, panel_half = pltpu.VMEM((WIDTH * ALONE // 2, WIDTH), f32), pltpu.VMEM((HALF, 2 * WIDTH), f32)
    (mixed_own,) = call(
        mix_own_kernel, [((WIDTH * ALONE // 2, WIDTH), bf16)], left, right_own, scratch=[line_half, panel_half], name="mix_own",
    )
    grad_mixnorm, factor = call(
        ready_later_kernel, [many, many], *made, *given, name="ready"
    )
    mixed_own, grad_mixnorm, factor = lax.optimization_barrier((mixed_own, grad_mixnorm, factor))
    (sent,) = call(
        mix_kernel, [one], mixed_own, left, right_other, scratch=[line_half, panel_half], name="mix"
    )
    came = spread(sent)
    sent, mix_normed = call(
        middle_kernel, [one, ((PAIRS, WIDTH), bf16)], came, grad_mixnorm, scratch=[line_one], name="middle"
    )
    came = spread(sent)
    given = [
        pair, norm_mean, norm_scale, pair_mask, mix_normed, factor, output_weight, left_gate, left_value, right_gate,
        right_value, output_gate,
    ]
    factors = ((4, PAIRS, WIDTH), f32)
    grad, own, sent, *made = call(
        right_grad_kernel, [panel, wide, panel, many, many, many, factors], came, left, *given,
        scratch=[line_one, panel_left], name="right_grad",
    )
    other = swap(sent)
    lined = ((WIDTH * 2 * PAIRED, WIDTH), f32)
    grad, own, *prepared = call(
        right_grad_later_kernel, [panel, wide, many, many, many, factors], grad, own, *made, came, left, *given,
        scratch=[line_one, panel_left], name="right_grad_later",
    )
    (lines,) = call(
        left_grad_kernel, [lined], grad, right_own, right_other,
        scratch=[pltpu.VMEM((2, HALF, TOKENS), bf16), panel_left], name="left_grad",
    )
    lines, prepared = lax.optimization_barrier((lines, prepared))
    (sent,) = call(return_kernel, [two], lines, own, other, scratch=[line_two, panels_out], name="return")
    came = spread(sent)
    (out,) = call(
        last_kernel, [many], came, *prepared, left_gate, left_value, right_gate, right_value,
        scratch=[line_two, pltpu.VMEM((PAIRS, WIDTH), f32), pltpu.SemaphoreType.DMA((PAIRED,))], name="last",
        out_space=HBM,
    )
    return out.reshape(SIDE, SIDE, WIDTH)


def solution(mesh):
    fine = Mesh(mesh.devices.reshape(2, 4, 2, 4, 4), ("z_lo", "x", "core", "z_hi", "y"))
    row, col = ("z_lo", "x", "core"), ("z_hi", "y")
    placed = (P(row, col, None), P(row, col), P(row, col), P(row, col), P(row, col, None)) + (P(),) * 6
    return jax.shard_map(per_device, mesh=fine, in_specs=placed, out_specs=P(row, col, None), check_vma=False)
```

```python
import jax
import jax.numpy as jnp
from jax import lax
from jax.experimental import pallas as pl
from jax.experimental.pallas import tpu as pltpu
from jax.sharding import Mesh, PartitionSpec as P

epsilon = 1e-05
SIDE = 24
BLOCKS = 16
PAIRS = SIDE * SIDE
WIDTH = 128
GROUPS = 8
HALF = GROUPS * SIDE
TOKENS = SIDE * BLOCKS
SPREAD = ("z_hi", "y", "z_lo", "x")
TILES = TOKENS // WIDTH
ALONE, PAIRED = 6, 5
f32 = jnp.float32
bf16 = jnp.bfloat16
VMEM = pl.BlockSpec(memory_space=pltpu.VMEM)
HBM = pl.BlockSpec(memory_space=pltpu.HBM)


def dot(a, b, over=((1,), (0,))):
    return lax.dot_general(a, b, (over, ((), ())), preferred_element_type=f32)


def spread_pairs(value):
    turned = jnp.transpose(value)
    return jnp.concatenate([jnp.broadcast_to(turned[:, i : i + 1], (SIDE, WIDTH)) for i in range(SIDE)], axis=0)


def lanes(rows):
    return lax.broadcasted_iota(jnp.int32, (rows, WIDTH), 1)


def roll(value, by):
    by = by % WIDTH
    return value if by == 0 else pltpu.roll(value, by, 1)


def place(c):
    return (c % 2) * GROUPS + c // 2


def layer_back(grad, normed, scale):
    centre = jnp.mean(grad, axis=-1, keepdims=True)
    along = jnp.mean(grad * normed, axis=-1, keepdims=True)
    return scale * (grad - centre - normed * along)


def rows_in(line, lines):
    many = -(-SIDE // lines)
    return range(line * many, min((line + 1) * many, SIDE))


def to_messages(parts, scratch):
    total = scratch.shape[0] // WIDTH
    lines = total // len(parts)
    for p, part in enumerate(parts):
        for r in range(lines):
            stack = [part[i * SIDE : (i + 1) * SIDE] for i in rows_in(r, lines)]
            stack.append(jnp.zeros((WIDTH - len(stack) * SIDE, WIDTH), f32))
            turned = jnp.transpose(jnp.concatenate(stack, axis=0))
            scratch[pl.ds(lines * p + r, WIDTH, stride=total), :] = turned
    return scratch[...].astype(bf16)


def from_messages(in_ref, scratch, count):
    total = in_ref.shape[0] // WIDTH
    lines = total // count
    scratch[...] = in_ref[...].astype(f32)
    parts = []
    for p in range(count):
        rows = [None] * SIDE
        for r in range(lines):
            turned = jnp.transpose(scratch[pl.ds(lines * p + r, WIDTH, stride=total), :])
            for n, i in enumerate(rows_in(r, lines)):
                rows[i] = turned[n * SIDE : (n + 1) * SIDE]
        parts.append(jnp.concatenate(rows, axis=0))
    return parts


def chain(segments, lane):
    line = None
    for begin, source in sorted(segments, key=lambda segment: segment[0]):
        line = source if line is None else jnp.where(lane >= begin, source, line)
    return line


def assemble(scratch, lines, first, spot, store, spots=range(BLOCKS)):
    total = scratch.shape[0] // WIDTH
    lane = lanes(GROUPS)
    order = {spot(c): c for c in range(BLOCKS)}
    for r in range(lines):
        found = {
            at: scratch[pl.ds(order[at] * GROUPS * total + first + r, GROUPS, stride=total), :] for at in spots
        }
        for n, i in enumerate(rows_in(r, lines)):
            for t in range(TILES):
                tile = None
                for at in spots:
                    begin, end = at * SIDE - t * WIDTH, (at + 1) * SIDE - t * WIDTH
                    if end <= 0 or begin >= WIDTH:
                        continue
                    piece = roll(found[at], begin - n * SIDE)
                    tile = piece if tile is None else jnp.where(lane >= begin, piece, tile)
                if tile is not None:
                    store(i, t, tile)


def disassemble(load, scratch, lines, first, blocks):
    total = scratch.shape[0] // (GROUPS * blocks)
    tiles = -(-blocks * SIDE // WIDTH)
    lane = lanes(GROUPS)
    for r in range(lines):
        turned = []
        for n, i in enumerate(rows_in(r, lines)):
            shift = n * SIDE
            moved = [roll(load(i, t), shift) for t in range(tiles)]
            if shift:
                moved = [jnp.where(lane < shift, moved[t - 1], moved[t]) for t in range(tiles)]
            turned.append(moved)
        for c in range(blocks):
            segments = []
            for n, moved in enumerate(turned):
                t, start = divmod((c + n) * SIDE, WIDTH)
                segments.append((start, moved[t % tiles]))
                if start + SIDE > WIDTH:
                    segments.append((0, moved[(t + 1) % tiles]))
            line = roll(chain(segments, lane), -c * SIDE)
            scratch[pl.ds(c * GROUPS * total + first + r, GROUPS, stride=total), :] = line


def columns_of(t):
    return slice(t * WIDTH, (t + 1) * WIDTH)


def normalise(pair_ref, mean_ref, scale_ref):
    scale = spread_pairs(scale_ref[...])
    normed = (pair_ref[...].astype(f32) - spread_pairs(mean_ref[...])) * scale
    return normed, scale


def edges_kernel(*refs):
    given, out_ref, scratch, held, sems = refs[:8], refs[8], refs[9], refs[10:18], refs[18]
    copies = [pltpu.make_async_copy(a, b, sems.at[n]) for n, (a, b) in enumerate(zip(given, held))]
    for copy in copies:
        copy.start()
    for copy in copies:
        copy.wait()
    pair_ref, mean_ref, scale_ref, mask_ref, lg, lv, rg, rv = held
    kept_scale = spread_pairs(scale_ref[...] * mask_ref[...].astype(f32))
    low = ((pair_ref[...].astype(f32) - spread_pairs(mean_ref[...])) * kept_scale).astype(bf16)
    parts = []
    for gate, value in ((lg, lv), (rg, rv)):
        both = dot(low, jnp.concatenate([gate[...], value[...]], axis=1))
        parts.append(jax.nn.sigmoid(both[:, :WIDTH]) * both[:, WIDTH:])
    out_ref[...] = to_messages(parts, scratch)


def take_right_kernel(in_ref, *refs):
    given, (out_ref, *made), (scratch, panels) = refs[:6], refs[6:9], refs[9:]
    scratch[...] = in_ref[...].astype(f32)

    def store(i, t, tile):
        panels[t, pl.ds(i * (GROUPS + 1), GROUPS), :] = tile

    assemble(scratch, PAIRED, PAIRED, lambda c: c, store)
    for group in range(GROUPS):
        rows = [panels[t, pl.ds(group, SIDE, stride=GROUPS + 1), :] for t in range(TILES)]
        out_ref[group * SIDE : (group + 1) * SIDE, :] = jnp.concatenate(rows, axis=1).astype(bf16)
    on_core(1, lambda: ready(given, *made))


def assemble_left(in_ref, scratch, panel, lines, spot, spots=range(BLOCKS)):
    scratch[...] = in_ref[...].astype(f32)

    def store(i, t, tile):
        panel[i * GROUPS : (i + 1) * GROUPS, columns_of(t)] = tile

    assemble(scratch, lines, 0, spot, store, spots)


def rows_of(panel):
    return lambda i, t: panel[i * GROUPS : (i + 1) * GROUPS, columns_of(t)]


def take_left_kernel(in_ref, out_ref, scratch, panel):
    assemble_left(in_ref, scratch, panel, PAIRED, lambda c: c)
    out_ref[...] = panel[...].astype(bf16)


def half_mixed(left_ref, right_ref, scratch, panel):
    panel[:, :HALF] = dot(left_ref[...], jnp.transpose(right_ref[...]))
    disassemble(rows_of(panel), scratch, ALONE, 0, BLOCKS // 2)


def mix_own_kernel(left_ref, right_ref, out_ref, scratch, panel):
    half_mixed(left_ref, right_ref, scratch, panel)
    out_ref[...] = scratch[...].astype(bf16)


def mix_kernel(own_ref, left_ref, right_ref, out_ref, scratch, panel):
    half_mixed(left_ref, right_ref, scratch, panel)
    size = GROUPS * ALONE
    for core in range(2):

        @pl.when(lax.axis_index("core") == core)
        def _(core=core):
            for n in range(BLOCKS // 2):
                here, mine, other = (slice(at * size, (at + 1) * size) for at in (n, 2 * n + core, 2 * n + 1 - core))
                out_ref[mine, :] = own_ref[here, :]
                out_ref[other, :] = scratch[here, :].astype(bf16)


def ready(given, grad_ref, factor_ref):
    pair_ref, mean_ref, scale_ref, cot_ref, gate_ref, weight_ref = given
    normed, _ = normalise(pair_ref, mean_ref, scale_ref)
    out_sig = jax.nn.sigmoid(dot(normed.astype(bf16), gate_ref[...]))
    grad_y = cot_ref[...].astype(f32) * out_sig
    grad = dot(grad_y.astype(bf16), weight_ref[...], ((1,), (1,)))
    grad_ref[...] = grad - jnp.mean(grad, axis=-1, keepdims=True)
    factor_ref[...] = grad_y * (1.0 - out_sig)


def on_core(core, work):
    pl.when(lax.axis_index("core") == core)(work)


def hand_on(early, made):
    def work():
        for a, b in zip(early, made):
            b[...] = a[...]

    on_core(1, work)


def ready_later_kernel(*refs):
    early, given, made = refs[:2], refs[2:-2], refs[-2:]
    hand_on(early, made)
    on_core(0, lambda: ready(given, *made))


def middle_kernel(in_ref, grad_ref, out_ref, normed_ref, scratch):
    (mixed,) = from_messages(in_ref, scratch, 1)
    centred = mixed - dot(mixed.astype(bf16), jnp.full((WIDTH, WIDTH), 1 / WIDTH, bf16))
    mix_scale = lax.rsqrt(jnp.mean(centred * centred, axis=-1, keepdims=True) + epsilon)
    mix_normed = centred * mix_scale
    normed_ref[...] = mix_normed.astype(bf16)
    grad = grad_ref[...]
    grad_mix = mix_scale * (grad - mix_normed * jnp.mean(grad * mix_normed, axis=-1, keepdims=True))
    out_ref[...] = to_messages([grad_mix], scratch)


def right_grad_all(in_ref, left_ref, grad_ref, own_ref, scratch, panel):
    assemble_left(in_ref, scratch, panel, ALONE, place)
    grad = panel[...]
    grad_ref[...] = grad.astype(bf16)
    first = lax.axis_index("core") == 0
    sums = dot(grad.astype(bf16), left_ref[...], ((0,), (0,)))
    own_ref[...] = jnp.where(first, sums[:HALF], sums[HALF:])
    return jnp.where(first, sums[HALF:], sums[:HALF])


def right_grad_kernel(in_ref, left_ref, *refs):
    given, (grad_ref, own_ref, sent_ref), made, (scratch, panel) = refs[:12], refs[12:15], refs[15:19], refs[19:]

    def only_sent():
        assemble_left(in_ref, scratch, panel, ALONE, place, range(BLOCKS // 2, BLOCKS))
        sums = dot(panel[:, WIDTH:].astype(bf16), left_ref[...], ((0,), (0,)))
        sent_ref[...] = sums[HALF - WIDTH :].astype(bf16)

    def everything():
        sent_ref[...] = right_grad_all(in_ref, left_ref, grad_ref, own_ref, scratch, panel).astype(bf16)
        prepare(given, *made)

    on_core(0, only_sent)
    on_core(1, everything)


def right_grad_later_kernel(*refs):
    early, (in_ref, left_ref, *given), made, (scratch, panel) = refs[:6], refs[6:20], refs[20:26], refs[26:]
    hand_on(early, made)

    def everything():
        right_grad_all(in_ref, left_ref, *made[:2], scratch, panel)
        prepare(given, *made[2:])

    on_core(0, everything)


def left_grad_kernel(grad_ref, own_ref, other_ref, out_ref, right, panel):
    core = lax.axis_index("core")
    right[core] = own_ref[...]
    right[1 - core] = other_ref[...]
    panel[...] = dot(grad_ref[...], right[...].reshape(TOKENS, TOKENS))
    disassemble(rows_of(panel), out_ref, PAIRED, 0, BLOCKS)


def return_kernel(lines_ref, own_ref, other_ref, out_ref, scratch, panels):
    for group in range(GROUPS):
        here = slice(group * SIDE, (group + 1) * SIDE)
        total = own_ref[here, :] + other_ref[here, :].astype(f32)
        for t in range(TILES):
            panels[t, pl.ds(group * (SIDE + 1), SIDE), :] = total[:, columns_of(t)]
    load = lambda i, t: panels[t, pl.ds(i, GROUPS, stride=SIDE + 1), :]
    disassemble(load, scratch, PAIRED, PAIRED, BLOCKS)
    size = GROUPS * 2 * PAIRED
    is_left = lax.broadcasted_iota(jnp.int32, (size, WIDTH), 0) % (2 * PAIRED) < PAIRED
    for c in range(BLOCKS):
        here = slice(c * size, (c + 1) * size)
        out_ref[here, :] = jnp.where(is_left, lines_ref[here, :], scratch[here, :]).astype(bf16)


def prepare(given, normed_ref, scaled_ref, base_ref, factors_ref):
    pair_ref, mean_ref, scale_ref, mask_ref, mix_normed_ref, factor_ref, weight_ref, lg, lv, rg, rv, og = given
    normed, scale = normalise(pair_ref, mean_ref, scale_ref)
    normed_ref[...] = normed
    scaled_ref[...] = scale
    grad_gate = factor_ref[...] * dot(mix_normed_ref[...], weight_ref[...])
    base_ref[...] = dot(grad_gate.astype(bf16), og[...], ((1,), (1,)))
    low = normed.astype(bf16)
    keep = spread_pairs(mask_ref[...].astype(f32))
    for n, (gate, value) in enumerate(((lg, lv), (rg, rv))):
        both = dot(low, jnp.concatenate([gate[...], value[...]], axis=1))
        sig, lin = jax.nn.sigmoid(both[:, :WIDTH]), both[:, WIDTH:]
        factors_ref[2 * n + 1] = keep * sig
        factors_ref[2 * n] = keep * lin * sig * (1.0 - sig)


def last_kernel(
    in_ref, normed_ref, scale_ref, base_ref, factors_ref, lg, lv, rg, rv, out_ref, scratch, held, sems
):
    scratch[...] = in_ref[...].astype(f32)
    weights = [jnp.concatenate([gate[...], value[...]], axis=1) for gate, value in ((lg, lv), (rg, rv))]
    copies = []
    for r in range(PAIRED):
        rows = rows_in(r, PAIRED)
        here = slice(rows[0] * SIDE, (rows[-1] + 1) * SIDE)
        grad_normed = base_ref[here, :]
        for n in range(2):
            turned = jnp.transpose(scratch[pl.ds(PAIRED * n + r, WIDTH, stride=2 * PAIRED), :])
            grad = turned[: len(rows) * SIDE]
            pre_grads = jnp.concatenate([grad * factors_ref[2 * n, here], grad * factors_ref[2 * n + 1, here]], axis=1)
            grad_normed += dot(pre_grads.astype(bf16), weights[n], ((1,), (1,)))
        held[here, :] = layer_back(grad_normed, normed_ref[here, :], scale_ref[here, :])
        copies.append(pltpu.make_async_copy(held.at[here], out_ref.at[here], sems.at[r]))
        copies[-1].start()
    for copy in copies:
        copy.wait()


def call(kernel, outs, *args, scratch=(), name=None, space=VMEM, out_space=VMEM):
    return pl.pallas_call(
        kernel,
        out_shape=[jax.ShapeDtypeStruct(shape, dtype) for shape, dtype in outs],
        in_specs=[space for _ in args],
        out_specs=[out_space for _ in outs],
        scratch_shapes=list(scratch),
        compiler_params=pltpu.CompilerParams(vmem_limit_bytes=48 * 1024 * 1024),
        name=name,
    )(*args)


def spread(messages):
    paired = messages.reshape(WIDTH, -1, 2, WIDTH)
    return lax.all_to_all(paired, SPREAD, 0, 0, tiled=True).reshape(messages.shape)


def swap(value):
    return lax.ppermute(value, "core", [(0, 1), (1, 0)])


def per_device(
    pair_input,
    norm_mean,
    norm_scale,
    pair_mask,
    cotangent,
    left_gate,
    left_value,
    right_gate,
    right_value,
    output_gate,
    output_weight,
):
    pair = pair_input.reshape(PAIRS, WIDTH)
    cot = cotangent.reshape(PAIRS, WIDTH)
    one, two = (WIDTH * ALONE, WIDTH), (WIDTH * 2 * PAIRED, WIDTH)
    line_one, line_two = pltpu.VMEM(one, f32), pltpu.VMEM(two, f32)
    panel_left = pltpu.VMEM((HALF, TOKENS), f32)
    panels_in = pltpu.VMEM((TILES, SIDE * (GROUPS + 1), WIDTH), f32)
    panels_out = pltpu.VMEM((TILES, GROUPS * (SIDE + 1), WIDTH), f32)
    one, two = (one, bf16), (two, bf16)
    panel, wide = ((HALF, TOKENS), bf16), ((HALF, TOKENS), f32)
    given = [
        pltpu.with_memory_space_constraint(a, pltpu.HBM)
        for a in (pair, norm_mean, norm_scale, pair_mask, left_gate, left_value, right_gate, right_value)
    ]
    held = [pltpu.VMEM(a.shape, a.dtype) for a in given]
    (sent,) = call(
        edges_kernel, [two], *given, scratch=[line_two] + held + [pltpu.SemaphoreType.DMA((len(given),))],
        name="edges", space=HBM,
    )
    came = spread(sent)
    many = ((PAIRS, WIDTH), f32)
    given = [pair, norm_mean, norm_scale, cot, output_gate, output_weight]
    right_own, *made = call(
        take_right_kernel, [panel, many, many], came, *given, scratch=[line_two, panels_in], name="take_right"
    )
    right_other = swap(right_own)
    (left,) = call(take_left_kernel, [panel], came, scratch=[line_two, panel_left], name="take_left")
    line_half, panel_half = pltpu.VMEM((WIDTH * ALONE // 2, WIDTH), f32), pltpu.VMEM((HALF, 2 * WIDTH), f32)
    (mixed_own,) = call(
        mix_own_kernel, [((WIDTH * ALONE // 2, WIDTH), bf16)], left, right_own, scratch=[line_half, panel_half], name="mix_own",
    )
    grad_mixnorm, factor = call(
        ready_later_kernel, [many, many], *made, *given, name="ready"
    )
    mixed_own, grad_mixnorm, factor = lax.optimization_barrier((mixed_own, grad_mixnorm, factor))
    (sent,) = call(
        mix_kernel, [one], mixed_own, left, right_other, scratch=[line_half, panel_half], name="mix"
    )
    came = spread(sent)
    sent, mix_normed = call(
        middle_kernel, [one, ((PAIRS, WIDTH), bf16)], came, grad_mixnorm, scratch=[line_one], name="middle"
    )
    came = spread(sent)
    given = [
        pair, norm_mean, norm_scale, pair_mask, mix_normed, factor, output_weight, left_gate, left_value, right_gate,
        right_value, output_gate,
    ]
    factors = ((4, PAIRS, WIDTH), f32)
    grad, own, sent, *made = call(
        right_grad_kernel, [panel, wide, panel, many, many, many, factors], came, left, *given,
        scratch=[line_one, panel_left], name="right_grad",
    )
    other = swap(sent)
    lined = ((WIDTH * 2 * PAIRED, WIDTH), f32)
    grad, own, *prepared = call(
        right_grad_later_kernel, [panel, wide, many, many, many, factors], grad, own, *made, came, left, *given,
        scratch=[line_one, panel_left], name="right_grad_later",
    )
    (lines,) = call(
        left_grad_kernel, [lined], grad, right_own, right_other,
        scratch=[pltpu.VMEM((2, HALF, TOKENS), bf16), panel_left], name="left_grad",
    )
    lines, prepared = lax.optimization_barrier((lines, prepared))
    (sent,) = call(return_kernel, [two], lines, own, other, scratch=[line_two, panels_out], name="return")
    came = spread(sent)
    (out,) = call(
        last_kernel, [many], came, *prepared, left_gate, left_value, right_gate, right_value,
        scratch=[line_two, pltpu.VMEM((PAIRS, WIDTH), f32), pltpu.SemaphoreType.DMA((PAIRED,))], name="last",
        out_space=HBM,
    )
    return out.reshape(SIDE, SIDE, WIDTH)


def solution(mesh):
    fine = Mesh(mesh.devices.reshape(2, 4, 2, 4, 4), ("z_lo", "x", "core", "z_hi", "y"))
    row, col = ("z_lo", "x", "core"), ("z_hi", "y")
    placed = (P(row, col, None), P(row, col), P(row, col), P(row, col), P(row, col, None)) + (P(),) * 6
    return jax.shard_map(per_device, mesh=fine, in_specs=placed, out_specs=P(row, col, None), check_vma=False)
```

```python
import jax
import jax.numpy as jnp
from jax import lax
from jax.experimental import pallas as pl
from jax.experimental.pallas import tpu as pltpu
from jax.sharding import Mesh, PartitionSpec as P

epsilon = 1e-05
SIDE = 24
BLOCKS = 16
PAIRS = SIDE * SIDE
WIDTH = 128
GROUPS = 8
HALF = GROUPS * SIDE
TOKENS = SIDE * BLOCKS
SPREAD = ("z_hi", "y", "z_lo", "x")
TILES = TOKENS // WIDTH
ALONE, PAIRED = 6, 5
f32 = jnp.float32
bf16 = jnp.bfloat16
VMEM = pl.BlockSpec(memory_space=pltpu.VMEM)
HBM = pl.BlockSpec(memory_space=pltpu.HBM)


def dot(a, b, over=((1,), (0,))):
    return lax.dot_general(a, b, (over, ((), ())), preferred_element_type=f32)


def spread_pairs(value):
    turned = jnp.transpose(value)
    return jnp.concatenate([jnp.broadcast_to(turned[:, i : i + 1], (SIDE, WIDTH)) for i in range(SIDE)], axis=0)


def lanes(rows):
    return lax.broadcasted_iota(jnp.int32, (rows, WIDTH), 1)


def roll(value, by):
    by = by % WIDTH
    return value if by == 0 else pltpu.roll(value, by, 1)


def place(c):
    return (c % 2) * GROUPS + c // 2


def layer_back(grad, normed, scale):
    centre = jnp.mean(grad, axis=-1, keepdims=True)
    along = jnp.mean(grad * normed, axis=-1, keepdims=True)
    return scale * (grad - centre - normed * along)


def rows_in(line, lines):
    many = -(-SIDE // lines)
    return range(line * many, min((line + 1) * many, SIDE))


def to_messages(parts, scratch):
    total = scratch.shape[0] // WIDTH
    lines = total // len(parts)
    for p, part in enumerate(parts):
        for r in range(lines):
            stack = [part[i * SIDE : (i + 1) * SIDE] for i in rows_in(r, lines)]
            stack.append(jnp.zeros((WIDTH - len(stack) * SIDE, WIDTH), f32))
            turned = jnp.transpose(jnp.concatenate(stack, axis=0))
            scratch[pl.ds(lines * p + r, WIDTH, stride=total), :] = turned
    return scratch[...].astype(bf16)


def from_messages(in_ref, scratch, count):
    total = in_ref.shape[0] // WIDTH
    lines = total // count
    scratch[...] = in_ref[...].astype(f32)
    parts = []
    for p in range(count):
        rows = [None] * SIDE
        for r in range(lines):
            turned = jnp.transpose(scratch[pl.ds(lines * p + r, WIDTH, stride=total), :])
            for n, i in enumerate(rows_in(r, lines)):
                rows[i] = turned[n * SIDE : (n + 1) * SIDE]
        parts.append(jnp.concatenate(rows, axis=0))
    return parts


def chain(segments, lane):
    line = None
    for begin, source in sorted(segments, key=lambda segment: segment[0]):
        line = source if line is None else jnp.where(lane >= begin, source, line)
    return line


def assemble(scratch, lines, first, spot, store, spots=range(BLOCKS)):
    total = scratch.shape[0] // WIDTH
    lane = lanes(GROUPS)
    order = {spot(c): c for c in range(BLOCKS)}
    for r in range(lines):
        found = {
            at: scratch[pl.ds(order[at] * GROUPS * total + first + r, GROUPS, stride=total), :] for at in spots
        }
        for n, i in enumerate(rows_in(r, lines)):
            for t in range(TILES):
                tile = None
                for at in spots:
                    begin, end = at * SIDE - t * WIDTH, (at + 1) * SIDE - t * WIDTH
                    if end <= 0 or begin >= WIDTH:
                        continue
                    piece = roll(found[at], begin - n * SIDE)
                    tile = piece if tile is None else jnp.where(lane >= begin, piece, tile)
                if tile is not None:
                    store(i, t, tile)


def disassemble(load, scratch, lines, first, blocks):
    total = scratch.shape[0] // (GROUPS * blocks)
    tiles = -(-blocks * SIDE // WIDTH)
    lane = lanes(GROUPS)
    for r in range(lines):
        turned = []
        for n, i in enumerate(rows_in(r, lines)):
            shift = n * SIDE
            moved = [roll(load(i, t), shift) for t in range(tiles)]
            if shift:
                moved = [jnp.where(lane < shift, moved[t - 1], moved[t]) for t in range(tiles)]
            turned.append(moved)
        for c in range(blocks):
            segments = []
            for n, moved in enumerate(turned):
                t, start = divmod((c + n) * SIDE, WIDTH)
                segments.append((start, moved[t % tiles]))
                if start + SIDE > WIDTH:
                    segments.append((0, moved[(t + 1) % tiles]))
            line = roll(chain(segments, lane), -c * SIDE)
            scratch[pl.ds(c * GROUPS * total + first + r, GROUPS, stride=total), :] = line


def columns_of(t):
    return slice(t * WIDTH, (t + 1) * WIDTH)


def normalise(pair_ref, mean_ref, scale_ref):
    scale = spread_pairs(scale_ref[...])
    normed = (pair_ref[...].astype(f32) - spread_pairs(mean_ref[...])) * scale
    return normed, scale


def edges_kernel(*refs):
    given, out_ref, scratch, held, sems = refs[:8], refs[8], refs[9], refs[10:18], refs[18]
    copies = [pltpu.make_async_copy(a, b, sems.at[n]) for n, (a, b) in enumerate(zip(given, held))]
    for copy in copies:
        copy.start()
    for copy in copies:
        copy.wait()
    pair_ref, mean_ref, scale_ref, mask_ref, lg, lv, rg, rv = held
    kept_scale = spread_pairs(scale_ref[...] * mask_ref[...].astype(f32))
    low = ((pair_ref[...].astype(f32) - spread_pairs(mean_ref[...])) * kept_scale).astype(bf16)
    parts = []
    every = dot(low, jnp.concatenate([lg[...], lv[...], rg[...], rv[...]], axis=1))
    for n in (0, 2):
        gate, value = (every[:, m * WIDTH : (m + 1) * WIDTH] for m in (n, n + 1))
        parts.append(jax.nn.sigmoid(gate) * value)
    out_ref[...] = to_messages(parts, scratch)


def take_right_kernel(in_ref, *refs):
    given, (out_ref, *made), (scratch, panels) = refs[:6], refs[6:9], refs[9:]
    scratch[...] = in_ref[...].astype(f32)

    def store(i, t, tile):
        panels[t, pl.ds(i * (GROUPS + 1), GROUPS), :] = tile

    assemble(scratch, PAIRED, PAIRED, lambda c: c, store)
    for group in range(GROUPS):
        rows = [panels[t, pl.ds(group, SIDE, stride=GROUPS + 1), :] for t in range(TILES)]
        out_ref[group * SIDE : (group + 1) * SIDE, :] = jnp.concatenate(rows, axis=1).astype(bf16)
    on_core(1, lambda: ready(given, *made))


def assemble_left(in_ref, scratch, panel, lines, spot, spots=range(BLOCKS)):
    scratch[...] = in_ref[...].astype(f32)

    def store(i, t, tile):
        panel[i * GROUPS : (i + 1) * GROUPS, columns_of(t)] = tile

    assemble(scratch, lines, 0, spot, store, spots)


def rows_of(panel):
    return lambda i, t: panel[i * GROUPS : (i + 1) * GROUPS, columns_of(t)]


def take_left_kernel(in_ref, out_ref, scratch, panel):
    assemble_left(in_ref, scratch, panel, PAIRED, lambda c: c)
    out_ref[...] = panel[...].astype(bf16)


def half_mixed(left_ref, right_ref, scratch, panel):
    panel[:, :HALF] = dot(left_ref[...], jnp.transpose(right_ref[...]))
    disassemble(rows_of(panel), scratch, ALONE, 0, BLOCKS // 2)


def mix_own_kernel(left_ref, right_ref, out_ref, scratch, panel):
    half_mixed(left_ref, right_ref, scratch, panel)
    out_ref[...] = scratch[...].astype(bf16)


def mix_kernel(own_ref, left_ref, right_ref, out_ref, scratch, panel):
    half_mixed(left_ref, right_ref, scratch, panel)
    size = GROUPS * ALONE
    for core in range(2):

        @pl.when(lax.axis_index("core") == core)
        def _(core=core):
            for n in range(BLOCKS // 2):
                here, mine, other = (slice(at * size, (at + 1) * size) for at in (n, 2 * n + core, 2 * n + 1 - core))
                out_ref[mine, :] = own_ref[here, :]
                out_ref[other, :] = scratch[here, :].astype(bf16)


def ready(given, grad_ref, factor_ref):
    pair_ref, mean_ref, scale_ref, cot_ref, gate_ref, weight_ref = given
    normed, _ = normalise(pair_ref, mean_ref, scale_ref)
    out_sig = jax.nn.sigmoid(dot(normed.astype(bf16), gate_ref[...]))
    grad_y = cot_ref[...].astype(f32) * out_sig
    grad = dot(grad_y.astype(bf16), weight_ref[...], ((1,), (1,)))
    grad_ref[...] = grad - jnp.mean(grad, axis=-1, keepdims=True)
    factor_ref[...] = grad_y * (1.0 - out_sig)


def on_core(core, work):
    pl.when(lax.axis_index("core") == core)(work)


def hand_on(early, made):
    def work():
        for a, b in zip(early, made):
            b[...] = a[...]

    on_core(1, work)


def ready_later_kernel(*refs):
    early, given, made = refs[:2], refs[2:-2], refs[-2:]
    hand_on(early, made)
    on_core(0, lambda: ready(given, *made))


def middle_kernel(in_ref, grad_ref, out_ref, normed_ref, scratch):
    (mixed,) = from_messages(in_ref, scratch, 1)
    centred = mixed - dot(mixed.astype(bf16), jnp.full((WIDTH, WIDTH), 1 / WIDTH, bf16))
    mix_scale = lax.rsqrt(jnp.mean(centred * centred, axis=-1, keepdims=True) + epsilon)
    mix_normed = centred * mix_scale
    normed_ref[...] = mix_normed.astype(bf16)
    grad = grad_ref[...]
    grad_mix = mix_scale * (grad - mix_normed * jnp.mean(grad * mix_normed, axis=-1, keepdims=True))
    out_ref[...] = to_messages([grad_mix], scratch)


def right_grad_all(in_ref, left_ref, grad_ref, own_ref, scratch, panel):
    assemble_left(in_ref, scratch, panel, ALONE, place)
    grad = panel[...]
    grad_ref[...] = grad.astype(bf16)
    first = lax.axis_index("core") == 0
    sums = dot(grad.astype(bf16), left_ref[...], ((0,), (0,)))
    own_ref[...] = jnp.where(first, sums[:HALF], sums[HALF:])
    return jnp.where(first, sums[HALF:], sums[:HALF])


def right_grad_kernel(in_ref, left_ref, *refs):
    given, (grad_ref, own_ref, sent_ref), made, (scratch, panel) = refs[:12], refs[12:15], refs[15:19], refs[19:]

    def only_sent():
        assemble_left(in_ref, scratch, panel, ALONE, place, range(BLOCKS // 2, BLOCKS))
        sums = dot(panel[:, WIDTH:].astype(bf16), left_ref[...], ((0,), (0,)))
        sent_ref[...] = sums[HALF - WIDTH :].astype(bf16)

    def everything():
        sent_ref[...] = right_grad_all(in_ref, left_ref, grad_ref, own_ref, scratch, panel).astype(bf16)
        prepare(given, *made)

    on_core(0, only_sent)
    on_core(1, everything)


def right_grad_later_kernel(*refs):
    early, (in_ref, left_ref, *given), made, (scratch, panel) = refs[:6], refs[6:20], refs[20:26], refs[26:]
    hand_on(early, made)

    def everything():
        right_grad_all(in_ref, left_ref, *made[:2], scratch, panel)
        prepare(given, *made[2:])

    on_core(0, everything)


def left_grad_kernel(grad_ref, own_ref, other_ref, out_ref, right, panel):
    core = lax.axis_index("core")
    right[core] = own_ref[...]
    right[1 - core] = other_ref[...]
    panel[...] = dot(grad_ref[...], right[...].reshape(TOKENS, TOKENS))
    disassemble(rows_of(panel), out_ref, PAIRED, 0, BLOCKS)


def return_kernel(lines_ref, own_ref, other_ref, out_ref, scratch, panels):
    for group in range(GROUPS):
        here = slice(group * SIDE, (group + 1) * SIDE)
        total = own_ref[here, :] + other_ref[here, :].astype(f32)
        for t in range(TILES):
            panels[t, pl.ds(group * (SIDE + 1), SIDE), :] = total[:, columns_of(t)]
    load = lambda i, t: panels[t, pl.ds(i, GROUPS, stride=SIDE + 1), :]
    disassemble(load, scratch, PAIRED, PAIRED, BLOCKS)
    size = GROUPS * 2 * PAIRED
    is_left = lax.broadcasted_iota(jnp.int32, (size, WIDTH), 0) % (2 * PAIRED) < PAIRED
    for c in range(BLOCKS):
        here = slice(c * size, (c + 1) * size)
        out_ref[here, :] = jnp.where(is_left, lines_ref[here, :], scratch[here, :]).astype(bf16)


def prepare(given, normed_ref, scaled_ref, base_ref, factors_ref):
    pair_ref, mean_ref, scale_ref, mask_ref, mix_normed_ref, factor_ref, weight_ref, lg, lv, rg, rv, og = given
    normed, scale = normalise(pair_ref, mean_ref, scale_ref)
    normed_ref[...] = normed
    scaled_ref[...] = scale
    grad_gate = factor_ref[...] * dot(mix_normed_ref[...], weight_ref[...])
    base_ref[...] = dot(grad_gate.astype(bf16), og[...], ((1,), (1,)))
    low = normed.astype(bf16)
    keep = spread_pairs(mask_ref[...].astype(f32))
    for n, (gate, value) in enumerate(((lg, lv), (rg, rv))):
        both = dot(low, jnp.concatenate([gate[...], value[...]], axis=1))
        sig, lin = jax.nn.sigmoid(both[:, :WIDTH]), both[:, WIDTH:]
        factors_ref[2 * n + 1] = keep * sig
        factors_ref[2 * n] = keep * lin * sig * (1.0 - sig)


def last_kernel(
    in_ref, normed_ref, scale_ref, base_ref, factors_ref, lg, lv, rg, rv, out_ref, scratch, held, sems
):
    scratch[...] = in_ref[...].astype(f32)
    weights = [jnp.concatenate([gate[...], value[...]], axis=1) for gate, value in ((lg, lv), (rg, rv))]
    copies = []
    for r in range(PAIRED):
        rows = rows_in(r, PAIRED)
        here = slice(rows[0] * SIDE, (rows[-1] + 1) * SIDE)
        grad_normed = base_ref[here, :]
        for n in range(2):
            turned = jnp.transpose(scratch[pl.ds(PAIRED * n + r, WIDTH, stride=2 * PAIRED), :])
            grad = turned[: len(rows) * SIDE]
            pre_grads = jnp.concatenate([grad * factors_ref[2 * n, here], grad * factors_ref[2 * n + 1, here]], axis=1)
            grad_normed += dot(pre_grads.astype(bf16), weights[n], ((1,), (1,)))
        held[here, :] = layer_back(grad_normed, normed_ref[here, :], scale_ref[here, :])
        copies.append(pltpu.make_async_copy(held.at[here], out_ref.at[here], sems.at[r]))
        copies[-1].start()
    for copy in copies:
        copy.wait()


def call(kernel, outs, *args, scratch=(), name=None, space=VMEM, out_space=VMEM):
    return pl.pallas_call(
        kernel,
        out_shape=[jax.ShapeDtypeStruct(shape, dtype) for shape, dtype in outs],
        in_specs=[space for _ in args],
        out_specs=[out_space for _ in outs],
        scratch_shapes=list(scratch),
        compiler_params=pltpu.CompilerParams(vmem_limit_bytes=48 * 1024 * 1024),
        name=name,
    )(*args)


def spread(messages):
    paired = messages.reshape(WIDTH, -1, 2, WIDTH)
    return lax.all_to_all(paired, SPREAD, 0, 0, tiled=True).reshape(messages.shape)


def swap(value):
    return lax.ppermute(value, "core", [(0, 1), (1, 0)])


def per_device(
    pair_input,
    norm_mean,
    norm_scale,
    pair_mask,
    cotangent,
    left_gate,
    left_value,
    right_gate,
    right_value,
    output_gate,
    output_weight,
):
    pair = pair_input.reshape(PAIRS, WIDTH)
    cot = cotangent.reshape(PAIRS, WIDTH)
    one, two = (WIDTH * ALONE, WIDTH), (WIDTH * 2 * PAIRED, WIDTH)
    line_one, line_two = pltpu.VMEM(one, f32), pltpu.VMEM(two, f32)
    panel_left = pltpu.VMEM((HALF, TOKENS), f32)
    panels_in = pltpu.VMEM((TILES, SIDE * (GROUPS + 1), WIDTH), f32)
    panels_out = pltpu.VMEM((TILES, GROUPS * (SIDE + 1), WIDTH), f32)
    one, two = (one, bf16), (two, bf16)
    panel, wide = ((HALF, TOKENS), bf16), ((HALF, TOKENS), f32)
    given = [
        pltpu.with_memory_space_constraint(a, pltpu.HBM)
        for a in (pair, norm_mean, norm_scale, pair_mask, left_gate, left_value, right_gate, right_value)
    ]
    held = [pltpu.VMEM(a.shape, a.dtype) for a in given]
    (sent,) = call(
        edges_kernel, [two], *given, scratch=[line_two] + held + [pltpu.SemaphoreType.DMA((len(given),))],
        name="edges", space=HBM,
    )
    came = spread(sent)
    many = ((PAIRS, WIDTH), f32)
    given = [pair, norm_mean, norm_scale, cot, output_gate, output_weight]
    right_own, *made = call(
        take_right_kernel, [panel, many, many], came, *given, scratch=[line_two, panels_in], name="take_right"
    )
    right_other = swap(right_own)
    (left,) = call(take_left_kernel, [panel], came, scratch=[line_two, panel_left], name="take_left")
    line_half, panel_half = pltpu.VMEM((WIDTH * ALONE // 2, WIDTH), f32), pltpu.VMEM((HALF, 2 * WIDTH), f32)
    (mixed_own,) = call(
        mix_own_kernel, [((WIDTH * ALONE // 2, WIDTH), bf16)], left, right_own, scratch=[line_half, panel_half], name="mix_own",
    )
    grad_mixnorm, factor = call(
        ready_later_kernel, [many, many], *made, *given, name="ready"
    )
    mixed_own, grad_mixnorm, factor = lax.optimization_barrier((mixed_own, grad_mixnorm, factor))
    (sent,) = call(
        mix_kernel, [one], mixed_own, left, right_other, scratch=[line_half, panel_half], name="mix"
    )
    came = spread(sent)
    sent, mix_normed = call(
        middle_kernel, [one, ((PAIRS, WIDTH), bf16)], came, grad_mixnorm, scratch=[line_one], name="middle"
    )
    came = spread(sent)
    given = [
        pair, norm_mean, norm_scale, pair_mask, mix_normed, factor, output_weight, left_gate, left_value, right_gate,
        right_value, output_gate,
    ]
    factors = ((4, PAIRS, WIDTH), f32)
    grad, own, sent, *made = call(
        right_grad_kernel, [panel, wide, panel, many, many, many, factors], came, left, *given,
        scratch=[line_one, panel_left], name="right_grad",
    )
    other = swap(sent)
    lined = ((WIDTH * 2 * PAIRED, WIDTH), f32)
    grad, own, *prepared = call(
        right_grad_later_kernel, [panel, wide, many, many, many, factors], grad, own, *made, came, left, *given,
        scratch=[line_one, panel_left], name="right_grad_later",
    )
    (lines,) = call(
        left_grad_kernel, [lined], grad, right_own, right_other,
        scratch=[pltpu.VMEM((2, HALF, TOKENS), bf16), panel_left], name="left_grad",
    )
    lines, prepared = lax.optimization_barrier((lines, prepared))
    (sent,) = call(return_kernel, [two], lines, own, other, scratch=[line_two, panels_out], name="return")
    came = spread(sent)
    (out,) = call(
        last_kernel, [many], came, *prepared, left_gate, left_value, right_gate, right_value,
        scratch=[line_two, pltpu.VMEM((PAIRS, WIDTH), f32), pltpu.SemaphoreType.DMA((PAIRED,))], name="last",
        out_space=HBM,
    )
    return out.reshape(SIDE, SIDE, WIDTH)


def solution(mesh):
    fine = Mesh(mesh.devices.reshape(2, 4, 2, 4, 4), ("z_lo", "x", "core", "z_hi", "y"))
    row, col = ("z_lo", "x", "core"), ("z_hi", "y")
    placed = (P(row, col, None), P(row, col), P(row, col), P(row, col), P(row, col, None)) + (P(),) * 6
    return jax.shard_map(per_device, mesh=fine, in_specs=placed, out_specs=P(row, col, None), check_vma=False)
```
